32 devices in a mesh: dp: 16 (over z, y, x), tensor: 2 (over core).
Axes of the slice: x: 2, y: 2, z: 4, core: 2. Of those that a mesh axis runs over, the one named last changes fastest.
Arguments:
- block_in: float32 [4096, 768], P(('dp', 'tensor')), may hold values from -6 to 6
- seq_lengths: int32 [16, 4], P('dp'), may hold values from 1 to 160, 256 in all within a row
- routes: int32 [4096, 2], P('dp'), may hold values from 0 to 7, all different within a row; in each aligned block of 256 rows (0 to 255, 256 to 511, ...) at most 128 rows name the same one
- w_query: bfloat16 [768, 768], P('dp', 'tensor'), may hold values from -0.21875 to 0.21875
- w_key: bfloat16 [768, 768], P('dp', 'tensor'), may hold values from -0.21875 to 0.21875
- w_value: bfloat16 [768, 768], P('dp', 'tensor'), may hold values from -0.21875 to 0.21875
- w_out_proj: bfloat16 [768, 768], P('tensor', 'dp'), may hold values from -0.875 to 0.875
- router: bfloat16 [768, 8], P('dp'), may hold values from -0.15625 to 0.15625
- gain_attn: bfloat16 [768], P('dp'), may hold values from 0.099609375 to 1.8984375
- gain_moe: bfloat16 [768], P('dp'), may hold values from 0.099609375 to 1.8984375
- expert_in: bfloat16 [16, 768, 1536], P('dp', None, 'tensor'), may hold values from -0.21875 to 0.21875
- expert_out: bfloat16 [16, 1536, 768], P('dp', 'tensor'), may hold values from -0.109375 to 0.109375
- cotangent: float32 [4096, 768], P('dp'), may hold values from -6 to 6
Outputs:
- block_out: float32 [4096, 768], P(('dp', 'tensor'))
- grad_in: float32 [4096, 768], P(('dp', 'tensor'))
- grad_query: float32 [768, 768], P('dp', 'tensor')
- grad_key: float32 [768, 768], P('dp', 'tensor')
- grad_value: float32 [768, 768], P('dp', 'tensor')
- grad_out_proj: float32 [768, 768], P('tensor', 'dp')
- grad_router: float32 [768, 8], P(('dp', 'tensor'))
- grad_gain_attn: float32 [768], P(('dp', 'tensor'))
- grad_gain_moe: float32 [768], P(('dp', 'tensor'))
- grad_expert_in: float32 [16, 768, 1536], P('dp', None, 'tensor')
- grad_expert_out: float32 [16, 1536, 768], P('dp', 'tensor')
The draws below stay inside these ranges and needn't reach their ends.
Inputs may be any that keep to these rules, and one draw needn't show every extreme that they name: `seq_lengths`: each group's 4 lengths sum to 256, and the largest is exactly 160. A token names 2 different experts. Among the 256 tokens of one group no expert is named by more than 128 routes, a bound that some block reaches.
All inputs are finite; a program needn't handle non-finite values.
Results may differ from the reference program's by a relative error of at most 0.015.
Values may be sent and summed in bfloat16 or wider, within the bound.
No kernel may reach another device: no remote copies, remote signals or barrier semaphores. Data moves between devices by JAX's collectives and lax.ppermute only.
A program may use at most 128 MiB of HBM per device.

```python
import math
import jax
import jax.numpy as jnp
import numpy as np
from jax import lax

D = 768
HEADS = 12
HEAD_DIM = 64
FF = 3072
TOP = 2
SEQS = 4
GT = 256
TOKENS = 4096
EXPERTS = 8
SLICES = 4
CAP = 128
LONGEST = 160
N_DP = 16


def level_of(key, extent, shards, smallest, largest):
    loudness, own = 1.0, jax.random.fold_in(key, 6)
    for axis_at, blocks in shards:
        draws = jnp.exp(jax.random.uniform(jax.random.fold_in(own, axis_at), (blocks,), jnp.float32, smallest / len(shards), largest / len(shards)))
        loudness = loudness * jnp.repeat(draws, extent[axis_at] // blocks).reshape([-1 if axis == axis_at else 1 for axis in range(len(extent))])
    return loudness


def split_up(count, total, bound, skew):
    weights = [(1 << 20) // math.isqrt(standing ** skew) + 1 for standing in range(2, count + 1)]
    spare, holding = total - bound - (count - 1), [1] * (count - 1)
    while spare > 0:
        candidates = [i for i in range(count - 1) if holding[i] < bound]
        mass, budget = sum([weights[i] for i in candidates]), spare
        for i in candidates:
            addition = min(bound - holding[i], max(1, budget * weights[i] // mass), spare)
            holding[i] = holding[i] + addition
            spare = spare - addition
    return np.array([bound] + holding)


def ragged_sizes(own_key, count, total, bound, lean):
    if count == 2:
        one = jax.random.randint(own_key, (), max(1, total - bound), min(bound, total - 1) + 1)
        return jnp.stack([one, total - one])
    sizes = jnp.asarray(split_up(count, total, bound, lean), jnp.int32)
    pairs = (count - 1) // 2
    source_of, receiver = sizes[1:1 + 2 * pairs:2], sizes[2:2 + 2 * pairs:2]
    slack = jnp.minimum(source_of - 1, bound - receiver)
    shifted = jax.random.randint(jax.random.fold_in(own_key, 1), (pairs,), 0, 1 << 20) % (slack + 1)
    sizes = sizes.at[1:1 + 2 * pairs:2].set(source_of - shifted).at[2:2 + 2 * pairs:2].set(receiver + shifted)
    return sizes[jax.random.permutation(jax.random.fold_in(own_key, 2), count)]


def shared_out(key, own, number, rows, count, top, limit, slope):
    ranking = jax.random.permutation(key, count)
    packed, usual = load_shares(count, rows * top, limit, slope, True), load_shares(count, rows * top, limit, slope, False)
    places = jnp.arange(count)

    def named(tallies, offset_by):
        used = int((tallies > 0).sum())
        fixed = max(1, used // 4)
        moved = fixed + (places - fixed + offset_by * (used - fixed)) % max(1, count - fixed)
        return jnp.zeros((count,), jnp.int32).at[ranking[jnp.where(places < fixed, places, moved)]].set(jnp.asarray(tallies, jnp.int32))

    tallies = jnp.where(number % 4 == 0, named(packed, number // 4), named(usual, number - number // 4 - 1))
    mixed = jax.random.permutation(jax.random.fold_in(own, 3), count)
    giver, taker = mixed[0:count // 2 * 2:2], mixed[1:count // 2 * 2:2]
    margin = jnp.minimum(tallies[giver] - 1, limit - tallies[taker]) // 2
    margin = jnp.where((giver == ranking[0]) | (taker == ranking[0]) | (tallies[taker] == 0), 0, jnp.maximum(margin, 0))
    moved = jax.random.randint(jax.random.fold_in(own, 4), (count // 2,), 0, 1 << 20) % (margin + 1)
    tallies = tallies.at[giver].add(-moved).at[taker].add(moved)
    members = jnp.searchsorted(jnp.cumsum(tallies), jnp.arange(rows * top), side="right").astype(jnp.int32)
    table = members.reshape(top, rows).T
    table = table[jax.random.permutation(jax.random.fold_in(own, 1), rows)]
    offset_by = jax.random.randint(jax.random.fold_in(own, 2), (rows, 1), 0, top)
    return jnp.take_along_axis(table, (jnp.arange(top)[None, :] + offset_by) % top, axis=1)


def load_shares(count, total, limit, skew, full):
    loads = [(1 << 20) // math.isqrt(grade ** skew) + 1 for grade in range(1, count + 1)]
    largest = limit if full else min(limit, max(-(-total // count), total * loads[0] // sum(loads)))
    least = 1 if total - largest >= count - 1 else 0
    given, rest = [largest] + [least] * (count - 1), total - largest - least * (count - 1)
    while rest > 0:
        candidates = [i for i in range(1, count) if given[i] < largest] or [i for i in range(1, count) if given[i] < limit]
        mass, remaining = sum([loads[i] for i in candidates]), rest
        for i in candidates:
            extra = min(limit - given[i], max(1, remaining * loads[i] // mass), rest)
            given[i] = given[i] + extra
            rest = rest - extra
    return np.array(given)


def gaussian(stream_key, shape, scale, reach, cuts=(), held_as=jnp.bfloat16):
    gain = level_of(stream_key, shape, cuts, -0.22, 0.18) if cuts else 1.0
    array = jax.random.normal(stream_key, shape, jnp.float32) * scale * gain
    return jnp.minimum(jnp.maximum(array, -reach), reach).astype(held_as)


def setup_inputs(seed: int = 0) -> dict:
    key_list = jax.random.split(jax.random.key(seed), 14)
    block_in = gaussian(key_list[0], (TOKENS, D), 1.0, 6.0, ((0, 32),), jnp.float32)
    seq_lengths = jax.vmap(lambda own: ragged_sizes(own, SEQS, GT, LONGEST, 2))(jax.random.split(key_list[1], N_DP)).reshape((N_DP, SEQS)).astype(jnp.int32)
    routes_keys = jax.random.split(jax.random.fold_in(key_list[2], 1), TOKENS // GT)
    routes_turns = jax.random.permutation(jax.random.fold_in(key_list[2], 3), TOKENS // GT)
    routes = jax.vmap(lambda own, number: shared_out(jax.random.fold_in(key_list[2], 2), own, number, GT, EXPERTS, TOP, CAP, 1))(routes_keys, routes_turns).reshape((TOKENS, TOP))
    w_query = gaussian(key_list[3], (D, D), D ** -0.5, 0.21875, ((0, 16), (1, 2)))
    w_key = gaussian(key_list[4], (D, D), D ** -0.5, 0.21875, ((0, 16), (1, 2)))
    w_value = gaussian(key_list[5], (D, D), D ** -0.5, 0.21875, ((0, 16), (1, 2)))
    w_out_proj = gaussian(key_list[6], (D, D), (D // 16) ** -0.5, 0.875, ((0, 2), (1, 16)))
    router = gaussian(key_list[7], (D, EXPERTS), (2 * D) ** -0.5, 0.15625, ((0, 16),))
    gain_attn = jnp.clip(1.0 + 0.18 * jax.random.normal(key_list[8], (D,), jnp.float32), 0.099609375, 1.8984375).astype(jnp.bfloat16)
    gain_moe = jnp.clip(1.0 + 0.18 * jax.random.normal(key_list[9], (D,), jnp.float32), 0.099609375, 1.8984375).astype(jnp.bfloat16)
    expert_in = gaussian(key_list[10], (2 * EXPERTS, D, FF // 2), D ** -0.5, 0.21875, ((0, 16), (2, 2)))
    expert_out = gaussian(key_list[11], (2 * EXPERTS, FF // 2, D), FF ** -0.5, 0.109375, ((0, 16), (1, 2)))
    cotangent = gaussian(key_list[12], (TOKENS, D), 1.0, 6.0, ((0, 16),), jnp.float32)
    return dict(block_in=block_in, seq_lengths=seq_lengths, routes=routes, w_query=w_query, w_key=w_key, w_value=w_value, w_out_proj=w_out_proj, router=router, gain_attn=gain_attn, gain_moe=gain_moe, expert_in=expert_in, expert_out=expert_out, cotangent=cotangent)


@jax.custom_vjp
def low(v):
    return lax.optimization_barrier(v.astype(jnp.bfloat16)).astype(jnp.float32)

@jax.custom_vjp
def low_back(v):
    return v

def low_keep(v):
    return (low(v), None)

def low_pass(kept, grad):
    return (grad,)

def back_keep(v):
    return (v, None)

def back_low(kept, grad):
    return (low(grad),)
low.defvjp(low_keep, low_pass)
low_back.defvjp(back_keep, back_low)
EPSILON = 1e-06
NEGATIVE = -1e+30
PRECISE = lax.Precision.HIGHEST

def segment_ids(lengths, row_count):
    seq_ends = jnp.cumsum(lengths).astype(jnp.int32)
    places = jnp.arange(row_count, dtype=jnp.int32)
    return lax.optimization_barrier(jnp.sum((places[:, None] >= seq_ends[None, :]).astype(jnp.int32), axis=1)).astype(jnp.int32)

def rms_scale(row_block, gain_vector):
    inv_rms = lax.rsqrt(lax.optimization_barrier(jnp.mean(row_block * row_block, axis=1, keepdims=True)) + EPSILON)
    return row_block * inv_rms * gain_vector

def expert_table(routes):
    flat_routes = routes.reshape(-1)
    expert_hits = (flat_routes[:, None] == jnp.arange(EXPERTS, dtype=jnp.int32)[None, :]).astype(jnp.int32)
    expert_rank = jnp.cumsum(expert_hits.reshape(N_DP, GT * TOP, EXPERTS), axis=1).astype(jnp.int32) - 1
    slot_index = lax.optimization_barrier(jnp.sum(expert_hits * expert_rank.reshape(-1, EXPERTS), axis=1)).astype(jnp.int32)
    group_ids = jnp.arange(TOKENS * TOP, dtype=jnp.int32) // (GT * TOP)
    slot_place = flat_routes * (N_DP * CAP) + group_ids * CAP + slot_index
    slot_table = jnp.full((EXPERTS * N_DP * CAP,), TOKENS * TOP, dtype=jnp.int32)
    slot_table = slot_table.at[slot_place].set(jnp.arange(TOKENS * TOP, dtype=jnp.int32))
    return slot_table.reshape(EXPERTS, N_DP * CAP)

def group_attention(h_rows, seg_id, query_full, key_full, value_full):

    def project(weight):
        return low(low_back(jnp.dot(h_rows, weight, precision=PRECISE))).reshape(GT, HEADS, HEAD_DIM)
    queries = project(query_full)
    key_rows = project(key_full)
    value_rows = project(value_full)
    scores = low_back(jnp.einsum('qhd,khd->hqk', queries, key_rows, precision=PRECISE) * HEAD_DIM ** (-0.5))
    places = jnp.arange(GT, dtype=jnp.int32)
    allowed = (seg_id[:, None] == seg_id[None, :]) & (places[:, None] >= places[None, :])
    prob_rows = jax.nn.softmax(jnp.where(allowed[None], scores, NEGATIVE), axis=-1)
    mixed_rows = jnp.einsum('hqk,khd->qhd', low(prob_rows), value_rows, precision=PRECISE)
    return low(low_back(mixed_rows.reshape(GT, D)))

def expert_block(rows_by_piece, weight_in, weight_out):
    piece_width = FF // SLICES
    summed = jnp.zeros((rows_by_piece[0].shape[0], D), dtype=jnp.float32)
    for piece_index in range(SLICES):
        first_part = weight_in[:, piece_index * piece_width:(piece_index + 1) * piece_width]
        second_part = weight_out[piece_index * piece_width:(piece_index + 1) * piece_width]
        pre_act = low_back(jnp.dot(rows_by_piece[piece_index], first_part, precision=PRECISE))
        hidden = low(jax.nn.gelu(pre_act))
        summed = summed + low(low_back(jnp.dot(hidden, second_part, precision=PRECISE)))
    return summed

def reference(block_in, seq_lengths, routes, w_query, w_key, w_value, w_out_proj, router, gain_attn, gain_moe, expert_in, expert_out, cotangent):
    seg_all = jnp.stack([segment_ids(seq_lengths[group_index], GT) for group_index in range(N_DP)], axis=0)
    slot_table = expert_table(routes)

    def forward(inputs, query_full, key_full, value_full, proj_full, router_full, gain_one, gain_two, weight_in, weight_out):
        h_one = low(rms_scale(inputs, gain_one))

        def group_step(member):
            return group_attention(member[0], member[1], query_full, key_full, value_full)
        mixed_all = lax.map(jax.checkpoint(group_step), (h_one.reshape(N_DP, GT, D), seg_all)).reshape(TOKENS, D)
        residual = inputs + low_back(jnp.dot(mixed_all, proj_full, precision=PRECISE))
        h_two = low(rms_scale(residual, gain_two))
        logits = jnp.dot(h_two, router_full, precision=PRECISE)
        gate_values = jax.nn.softmax(jnp.take_along_axis(logits, routes, axis=1), axis=1)
        blank_row = jnp.zeros((1, D), dtype=h_two.dtype)
        pieces = []
        for piece_index in range(SLICES):
            copies = jnp.stack([low_back(h_two) for pick_index in range(TOP)], axis=1).reshape(TOKENS * TOP, D)
            pieces.append(jnp.concatenate([copies, blank_row], axis=0))
        in_full = weight_in.reshape(EXPERTS, 2, D, FF // 2).transpose(0, 2, 1, 3).reshape(EXPERTS, D, FF)
        out_full = weight_out.reshape(EXPERTS, FF, D)

        def one_expert(member):
            slot_index, first_weight, second_weight = member
            return expert_block([piece_rows[slot_index] for piece_rows in pieces], first_weight, second_weight)
        produced = lax.map(jax.checkpoint(one_expert), (slot_table, in_full, out_full))
        pair_out = jnp.zeros((TOKENS * TOP + 1, D), dtype=produced.dtype).at[slot_table.reshape(-1)].add(produced.reshape(-1, D))
        pair_out = pair_out[:TOKENS * TOP].reshape(TOKENS, TOP, D)
        return residual + lax.optimization_barrier(jnp.sum(gate_values[:, :, None] * pair_out, axis=1))
    primals = (block_in.astype(jnp.float32), w_query.astype(jnp.float32), w_key.astype(jnp.float32), w_value.astype(jnp.float32), w_out_proj.astype(jnp.float32), router.astype(jnp.float32), gain_attn.astype(jnp.float32), gain_moe.astype(jnp.float32), expert_in.astype(jnp.float32), expert_out.astype(jnp.float32))
    block_out, pullback = jax.vjp(forward, *primals)
    gradients = pullback(cotangent.astype(jnp.float32))
    return (block_out, gradients[0], gradients[1], gradients[2], gradients[3], gradients[4], gradients[5], gradients[6], gradients[7], gradients[8], gradients[9])
```

```python
import jax
import jax.numpy as jnp
from jax import lax
from jax.sharding import PartitionSpec as P

HEAD_DIM = 64
LANES = 128


EPSILON = 1e-06
NEGATIVE = -1e30
PRECISE = lax.Precision.HIGHEST
LOW = jnp.bfloat16
FULL = jnp.float32


def dot(left_side, right_side):
    return jnp.dot(left_side, right_side, preferred_element_type=FULL)


def contract_rows(left_side, right_side):
    return lax.dot_general(
        left_side, right_side, (((0,), (0,)), ((), ())), preferred_element_type=FULL
    )


def contract_cols(left_side, right_side):
    return lax.dot_general(
        left_side, right_side, (((1,), (1,)), ((), ())), preferred_element_type=FULL
    )


def segment_ids(lengths, row_count):
    seq_ends = jnp.cumsum(lengths)
    places = jnp.arange(row_count, dtype=jnp.int32)
    return jnp.sum((places[:, None] >= seq_ends[None, :]).astype(jnp.int32), axis=1)


def swap(values):
    return lax.ppermute(values, "tensor", [(0, 1), (1, 0)])


def bit_orders():
    bits = lax.axis_size("dp").bit_length() - 1
    falling = list(range(bits - 1, -1, -1))
    return falling, falling[:-2] + [falling[-1], falling[-2]]


def partners(bit):
    return [(i, i ^ (1 << bit)) for i in range(lax.axis_size("dp"))]


def gather_dp(shard, order):
    bits, own = len(order), lax.axis_index("dp")
    block = shard.reshape((1,) * bits + shard.shape)
    for bit in order:
        other = lax.ppermute(block, "dp", partners(bit))
        axis = bits - 1 - bit
        upper = ((own >> bit) & 1) == 1
        block = jnp.where(
            upper,
            jnp.concatenate([other, block], axis=axis),
            jnp.concatenate([block, other], axis=axis),
        )
    return block.reshape(shard.shape[0] << bits, shard.shape[1])


def reduce_dp(partial, order):
    bits, own = len(order), lax.axis_index("dp")
    rows, width = partial.shape[0] >> len(order), partial.shape[1]
    block = partial.reshape((2,) * bits + (rows, width))
    for bit in order:
        axis, place = bits - 1 - bit, (own >> bit) & 1
        given = lax.dynamic_index_in_dim(block, 1 - place, axis, keepdims=True).astype(LOW)
        kept = lax.dynamic_index_in_dim(block, place, axis, keepdims=True)
        block = kept.astype(FULL) + lax.ppermute(given, "dp", partners(bit)).astype(FULL)
    return block.reshape(rows, width)


def trade(values):
    return lax.all_to_all(values, "dp", split_axis=0, concat_axis=0, tiled=True)


def local(
    block_in,
    seq_lengths,
    routes,
    w_query,
    w_key,
    w_value,
    w_out_proj,
    router,
    gain_attn,
    gain_moe,
    expert_in,
    expert_out,
    cotangent,
):
    dp_count = lax.axis_size("dp")
    core = lax.axis_index("tensor")
    tok_rows, model_width = block_in.shape
    group_rows, top_count = routes.shape
    experts = router.shape[1]
    owners = dp_count // experts
    half_cap = top_count * group_rows // experts
    slots = dp_count * half_cap
    inner_width = w_query.shape[1]
    head_count = inner_width // HEAD_DIM
    order_a, order_b = bit_orders()

    extra_width = -(-(2 + experts) // LANES) * LANES
    extra = jnp.concatenate(
        [
            gain_attn[:, None],
            gain_moe[:, None],
            router,
            jnp.zeros((router.shape[0], extra_width - 2 - experts), LOW),
        ],
        axis=1,
    )
    qk_full = gather_dp(jnp.concatenate([w_query, w_key], axis=1), order_a)
    ve_full = gather_dp(jnp.concatenate([w_value, extra], axis=1), order_b)
    proj_back = gather_dp(w_out_proj.T, order_b)
    qkv_full = jnp.concatenate([qk_full, ve_full[:, :inner_width]], axis=1)
    gain_one = ve_full[:, inner_width].astype(FULL)[None, :]
    gain_two = ve_full[:, inner_width + 1].astype(FULL)[None, :]
    router_full = ve_full[:, inner_width + 2 : inner_width + 2 + experts]

    hits = jnp.any(
        routes[:, :, None] == jnp.arange(experts, dtype=jnp.int32)[None, None, :], axis=1
    )
    places = jnp.arange(group_rows, dtype=jnp.int32)
    earlier = (places[:, None] > places[None, :]).astype(LOW)
    rank = dot(earlier, hits.astype(LOW)).astype(jnp.int32)
    slot_of = jnp.where(hits, rank, -1).T
    hits_t = slot_of >= 0
    slot_ids = core * half_cap + jnp.arange(half_cap, dtype=jnp.int32)
    in_slot = slot_of[:, None, :] == slot_ids[None, :, None]
    dispatch = (
        jnp.broadcast_to(in_slot[:, None], (experts, owners, half_cap, group_rows))
        .astype(LOW)
        .reshape(slots, group_rows)
    )

    def send_rows(token_rows):
        picked = dot(dispatch, token_rows).astype(LOW)
        return trade(picked.reshape(dp_count, half_cap, model_width)).reshape(slots, model_width)

    def both_halves(own):
        return jnp.concatenate([own, swap(own)], axis=0)

    cot_rows = both_halves(send_rows(cotangent.astype(LOW)))

    seg_id = segment_ids(seq_lengths[0], group_rows)
    score_scale = HEAD_DIM ** (-0.5)
    rows_all = lax.all_gather(block_in, "tensor", axis=0, tiled=True)
    inv_one = lax.rsqrt(jnp.mean(rows_all * rows_all, axis=1, keepdims=True) + EPSILON)
    normed_one = rows_all * inv_one
    h_one = (normed_one * gain_one).astype(LOW)
    qkv = dot(h_one, qkv_full).astype(LOW).reshape(group_rows, 3, head_count, HEAD_DIM)
    queries, key_rows, value_rows = qkv[:, 0], qkv[:, 1], qkv[:, 2]
    scores = jnp.einsum("qhd,khd->hqk", queries, key_rows, preferred_element_type=FULL) * score_scale
    allowed = (seg_id[:, None] == seg_id[None, :]) & (places[:, None] >= places[None, :])
    scores = jnp.where(allowed[None], scores, NEGATIVE)
    exp_terms = jnp.exp(scores - jnp.max(scores, axis=-1, keepdims=True))
    probs = exp_terms / jnp.sum(exp_terms, axis=-1, keepdims=True)
    prob_low = probs.astype(LOW)
    mixed_rows = (
        jnp.einsum("hqk,khd->qhd", prob_low, value_rows, preferred_element_type=FULL)
        .reshape(group_rows, inner_width)
        .astype(LOW)
    )
    attn_part = contract_cols(mixed_rows, proj_back)
    residual = rows_all + (attn_part + swap(attn_part))
    inv_two = lax.rsqrt(jnp.mean(residual * residual, axis=1, keepdims=True) + EPSILON)
    normed_two = residual * inv_two
    h_two = (normed_two * gain_two).astype(LOW)

    logits = lax.dot_general(
        router_full, h_two, (((0,), (1,)), ((), ())), preferred_element_type=FULL
    )
    peak = jnp.max(jnp.where(hits_t, logits, NEGATIVE), axis=0, keepdims=True)
    gate_terms = jnp.where(hits_t, jnp.exp(jnp.where(hits_t, logits - peak, 0.0)), 0.0)
    gates = gate_terms / jnp.sum(gate_terms, axis=0, keepdims=True)
    slot_gates = jnp.sum(jnp.where(in_slot, gates[:, None, :], 0.0), axis=2)
    gate_rows = jnp.broadcast_to(slot_gates[:, None], (experts, owners, half_cap)).reshape(
        dp_count, half_cap
    )

    incoming = both_halves(send_rows(h_two))
    gate_col = both_halves(trade(gate_rows).reshape(slots, 1))
    first_weight = expert_in[0]
    second_weight = expert_out[0]
    pre_act = dot(incoming, first_weight)
    hidden, gelu_back = jax.vjp(jax.nn.gelu, pre_act)
    hidden = hidden.astype(LOW)
    arrived = (gate_col * cot_rows.astype(FULL)).astype(LOW)
    grad_hidden = contract_cols(arrived, second_weight)
    gated_grad = jnp.sum(hidden.astype(FULL) * grad_hidden, axis=1)
    grad_pre = gelu_back(grad_hidden)[0].astype(LOW)
    given_rows = contract_cols(grad_pre[slots:], first_weight).astype(LOW)
    kept_rows = contract_cols(grad_pre[:slots], first_weight)
    in_rows = (kept_rows + swap(given_rows).astype(FULL)).astype(LOW)
    own_gated = gated_grad[:slots] + swap(gated_grad[slots:])
    back_gated = trade(own_gated.reshape(dp_count, half_cap))
    back_rows = trade(in_rows.reshape(dp_count, half_cap, model_width)).reshape(slots, model_width)

    given_out = (gate_col[slots:] * dot(hidden[slots:], second_weight)).astype(LOW)
    kept_out = gate_col[:slots] * dot(hidden[:slots], second_weight)
    out_rows = (kept_out + swap(given_out).astype(FULL)).astype(LOW)
    back_out = trade(out_rows.reshape(dp_count, half_cap, model_width)).reshape(slots, model_width)
    grad_second = contract_rows(hidden, arrived)
    grad_first = contract_rows(incoming, grad_pre)

    out_part = contract_rows(dispatch, back_out)
    own_start = core * tok_rows
    other_start = (1 - core) * tok_rows

    def rows_at(values, start):
        return lax.dynamic_slice_in_dim(values, start, tok_rows, 0)

    block_out = rows_at(residual, own_start) + (
        rows_at(out_part, own_start) + swap(rows_at(out_part, other_start))
    )

    slot_gated = jnp.sum(back_gated.reshape(experts, owners, half_cap), axis=1)
    gated = jnp.sum(jnp.where(in_slot, slot_gated[:, :, None], 0.0), axis=1)
    logit_grad = jnp.where(hits_t, gated - gates * jnp.sum(gated, axis=0, keepdims=True), 0.0)
    h_grad_part = contract_rows(dispatch, back_rows) + lax.dot_general(
        logit_grad, router_full.astype(FULL), (((0,), (1,)), ((), ())), precision=PRECISE
    )
    router_part = lax.dot_general(
        h_two.astype(FULL), logit_grad, (((0,), (1,)), ((), ())), precision=PRECISE
    )
    h_grad = h_grad_part + swap(h_grad_part)
    gain_two_part = 0.5 * jnp.sum(h_grad * normed_two, axis=0)
    scaled_two = h_grad * gain_two
    resid_grad = cotangent + inv_two * (
        scaled_two - normed_two * jnp.mean(scaled_two * normed_two, axis=1, keepdims=True)
    )
    attn_grad = resid_grad.astype(LOW)

    grad_proj_part = contract_rows(attn_grad, mixed_rows)
    mixed_grad = (
        dot(attn_grad, proj_back).astype(LOW).reshape(group_rows, head_count, HEAD_DIM)
    )
    prob_grad = jnp.einsum("qhd,khd->hqk", mixed_grad, value_rows, preferred_element_type=FULL)
    row_carry = jnp.sum(prob_grad * probs, axis=-1, keepdims=True)
    score_grad = (probs * (prob_grad - row_carry)).astype(LOW)
    query_grad = (
        jnp.einsum("hqk,khd->qhd", score_grad, key_rows, preferred_element_type=FULL) * score_scale
    )
    key_grad = (
        jnp.einsum("hqk,qhd->khd", score_grad, queries, preferred_element_type=FULL) * score_scale
    )
    value_grad = jnp.einsum("hqk,qhd->khd", prob_low, mixed_grad, preferred_element_type=FULL)
    qk_grad = jnp.concatenate(
        [query_grad.reshape(group_rows, inner_width), key_grad.reshape(group_rows, inner_width)],
        axis=1,
    ).astype(LOW)
    v_grad = value_grad.reshape(group_rows, inner_width).astype(LOW)
    grad_qk_part = contract_rows(h_one, qk_grad)
    grad_v_part = contract_rows(h_one, v_grad)
    one_grad_part = contract_cols(qk_grad, qk_full) + contract_cols(v_grad, ve_full[:, :inner_width])
    gain_one_part = jnp.sum(one_grad_part * normed_one, axis=0)
    extra_part = jnp.concatenate(
        [
            gain_one_part[:, None],
            gain_two_part[:, None],
            router_part,
            jnp.zeros((model_width, extra_width - 2 - experts), FULL),
        ],
        axis=1,
    )
    proj_sum = reduce_dp(grad_proj_part, order_b[::-1])
    qk_sum = reduce_dp(grad_qk_part, order_a[::-1])
    ve_sum = reduce_dp(jnp.concatenate([grad_v_part, extra_part], axis=1), order_b[::-1])
    one_grad = rows_at(one_grad_part, own_start) + swap(
        rows_at(one_grad_part, other_start).astype(LOW)
    ).astype(FULL)
    own_normed = rows_at(normed_one, own_start)
    scaled_one = one_grad * gain_one
    grad_in = rows_at(resid_grad, own_start) + rows_at(inv_one, own_start) * (
        scaled_one - own_normed * jnp.mean(scaled_one * own_normed, axis=1, keepdims=True)
    )
    extra_sum = ve_sum[:, inner_width:]
    extra_sum = extra_sum + swap(extra_sum)
    share = extra_sum.shape[0] // 2
    extra_own = lax.dynamic_slice_in_dim(extra_sum, core * share, share, 0)
    return (
        block_out,
        grad_in,
        qk_sum[:, :inner_width],
        qk_sum[:, inner_width:],
        ve_sum[:, :inner_width],
        proj_sum.T,
        extra_own[:, 2 : 2 + experts],
        extra_own[:, 0],
        extra_own[:, 1],
        grad_first[None],
        grad_second[None],
    )


def solution(mesh):
    in_specs = (
        P(("dp", "tensor"), None),
        P("dp", None),
        P("dp", None),
        P("dp", "tensor"),
        P("dp", "tensor"),
        P("dp", "tensor"),
        P("tensor", "dp"),
        P("dp", None),
        P("dp"),
        P("dp"),
        P("dp", None, "tensor"),
        P("dp", "tensor", None),
        P("dp", None),
    )
    out_specs = (
        P(("dp", "tensor"), None),
        P(("dp", "tensor"), None),
        P("dp", "tensor"),
        P("dp", "tensor"),
        P("dp", "tensor"),
        P("tensor", "dp"),
        P(("dp", "tensor"), None),
        P(("dp", "tensor")),
        P(("dp", "tensor")),
        P("dp", None, "tensor"),
        P("dp", "tensor", None),
    )
    return jax.shard_map(local, mesh=mesh, in_specs=in_specs, out_specs=out_specs, check_vma=False)
```

```python
import math

import jax
import jax.numpy as jnp
from jax import lax
from jax.experimental import pallas as pl
from jax.experimental.pallas import tpu as pltpu
from jax.sharding import PartitionSpec as P

HEAD_DIM = 64
LANES = 128


EPSILON = 1e-06
NEGATIVE = -1e30
VMEM_BYTES = 48 * 1024 * 1024
EXTRA_ROWS = 16
LOW = jnp.bfloat16
FULL = jnp.float32


def dot(left_side, right_side):
    return jnp.dot(left_side, right_side, preferred_element_type=FULL)


def contract_rows(left_side, right_side):
    return lax.dot_general(
        left_side, right_side, (((0,), (0,)), ((), ())), preferred_element_type=FULL
    )


def contract_cols(left_side, right_side):
    return lax.dot_general(
        left_side, right_side, (((1,), (1,)), ((), ())), preferred_element_type=FULL
    )


def split_low(values):
    high = values.astype(LOW)
    return high, (values - high.astype(FULL)).astype(LOW)


def iota(shape, axis):
    return lax.broadcasted_iota(jnp.int32, shape, axis)


def swap(values):
    return lax.ppermute(values, "tensor", [(0, 1), (1, 0)])


def bit_orders():
    bits = lax.axis_size("dp").bit_length() - 1
    falling = list(range(bits - 1, -1, -1))
    return falling, falling[:-2] + [falling[-1], falling[-2]]


def partners(bit):
    return [(i, i ^ (1 << bit)) for i in range(lax.axis_size("dp"))]


def double(block, bit, bits):
    other = lax.ppermute(block, "dp", partners(bit))
    axis = bits - 1 - bit
    upper = ((lax.axis_index("dp") >> bit) & 1) == 1
    return jnp.where(
        upper,
        jnp.concatenate([other, block], axis=axis),
        jnp.concatenate([block, other], axis=axis),
    )


def halve(block, bit, bits):
    axis, place = bits - 1 - bit, (lax.axis_index("dp") >> bit) & 1
    given = lax.dynamic_index_in_dim(block, 1 - place, axis, keepdims=True).astype(LOW)
    kept = lax.dynamic_index_in_dim(block, place, axis, keepdims=True)
    return kept.astype(FULL) + lax.ppermute(given, "dp", partners(bit)).astype(FULL)


def trade(values):
    return lax.all_to_all(values, "dp", split_axis=0, concat_axis=0, tiled=True)


def call(kernel, out_shape, *operands, flops=0, smem=()):
    moved = sum(x.size * x.dtype.itemsize for x in (*operands, *out_shape))
    return pl.pallas_call(
        kernel,
        out_shape=out_shape,
        in_specs=[
            pl.BlockSpec(memory_space=pltpu.SMEM if i in smem else pltpu.VMEM)
            for i in range(len(operands))
        ],
        out_specs=[pl.BlockSpec(memory_space=pltpu.VMEM) for _ in out_shape],
        compiler_params=pltpu.CompilerParams(vmem_limit_bytes=VMEM_BYTES),
        cost_estimate=pl.CostEstimate(flops=flops, bytes_accessed=moved, transcendentals=0),
    )(*operands)


def inverse_rms(rows):
    return lax.rsqrt(jnp.mean(rows * rows, axis=1, keepdims=True) + EPSILON)


GELU_SCALE = math.sqrt(2.0 / math.pi)
GELU_CUBE = 0.044715


def attention_kernel(
    len_ref, rows_ref, qk_ref, vx_ref, attn_ref, h_ref, qkv_ref, probs_ref, mixed_ref, ext_ref
):
    group_rows = rows_ref.shape[0]
    inner = qk_ref.shape[1] // 2
    rows = rows_ref[...]
    ext = vx_ref[:, 2 * inner :].astype(FULL).T
    ext_ref[...] = ext
    h_one = (rows * inverse_rms(rows) * ext[0:1, :]).astype(LOW)
    h_ref[...] = h_one
    qkv_ref[:, : 2 * inner] = dot(h_one, qk_ref[...]).astype(LOW)
    qkv_ref[:, 2 * inner :] = dot(h_one, vx_ref[:, :inner]).astype(LOW)
    down, across = iota((group_rows, group_rows), 0), iota((group_rows, group_rows), 1)
    allowed = down >= across
    end = jnp.int32(0)
    for place in range(len_ref.shape[1]):
        end = end + len_ref[0, place]
        allowed = allowed & ((down >= end) == (across >= end))
    low_lanes = iota((group_rows, LANES), 1) < HEAD_DIM
    for pair in range(inner // LANES):
        at = pair * LANES
        queries = qkv_ref[:, at : at + LANES]
        key_rows = qkv_ref[:, inner + at : inner + at + LANES]
        value_rows = qkv_ref[:, 2 * inner + at : 2 * inner + at + LANES]
        outs = []
        for sub in range(2):
            own = low_lanes if sub == 0 else ~low_lanes
            scores = contract_cols(jnp.where(own, queries, jnp.zeros_like(queries)), key_rows)
            scores = jnp.where(allowed, scores * HEAD_DIM ** (-0.5), NEGATIVE)
            terms = jnp.exp(scores - jnp.max(scores, axis=1, keepdims=True))
            probs = terms / jnp.sum(terms, axis=1, keepdims=True)
            probs_ref[2 * pair + sub] = probs
            outs.append(dot(probs.astype(LOW), value_rows))
        mixed_ref[:, at : at + LANES] = jnp.where(low_lanes, outs[0], outs[1]).astype(LOW)
    attn_ref[...] = contract_cols(mixed_ref[...], vx_ref[:, inner : 2 * inner])


def slot_tables(slot_row, base, half):
    experts, group_rows = slot_row.shape
    count, shift = experts * half, half.bit_length() - 1
    of_expert = (iota((count, experts), 0) >> shift) == iota((count, experts), 1)
    wanted = (iota((count, 1), 0) & (half - 1)) + base
    here = dot(of_expert.astype(LOW), slot_row) == wanted.astype(FULL)
    return here, of_expert


def dispatch_kernel(
    base_ref, rows_ref, attn_ref, other_ref, ext_ref, slot_ref, resid_ref, h_ref, gates_ref, send_ref
):
    experts, owners, rows_sent, _ = send_ref.shape
    blocks = rows_ref.shape[1] // LANES
    half = (rows_sent - EXTRA_ROWS) // blocks
    count = experts * half
    residual = rows_ref[...] + (attn_ref[...] + other_ref[...])
    resid_ref[...] = residual
    h_two = (residual * inverse_rms(residual) * ext_ref[1:2, :]).astype(LOW)
    h_ref[...] = h_two
    slot_row = slot_ref[...]
    hits = slot_row >= 0
    all_logits = contract_cols(ext_ref[...].astype(LOW), h_two)
    logits = all_logits[2 : 2 + experts, :]
    peak = jnp.max(jnp.where(hits, logits, NEGATIVE), axis=0, keepdims=True)
    terms = jnp.where(hits, jnp.exp(jnp.where(hits, logits - peak, 0.0)), 0.0)
    gates = terms / jnp.sum(terms, axis=0, keepdims=True)
    gates_ref[...] = gates
    here, of_expert = slot_tables(slot_row, base_ref[0], half)
    one_hot = here.astype(LOW)
    picked = dot(one_hot, h_two).astype(LOW).reshape(experts, half, blocks * LANES)
    high, low = split_low(gates)
    by_expert = contract_cols(one_hot, high) + contract_cols(one_hot, low)
    gate_col = jnp.sum(jnp.where(of_expert, by_expert, 0.0), axis=1, keepdims=True)
    on_lane = iota((count, LANES), 1) == (iota((count, LANES), 0) & (half - 1))
    high_rows, low_rows = [
        contract_rows(of_expert.astype(LOW), jnp.where(on_lane, part.astype(FULL), 0.0).astype(LOW))
        for part in split_low(gate_col)
    ]
    sub = iota((EXTRA_ROWS, LANES), 0)
    for owner in range(owners):
        for block in range(blocks):
            send_ref[:, owner, block * half : (block + 1) * half, :] = picked[
                :, :, block * LANES : (block + 1) * LANES
            ]
        for expert in range(experts):
            send_ref[expert, owner, blocks * half :, :] = jnp.where(
                sub == 0,
                high_rows[expert : expert + 1, :],
                jnp.where(sub == 1, low_rows[expert : expert + 1, :], 0.0),
            ).astype(LOW)


def rows_of(ref, half):
    blocks = (ref.shape[1] - EXTRA_ROWS) // half
    return jnp.concatenate(
        [
            ref[:, at * half : (at + 1) * half, :].reshape(ref.shape[0] * half, LANES)
            for at in range(blocks)
        ],
        axis=1,
    )


def expert_kernel(half, h_ref, cot_ref, first_ref, second_ref, back_ref, hid_ref, pre_ref, out_ref, gate_ref):
    sources = h_ref.shape[0]
    blocks = (h_ref.shape[1] - EXTRA_ROWS) // half
    count, shift = sources * half, half.bit_length() - 1
    extra = h_ref[:, blocks * half :, :].reshape(sources * EXTRA_ROWS, LANES)
    source = iota((count, sources * EXTRA_ROWS), 0) >> shift
    row = iota((count, sources * EXTRA_ROWS), 1)
    two_rows = (row == source * EXTRA_ROWS) | (row == source * EXTRA_ROWS + 1)
    on_lane = iota((count, LANES), 1) == (iota((count, LANES), 0) & (half - 1))
    gate_lanes = dot(two_rows.astype(LOW), extra)
    gate = jnp.sum(jnp.where(on_lane, gate_lanes, 0.0), axis=1, keepdims=True)
    gate_ref[...] = jnp.broadcast_to(gate, (count, LANES))
    arrived = (gate * cot_ref[...].reshape(count, blocks * LANES).astype(FULL)).astype(LOW)
    out_ref[...] = arrived
    incoming = rows_of(h_ref, half)
    pre = dot(incoming, first_ref[...])
    grad_hidden = contract_cols(arrived, second_ref[...])
    square = pre * pre
    bend = jnp.tanh(GELU_SCALE * pre * (1.0 + GELU_CUBE * square))
    rise = 0.5 * (1.0 + bend)
    hidden = (pre * rise).astype(LOW)
    hid_ref[...] = hidden
    slope = rise + (0.5 * GELU_SCALE) * pre * (1.0 - bend * bend) * (1.0 + 3.0 * GELU_CUBE * square)
    gated = jnp.sum(hidden.astype(FULL) * grad_hidden, axis=1, keepdims=True)
    grad_pre = (grad_hidden * slope).astype(LOW)
    pre_ref[...] = grad_pre
    grad_rows = contract_cols(grad_pre, first_ref[...]).astype(LOW).reshape(sources, half, blocks * LANES)
    for block in range(blocks):
        back_ref[:, block * half : (block + 1) * half, :] = grad_rows[
            :, :, block * LANES : (block + 1) * LANES
        ]
    source = iota((sources * EXTRA_ROWS, count), 1) >> shift
    row = iota((sources * EXTRA_ROWS, count), 0)
    high, low = [
        jnp.where(on_lane, part.astype(FULL), 0.0).astype(LOW) for part in split_low(gated)
    ]
    rows_back = dot((row == source * EXTRA_ROWS).astype(LOW), high) + dot(
        (row == source * EXTRA_ROWS + 1).astype(LOW), low
    )
    back_ref[:, blocks * half :, :] = rows_back.astype(LOW).reshape(sources, EXTRA_ROWS, LANES)


def expert_rows(h_rows, cot_rows, first_weight, second_weight, half):
    dp_count, rows_sent, _ = h_rows.shape
    width, hidden_width = first_weight.shape
    sources = min(dp_count, 256 // half)
    count = sources * half
    wide = lambda lanes, kind: jax.ShapeDtypeStruct((dp_count * half, lanes), kind)
    rows = lambda lanes: pl.BlockSpec((count, lanes), lambda i: (i, 0))
    block = lambda *shape: pl.BlockSpec((sources, *shape), lambda i: (i, 0, 0))
    whole = lambda array: pl.BlockSpec(array.shape, lambda i: (0, 0))
    return pl.pallas_call(
        lambda *refs: expert_kernel(half, *refs),
        grid=(dp_count // sources,),
        out_shape=[
            jax.ShapeDtypeStruct(h_rows.shape, LOW),
            wide(hidden_width, LOW),
            wide(hidden_width, LOW),
            wide(width, LOW),
            wide(LANES, FULL),
        ],
        in_specs=[
            block(rows_sent, LANES),
            block(half, width),
            whole(first_weight),
            whole(second_weight),
        ],
        out_specs=[
            block(rows_sent, LANES),
            rows(hidden_width),
            rows(hidden_width),
            rows(width),
            rows(LANES),
        ],
        compiler_params=pltpu.CompilerParams(vmem_limit_bytes=VMEM_BYTES),
        cost_estimate=pl.CostEstimate(
            flops=6 * dp_count * half * width * hidden_width,
            bytes_accessed=12 * dp_count * half * width,
            transcendentals=dp_count * half * hidden_width,
        ),
    )(h_rows, cot_rows, first_weight, second_weight)


def weight_kernel(half, h_ref, hid_ref, pre_ref, arr_ref, gate_ref, second_ref, first_in, second_in, out_ref, first_ref, second_out):
    @pl.when(pl.program_id(0) == 0)
    def _():
        first_ref[...] = first_in[...]
        second_out[...] = second_in[...]

    hidden = hid_ref[...]
    produced = dot(hidden, second_ref[...])
    out_ref[...] = (gate_ref[:, 0:1] * produced).astype(LOW)
    first_ref[...] += contract_rows(rows_of(h_ref, half), pre_ref[...])
    second_out[...] += contract_rows(hidden, arr_ref[...])


def expert_weights(h_rows, hidden, grad_pre, arrived, gate, second_weight, first_sum, second_sum, half):
    dp_count, rows_sent, _ = h_rows.shape
    hidden_width, width = second_weight.shape
    sources = min(dp_count, 512 // half)
    count = sources * half
    rows = lambda lanes: pl.BlockSpec((count, lanes), lambda i: (i, 0))
    whole = lambda array: pl.BlockSpec(array.shape, lambda i: (0, 0))
    return pl.pallas_call(
        lambda *refs: weight_kernel(half, *refs),
        grid=(dp_count // sources,),
        out_shape=[
            jax.ShapeDtypeStruct((dp_count * half, width), LOW),
            jax.ShapeDtypeStruct(first_sum.shape, FULL),
            jax.ShapeDtypeStruct(second_sum.shape, FULL),
        ],
        in_specs=[
            pl.BlockSpec((sources, rows_sent, LANES), lambda i: (i, 0, 0)),
            rows(hidden_width),
            rows(hidden_width),
            rows(width),
            rows(LANES),
            whole(second_weight),
            whole(first_sum),
            whole(second_sum),
        ],
        out_specs=[rows(width), whole(first_sum), whole(second_sum)],
        compiler_params=pltpu.CompilerParams(vmem_limit_bytes=VMEM_BYTES),
        cost_estimate=pl.CostEstimate(
            flops=6 * dp_count * half * width * hidden_width,
            bytes_accessed=10 * dp_count * half * width,
            transcendentals=0,
        ),
    )(h_rows, hidden, grad_pre, arrived, gate, second_weight, first_sum, second_sum)


def combine_kernel(base_ref, back_ref, slot_ref, col_ref, gates_ref, ext_ref, h_ref, part_ref, router_ref):
    experts, owners, rows_sent, _ = back_ref.shape
    blocks = h_ref.shape[1] // LANES
    half = (rows_sent - EXTRA_ROWS) // blocks
    count = experts * half
    slot_row = slot_ref[...]
    hits = slot_row >= 0
    here, of_expert = slot_tables(slot_row, base_ref[0], half)
    extra = back_ref[:, :, blocks * half :, :].reshape(experts * owners * EXTRA_ROWS, LANES)
    reach = owners * EXTRA_ROWS
    shift, reach_shift = half.bit_length() - 1, reach.bit_length() - 1
    row = iota((count, experts * reach), 1)
    wanted = (row >> reach_shift) == (iota((count, experts * reach), 0) >> shift)
    wanted = wanted & ((row & (EXTRA_ROWS - 1)) < 2)
    on_lane = iota((count, LANES), 1) == (iota((count, LANES), 0) & (half - 1))
    lanes = dot(wanted.astype(LOW), extra)
    slot_gated = jnp.sum(jnp.where(on_lane, lanes, 0.0), axis=1, keepdims=True)
    high, low = split_low(jnp.where(here, slot_gated, 0.0))
    gated = contract_rows(of_expert.astype(LOW), high) + contract_rows(of_expert.astype(LOW), low)
    gated = jnp.where(hits, gated, 0.0)
    logit_grad = gated - gates_ref[...] * jnp.sum(gated, axis=0, keepdims=True)
    logit_grad = jnp.where(hits, logit_grad, 0.0)
    high, low = split_low(logit_grad)
    router_ref[...] = dot(high, h_ref[...]) + dot(low, h_ref[...])
    router_rows = ext_ref[2 : 2 + experts, :].astype(LOW)
    span = owners * half
    span_shift = span.bit_length() - 1
    total = experts * span
    expand = (iota((experts, total), 1) >> span_shift) == iota((experts, total), 0)
    wanted = (iota((1, total), 1) & (half - 1)) + base_ref[0]
    one_hot = (dot(col_ref[...], expand.astype(LOW)) == wanted.astype(FULL)).astype(LOW)
    for block in range(blocks):
        rows = back_ref[:, :, block * half : (block + 1) * half, :].reshape(total, LANES)
        at = slice(block * LANES, (block + 1) * LANES)
        part_ref[:, at] = (
            dot(one_hot, rows)
            + contract_rows(high, router_rows[:, at])
            + contract_rows(low, router_rows[:, at])
        )


def backward_kernel(
    part_ref, other_ref, cot_ref, resid_ref, rows_ref, ext_ref, qk_ref, vx_ref, h_ref, qkv_ref, probs_ref,
    mixed_ref, router_ref, qk_out, vx_out, one_ref, rgrad_ref, qkg_ref, vg_ref,
):
    group_rows = rows_ref.shape[0]
    inner = qk_ref.shape[1] // 2
    h_grad = part_ref[...] + other_ref[...]
    residual = resid_ref[...]
    inv_two = inverse_rms(residual)
    normed_two = residual * inv_two
    gain_two_row = 0.5 * jnp.sum(h_grad * normed_two, axis=0, keepdims=True)
    scaled = h_grad * ext_ref[1:2, :]
    resid_grad = cot_ref[...] + inv_two * (
        scaled - normed_two * jnp.mean(scaled * normed_two, axis=1, keepdims=True)
    )
    rgrad_ref[...] = resid_grad
    attn_grad = resid_grad.astype(LOW)
    vx_out[:, inner : 2 * inner] = contract_rows(attn_grad, mixed_ref[...]).astype(LOW)
    mixed_grad = dot(attn_grad, vx_ref[:, inner : 2 * inner]).astype(LOW)
    low_lanes = iota((group_rows, LANES), 1) < HEAD_DIM
    for pair in range(inner // LANES):
        at = pair * LANES
        queries = qkv_ref[:, at : at + LANES]
        key_rows = qkv_ref[:, inner + at : inner + at + LANES]
        value_rows = qkv_ref[:, 2 * inner + at : 2 * inner + at + LANES]
        out_grad = mixed_grad[:, at : at + LANES]
        grads = []
        for sub in range(2):
            own = low_lanes if sub == 0 else ~low_lanes
            probs = probs_ref[2 * pair + sub]
            prob_grad = contract_cols(jnp.where(own, out_grad, jnp.zeros_like(out_grad)), value_rows)
            carry = jnp.sum(prob_grad * probs, axis=1, keepdims=True)
            score_grad = (probs * (prob_grad - carry)).astype(LOW)
            grads.append(
                (
                    dot(score_grad, key_rows),
                    contract_rows(score_grad, queries),
                    contract_rows(probs.astype(LOW), out_grad),
                )
            )
        scale = HEAD_DIM ** (-0.5)
        qkg_ref[:, at : at + LANES] = (jnp.where(low_lanes, grads[0][0], grads[1][0]) * scale).astype(LOW)
        qkg_ref[:, inner + at : inner + at + LANES] = (
            jnp.where(low_lanes, grads[0][1], grads[1][1]) * scale
        ).astype(LOW)
        vg_ref[:, at : at + LANES] = jnp.where(low_lanes, grads[0][2], grads[1][2]).astype(LOW)
    h_one = h_ref[...]
    qk_out[...] = contract_rows(h_one, qkg_ref[...]).astype(LOW)
    vx_out[:, :inner] = contract_rows(h_one, vg_ref[...]).astype(LOW)
    one_grad = contract_cols(qkg_ref[...], qk_ref[...]) + contract_cols(vg_ref[...], vx_ref[:, :inner])
    one_ref[...] = one_grad
    rows = rows_ref[...]
    gain_one_row = jnp.sum(one_grad * (rows * inverse_rms(rows)), axis=0, keepdims=True)
    router_rows = router_ref[...]
    sub = iota(router_rows.shape, 0)
    extra = jnp.where(sub == 0, gain_one_row, jnp.where(sub == 1, gain_two_row, router_rows))
    vx_out[:, 2 * inner :] = extra.T.astype(LOW)


def local(
    block_in,
    seq_lengths,
    routes,
    w_query,
    w_key,
    w_value,
    w_out_proj,
    router,
    gain_attn,
    gain_moe,
    expert_in,
    expert_out,
    cotangent,
):
    dp_count = lax.axis_size("dp")
    core = lax.axis_index("tensor")
    tok_rows, width = block_in.shape
    group_rows, top_count = routes.shape
    experts = router.shape[1]
    owners = dp_count // experts
    half = max(EXTRA_ROWS, top_count * group_rows // experts)
    slots = dp_count * half
    rows_sent = half * (width // LANES) + EXTRA_ROWS
    inner = w_query.shape[1]
    bits = dp_count.bit_length() - 1
    order_a, order_b = bit_orders()

    expert_ids = jnp.arange(experts, dtype=jnp.int32)
    hits = jnp.any(routes[:, :, None] == expert_ids[None, None, :], axis=1)
    places = jnp.arange(group_rows, dtype=jnp.int32)
    earlier = (places[:, None] > places[None, :]).astype(LOW)
    slot_col = jnp.where(hits, dot(earlier, hits.astype(LOW)), -1.0).astype(LOW)
    slot_row = slot_col.T
    base = core * half
    slot_ids = (base + jnp.arange(half, dtype=jnp.int32)).astype(LOW)
    in_slot = slot_row[:, None, :] == slot_ids[None, :, None]
    dispatch = (
        jnp.broadcast_to(in_slot[:, None], (experts, owners, half, group_rows))
        .astype(LOW)
        .reshape(slots, group_rows)
    )
    base = base.reshape(1).astype(jnp.int32)
    cot_picked = dot(dispatch, cotangent.astype(LOW)).astype(LOW).reshape(dp_count, half, width)

    extra_width = -(-(2 + experts) // LANES) * LANES
    extra = jnp.concatenate(
        [
            gain_attn[:, None],
            gain_moe[:, None],
            router,
            jnp.zeros((router.shape[0], extra_width - 2 - experts), LOW),
        ],
        axis=1,
    )
    qk_full = jnp.concatenate([w_query, w_key], axis=1)
    vx_full = jnp.concatenate([w_value, w_out_proj.T, extra], axis=1)
    qk_full = qk_full.reshape((1,) * bits + qk_full.shape)
    vx_full = vx_full.reshape((1,) * bits + vx_full.shape)
    for step in range(bits):
        vx_full = double(vx_full, order_b[step], bits)
        qk_full = double(qk_full, order_a[step], bits)
        if step == bits - 3:
            cot_picked, qk_full, vx_full = lax.optimization_barrier((cot_picked, qk_full, vx_full))
    qk_full = qk_full.reshape(width, 2 * inner)
    vx_full = vx_full.reshape(width, 2 * inner + extra_width)
    cot_own = trade(cot_picked)

    rows_all = lax.all_gather(block_in, "tensor", axis=0, tiled=True)
    shape = jax.ShapeDtypeStruct
    attn_part, h_one, qkv, probs, mixed, ext = call(
        attention_kernel,
        [
            shape((group_rows, width), FULL),
            shape((group_rows, width), LOW),
            shape((group_rows, 3 * inner), LOW),
            shape((inner // HEAD_DIM, group_rows, group_rows), FULL),
            shape((group_rows, inner), LOW),
            shape((extra_width, width), FULL),
        ],
        seq_lengths,
        rows_all,
        qk_full,
        vx_full,
        flops=8 * group_rows * width * inner + 4 * group_rows * group_rows * inner,
        smem=(0,),
    )
    attn_part, cot_own = lax.optimization_barrier((attn_part, cot_own))
    cot_other = swap(cot_own)

    residual, h_two, gates, sent = call(
        dispatch_kernel,
        [
            shape((group_rows, width), FULL),
            shape((group_rows, width), LOW),
            shape((experts, group_rows), FULL),
            shape((experts, owners, rows_sent, LANES), LOW),
        ],
        base,
        rows_all,
        attn_part,
        swap(attn_part),
        ext,
        slot_row,
        flops=2 * experts * half * group_rows * width,
        smem=(0,),
    )

    h_own = trade(sent.reshape(dp_count, rows_sent, LANES))
    h_other = swap(h_own)
    first_weight = expert_in[0]
    second_weight = expert_out[0]
    back_own, *own_kept = expert_rows(h_own, cot_own, first_weight, second_weight, half)
    back_other, *other_kept = expert_rows(h_other, cot_other, first_weight, second_weight, half)
    back = (back_own.astype(FULL) + swap(back_other).astype(FULL)).astype(LOW)
    back = trade(back)

    zeros = jnp.zeros((width, first_weight.shape[1]), FULL)
    out_other, first_sum, second_sum = expert_weights(
        h_other, *other_kept, second_weight, zeros, zeros.reshape(second_weight.shape), half
    )
    out_own, grad_first, grad_second = expert_weights(
        h_own, *own_kept, second_weight, first_sum, second_sum, half
    )
    out_rows = (out_own.astype(FULL) + swap(out_other).astype(FULL)).astype(LOW)
    out_rows, back = lax.optimization_barrier((out_rows, back))
    back_out = trade(out_rows.reshape(dp_count, half, width)).reshape(slots, width)

    h_part, router_part = call(
        combine_kernel,
        [shape((group_rows, width), FULL), shape((experts, width), FULL)],
        base,
        back.reshape(experts, owners, rows_sent, LANES),
        slot_row,
        slot_col,
        gates,
        ext,
        h_two,
        flops=2 * slots * group_rows * width,
        smem=(0,),
    )
    router_part = jnp.pad(router_part, ((2, extra_width - 2 - experts), (0, 0)))
    qk_part, vx_part, one_part, resid_grad, _, _ = call(
        backward_kernel,
        [
            shape((width, 2 * inner), LOW),
            shape((width, 2 * inner + extra_width), LOW),
            shape((group_rows, width), FULL),
            shape((group_rows, width), FULL),
            shape((group_rows, 2 * inner), LOW),
            shape((group_rows, inner), LOW),
        ],
        h_part,
        swap(h_part),
        cotangent,
        residual,
        rows_all,
        ext,
        qk_full,
        vx_full,
        h_one,
        qkv,
        probs,
        mixed,
        router_part,
        flops=20 * group_rows * width * inner + 12 * group_rows * group_rows * inner,
    )

    own_start = core * tok_rows
    other_start = (1 - core) * tok_rows

    def rows_at(values, start):
        return lax.dynamic_slice_in_dim(values, start, tok_rows, 0)

    one_other = swap(rows_at(one_part, other_start).astype(LOW)).astype(FULL)
    qk_sum = qk_part.reshape((2,) * bits + (width // dp_count, 2 * inner))
    vx_sum = vx_part.reshape((2,) * bits + (width // dp_count, 2 * inner + extra_width))
    for step in range(bits):
        vx_sum = halve(vx_sum, order_b[bits - 1 - step], bits)
        qk_sum = halve(qk_sum, order_a[bits - 1 - step], bits)
        if step == 1:
            vx_sum, qk_sum, back_out = lax.optimization_barrier((vx_sum, qk_sum, back_out))
    qk_sum = qk_sum.reshape(width // dp_count, 2 * inner)
    vx_sum = vx_sum.reshape(width // dp_count, 2 * inner + extra_width)

    out_part = contract_rows(dispatch, back_out)
    block_out = rows_at(residual, own_start) + (
        rows_at(out_part, own_start) + swap(rows_at(out_part, other_start))
    )
    scaled_one = (rows_at(one_part, own_start) + one_other) * ext[0:1, :]
    inv_own = inverse_rms(block_in)
    normed_own = block_in * inv_own
    grad_in = rows_at(resid_grad, own_start) + inv_own * (
        scaled_one - normed_own * jnp.mean(scaled_one * normed_own, axis=1, keepdims=True)
    )
    extra_sum = vx_sum[:, 2 * inner :]
    extra_sum = extra_sum + swap(extra_sum)
    share = extra_sum.shape[0] // 2
    extra_own = lax.dynamic_slice_in_dim(extra_sum, core * share, share, 0)
    return (
        block_out,
        grad_in,
        qk_sum[:, :inner],
        qk_sum[:, inner:],
        vx_sum[:, :inner],
        vx_sum[:, inner : 2 * inner].T,
        extra_own[:, 2 : 2 + experts],
        extra_own[:, 0],
        extra_own[:, 1],
        grad_first[None],
        grad_second[None],
    )


def solution(mesh):
    in_specs = (
        P(("dp", "tensor"), None),
        P("dp", None),
        P("dp", None),
        P("dp", "tensor"),
        P("dp", "tensor"),
        P("dp", "tensor"),
        P("tensor", "dp"),
        P("dp", None),
        P("dp"),
        P("dp"),
        P("dp", None, "tensor"),
        P("dp", "tensor", None),
        P("dp", None),
    )
    out_specs = (
        P(("dp", "tensor"), None),
        P(("dp", "tensor"), None),
        P("dp", "tensor"),
        P("dp", "tensor"),
        P("dp", "tensor"),
        P("tensor", "dp"),
        P(("dp", "tensor"), None),
        P(("dp", "tensor")),
        P(("dp", "tensor")),
        P("dp", None, "tensor"),
        P("dp", "tensor", None),
    )
    return jax.shard_map(local, mesh=mesh, in_specs=in_specs, out_specs=out_specs, check_vma=False)
```

```python
import math

import jax
import jax.numpy as jnp
from jax import lax
from jax.experimental import pallas as pl
from jax.experimental.pallas import tpu as pltpu
from jax.sharding import PartitionSpec as P

HEAD_DIM = 64
LANES = 128


EPSILON = 1e-06
NEGATIVE = -1e30
MIB = 1024 * 1024
EXTRA_ROWS = 16
LOW = jnp.bfloat16
FULL = jnp.float32


def dot(left_side, right_side):
    return jnp.dot(left_side, right_side, preferred_element_type=FULL)


def contract_rows(left_side, right_side):
    return lax.dot_general(
        left_side, right_side, (((0,), (0,)), ((), ())), preferred_element_type=FULL
    )


def contract_cols(left_side, right_side):
    return lax.dot_general(
        left_side, right_side, (((1,), (1,)), ((), ())), preferred_element_type=FULL
    )


def split_low(values):
    high = values.astype(LOW)
    return high, (values - high.astype(FULL)).astype(LOW)


def iota(shape, axis):
    return lax.broadcasted_iota(jnp.int32, shape, axis)


def swap(values):
    return lax.ppermute(values, "tensor", [(0, 1), (1, 0)])


def bit_orders():
    bits = lax.axis_size("dp").bit_length() - 1
    falling = list(range(bits - 1, -1, -1))
    return falling, falling[:-2] + [falling[-1], falling[-2]]


def partners(bit):
    return [(i, i ^ (1 << bit)) for i in range(lax.axis_size("dp"))]


def double(block, bit, bits):
    other = lax.ppermute(block, "dp", partners(bit))
    axis = bits - 1 - bit
    upper = ((lax.axis_index("dp") >> bit) & 1) == 1
    return jnp.where(
        upper,
        jnp.concatenate([other, block], axis=axis),
        jnp.concatenate([block, other], axis=axis),
    )


def halve(block, bit, bits):
    axis, place = bits - 1 - bit, (lax.axis_index("dp") >> bit) & 1
    given = lax.dynamic_index_in_dim(block, 1 - place, axis, keepdims=True).astype(LOW)
    kept = lax.dynamic_index_in_dim(block, place, axis, keepdims=True)
    return kept.astype(FULL) + lax.ppermute(given, "dp", partners(bit)).astype(FULL)


def trade(values):
    experts, dp_count = values.shape[0], lax.axis_size("dp")
    owners = dp_count // experts
    groups = [[owners * e + o for e in range(experts)] for o in range(owners)]
    return lax.all_to_all(
        values, "dp", split_axis=0, concat_axis=0, tiled=True, axis_index_groups=groups
    )


def cross(values):
    return lax.ppermute(values, "dp", partners(0))


def add_low(*parts):
    return sum(part.astype(FULL) for part in parts).astype(LOW)


def call(kernel, out_shape, *operands, flops=0, smem=(), limit=20):
    moved = sum(x.size * x.dtype.itemsize for x in (*operands, *out_shape))
    return pl.pallas_call(
        kernel,
        out_shape=out_shape,
        in_specs=[
            pl.BlockSpec(memory_space=pltpu.SMEM if i in smem else pltpu.VMEM)
            for i in range(len(operands))
        ],
        out_specs=[pl.BlockSpec(memory_space=pltpu.VMEM) for _ in out_shape],
        compiler_params=pltpu.CompilerParams(vmem_limit_bytes=limit * MIB),
        cost_estimate=pl.CostEstimate(flops=flops, bytes_accessed=moved, transcendentals=0),
    )(*operands)


def inverse_rms(rows):
    return lax.rsqrt(jnp.mean(rows * rows, axis=1, keepdims=True) + EPSILON)


GELU_SCALE = math.sqrt(2.0 / math.pi)
GELU_CUBE = 0.044715


def attention_kernel(
    len_ref, rows_ref, qk_ref, vx_ref, attn_ref, h_ref, qkv_ref, probs_ref, mixed_ref, ext_ref
):
    group_rows = rows_ref.shape[0]
    inner = qk_ref.shape[1] // 2
    rows = rows_ref[...]
    ext = vx_ref[:, 2 * inner :].astype(FULL).T
    ext_ref[...] = ext
    h_one = (rows * inverse_rms(rows) * ext[0:1, :]).astype(LOW)
    h_ref[...] = h_one
    qkv_ref[:, : 2 * inner] = dot(h_one, qk_ref[...]).astype(LOW)
    qkv_ref[:, 2 * inner :] = dot(h_one, vx_ref[:, :inner]).astype(LOW)
    down, across = iota((group_rows, group_rows), 0), iota((group_rows, group_rows), 1)
    allowed = down >= across
    end = jnp.int32(0)
    for place in range(len_ref.shape[1]):
        end = end + len_ref[0, place]
        allowed = allowed & ((down >= end) == (across >= end))
    low_lanes = iota((group_rows, LANES), 1) < HEAD_DIM
    for pair in range(inner // LANES):
        at = pair * LANES
        queries = qkv_ref[:, at : at + LANES]
        key_rows = qkv_ref[:, inner + at : inner + at + LANES]
        value_rows = qkv_ref[:, 2 * inner + at : 2 * inner + at + LANES]
        outs = []
        for sub in range(2):
            own = low_lanes if sub == 0 else ~low_lanes
            scores = contract_cols(jnp.where(own, queries, jnp.zeros_like(queries)), key_rows)
            scores = jnp.where(allowed, scores * HEAD_DIM ** (-0.5), NEGATIVE)
            terms = jnp.exp(scores - jnp.max(scores, axis=1, keepdims=True))
            probs = terms / jnp.sum(terms, axis=1, keepdims=True)
            probs_ref[2 * pair + sub] = probs
            outs.append(dot(probs.astype(LOW), value_rows))
        mixed_ref[:, at : at + LANES] = jnp.where(low_lanes, outs[0], outs[1]).astype(LOW)
    attn_ref[...] = contract_cols(mixed_ref[...], vx_ref[:, inner : 2 * inner])


def slot_tables(slot_row, base, half):
    experts, group_rows = slot_row.shape
    count, shift = experts * half, half.bit_length() - 1
    of_expert = (iota((count, experts), 0) >> shift) == iota((count, experts), 1)
    wanted = (iota((count, 1), 0) & (half - 1)) + base
    here = dot(of_expert.astype(LOW), slot_row) == wanted.astype(FULL)
    return here, of_expert


def dispatch_kernel(
    base_ref, rows_ref, attn_ref, other_ref, ext_ref, slot_ref, resid_ref, h_ref, gates_ref, send_ref
):
    experts, rows_sent, _ = send_ref.shape
    blocks = rows_ref.shape[1] // LANES
    half = (rows_sent - EXTRA_ROWS) // blocks
    count = experts * half
    residual = rows_ref[...] + (attn_ref[...] + other_ref[...])
    resid_ref[...] = residual
    h_two = (residual * inverse_rms(residual) * ext_ref[1:2, :]).astype(LOW)
    h_ref[...] = h_two
    slot_row = slot_ref[...]
    hits = slot_row >= 0
    all_logits = contract_cols(ext_ref[...].astype(LOW), h_two)
    logits = all_logits[2 : 2 + experts, :]
    peak = jnp.max(jnp.where(hits, logits, NEGATIVE), axis=0, keepdims=True)
    terms = jnp.where(hits, jnp.exp(jnp.where(hits, logits - peak, 0.0)), 0.0)
    gates = terms / jnp.sum(terms, axis=0, keepdims=True)
    gates_ref[...] = gates
    here, of_expert = slot_tables(slot_row, base_ref[0], half)
    one_hot = here.astype(LOW)
    picked = dot(one_hot, h_two).astype(LOW).reshape(experts, half, blocks * LANES)
    high, low = split_low(gates)
    by_expert = contract_cols(one_hot, high) + contract_cols(one_hot, low)
    gate_col = jnp.sum(jnp.where(of_expert, by_expert, 0.0), axis=1, keepdims=True)
    on_lane = iota((count, LANES), 1) == (iota((count, LANES), 0) & (half - 1))
    high_rows, low_rows = [
        contract_rows(of_expert.astype(LOW), jnp.where(on_lane, part.astype(FULL), 0.0).astype(LOW))
        for part in split_low(gate_col)
    ]
    sub = iota((EXTRA_ROWS, LANES), 0)
    for block in range(blocks):
        send_ref[:, block * half : (block + 1) * half, :] = picked[
            :, :, block * LANES : (block + 1) * LANES
        ]
    for expert in range(experts):
        send_ref[expert, blocks * half :, :] = jnp.where(
            sub == 0,
            high_rows[expert : expert + 1, :],
            jnp.where(sub == 1, low_rows[expert : expert + 1, :], 0.0),
        ).astype(LOW)


def rows_of(ref, half):
    blocks = (ref.shape[1] - EXTRA_ROWS) // half
    return jnp.concatenate(
        [
            ref[:, at * half : (at + 1) * half, :].reshape(ref.shape[0] * half, LANES)
            for at in range(blocks)
        ],
        axis=1,
    )


def expert_step(half, h_ref, cot_ref, first_ref, second_ref, back_ref, hid_ref, pre_ref, out_ref, gate_ref):
    sources = h_ref.shape[0]
    blocks = (h_ref.shape[1] - EXTRA_ROWS) // half
    count, shift = sources * half, half.bit_length() - 1
    extra = h_ref[:, blocks * half :, :].reshape(sources * EXTRA_ROWS, LANES)
    source = iota((count, sources * EXTRA_ROWS), 0) >> shift
    row = iota((count, sources * EXTRA_ROWS), 1)
    two_rows = (row == source * EXTRA_ROWS) | (row == source * EXTRA_ROWS + 1)
    on_lane = iota((count, LANES), 1) == (iota((count, LANES), 0) & (half - 1))
    gate_lanes = dot(two_rows.astype(LOW), extra)
    gate = jnp.sum(jnp.where(on_lane, gate_lanes, 0.0), axis=1, keepdims=True)
    gate_ref[...] = jnp.broadcast_to(gate, (count, LANES))
    arrived = (gate * cot_ref[...].reshape(count, blocks * LANES).astype(FULL)).astype(LOW)
    out_ref[...] = arrived
    incoming = rows_of(h_ref, half)
    pre = dot(incoming, first_ref[...])
    grad_hidden = contract_cols(arrived, second_ref[...])
    square = pre * pre
    bend = jnp.tanh(GELU_SCALE * pre * (1.0 + GELU_CUBE * square))
    rise = 0.5 * (1.0 + bend)
    hidden = (pre * rise).astype(LOW)
    hid_ref[...] = hidden
    slope = rise + (0.5 * GELU_SCALE) * pre * (1.0 - bend * bend) * (1.0 + 3.0 * GELU_CUBE * square)
    gated = jnp.sum(hidden.astype(FULL) * grad_hidden, axis=1, keepdims=True)
    grad_pre = (grad_hidden * slope).astype(LOW)
    pre_ref[...] = grad_pre
    grad_rows = contract_cols(grad_pre, first_ref[...]).astype(LOW).reshape(sources, half, blocks * LANES)
    for block in range(blocks):
        back_ref[:, block * half : (block + 1) * half, :] = grad_rows[
            :, :, block * LANES : (block + 1) * LANES
        ]
    source = iota((sources * EXTRA_ROWS, count), 1) >> shift
    row = iota((sources * EXTRA_ROWS, count), 0)
    high, low = [
        jnp.where(on_lane, part.astype(FULL), 0.0).astype(LOW) for part in split_low(gated)
    ]
    rows_back = dot((row == source * EXTRA_ROWS).astype(LOW), high) + dot(
        (row == source * EXTRA_ROWS + 1).astype(LOW), low
    )
    back_ref[:, blocks * half :, :] = rows_back.astype(LOW).reshape(sources, EXTRA_ROWS, LANES)


def part_specs(sources, steps, shapes):
    maps = (lambda i: (jnp.minimum(i, steps - 1), 0, 0), lambda i: (jnp.maximum(i - steps, 0), 0, 0))
    return [pl.BlockSpec((sources, *shape), place) for shape in shapes for place in maps]


def in_halves(steps, first, second):
    pl.when(pl.program_id(0) < steps)(first)
    pl.when(pl.program_id(0) >= steps)(second)


def whole(array):
    return pl.BlockSpec(array.shape, lambda i: (0,) * array.ndim, pipeline_mode=pl.Buffered(1))


def expert_rows(h_rows, cot_rows, first_weight, second_weight, half):
    experts, rows_sent, _ = h_rows[0].shape
    width, hidden_width = first_weight.shape
    sources = min(experts, 256 // half)
    count, steps = sources * half, experts // sources
    total = 2 * experts * half

    def kernel(h_a, h_b, cot_a, cot_b, first_ref, second_ref, back_a, back_b, *kept):
        in_halves(
            steps,
            lambda: expert_step(half, h_a, cot_a, first_ref, second_ref, back_a, *kept),
            lambda: expert_step(half, h_b, cot_b, first_ref, second_ref, back_b, *kept),
        )

    lanes = ((hidden_width, LOW), (hidden_width, LOW), (width, LOW), (LANES, FULL))
    back_a, back_b, *kept = pl.pallas_call(
        kernel,
        grid=(2 * steps,),
        out_shape=[jax.ShapeDtypeStruct(h_rows[0].shape, LOW)] * 2
        + [jax.ShapeDtypeStruct((total, n), kind) for n, kind in lanes],
        in_specs=part_specs(sources, steps, [(rows_sent, LANES), (half, width)])
        + [whole(first_weight), whole(second_weight)],
        out_specs=part_specs(sources, steps, [(rows_sent, LANES)])
        + [pl.BlockSpec((count, n), lambda i: (i, 0)) for n, _ in lanes],
        compiler_params=pltpu.CompilerParams(vmem_limit_bytes=24 * MIB),
        cost_estimate=pl.CostEstimate(
            flops=6 * total * width * hidden_width,
            bytes_accessed=12 * total * width,
            transcendentals=total * hidden_width,
        ),
    )(*h_rows, *cot_rows, first_weight, second_weight)
    return back_a, back_b, kept


def expert_weights(h_rows, kept, second_weight, sums, half):
    experts, rows_sent, _ = h_rows[0].shape
    hidden_width, width = second_weight.shape
    sources = min(experts, 256 // half)
    count, steps = sources * half, experts // sources
    total = 2 * experts * half

    def kernel(h_a, h_b, hid_ref, pre_ref, arr_ref, gate_ref, second_ref, *refs):
        out_a, out_b, grad_first, grad_second = refs[-4:]

        @pl.when(pl.program_id(0) == 0)
        def _():
            for at, grad in enumerate((grad_first, grad_second)):
                grad[...] = refs[at][...] if sums else jnp.zeros(grad.shape, FULL)

        def step(h_ref, out_ref):
            hidden = hid_ref[...]
            produced = dot(hidden, second_ref[...])
            out_ref[...] = (gate_ref[:, 0:1] * produced).astype(LOW).reshape(out_ref.shape)
            grad_first[...] += contract_rows(rows_of(h_ref, half), pre_ref[...])
            grad_second[...] += contract_rows(hidden, arr_ref[...])

        in_halves(steps, lambda: step(h_a, out_a), lambda: step(h_b, out_b))

    shape = jax.ShapeDtypeStruct
    grads = [shape((width, hidden_width), FULL), shape((hidden_width, width), FULL)]
    return pl.pallas_call(
        kernel,
        grid=(2 * steps,),
        out_shape=[shape((experts, half, width), LOW)] * 2 + grads,
        in_specs=part_specs(sources, steps, [(rows_sent, LANES)])
        + [pl.BlockSpec((count, x.shape[1]), lambda i: (i, 0)) for x in kept]
        + [whole(x) for x in (second_weight, *sums)],
        out_specs=part_specs(sources, steps, [(half, width)]) + [whole(x) for x in grads],
        compiler_params=pltpu.CompilerParams(vmem_limit_bytes=32 * MIB),
        cost_estimate=pl.CostEstimate(
            flops=6 * total * width * hidden_width,
            bytes_accessed=10 * total * width,
            transcendentals=0,
        ),
    )(*h_rows, *kept, second_weight, *sums)


def combine_kernel(base_ref, back_ref, slot_ref, col_ref, gates_ref, ext_ref, h_ref, part_ref, router_ref):
    experts, rows_sent, _ = back_ref.shape
    blocks = h_ref.shape[1] // LANES
    half = (rows_sent - EXTRA_ROWS) // blocks
    count = experts * half
    slot_row = slot_ref[...]
    hits = slot_row >= 0
    here, of_expert = slot_tables(slot_row, base_ref[0], half)
    extra = back_ref[:, blocks * half :, :].reshape(experts * EXTRA_ROWS, LANES)
    reach = EXTRA_ROWS
    shift, reach_shift = half.bit_length() - 1, reach.bit_length() - 1
    row = iota((count, experts * reach), 1)
    wanted = (row >> reach_shift) == (iota((count, experts * reach), 0) >> shift)
    wanted = wanted & ((row & (EXTRA_ROWS - 1)) < 2)
    on_lane = iota((count, LANES), 1) == (iota((count, LANES), 0) & (half - 1))
    lanes = dot(wanted.astype(LOW), extra)
    slot_gated = jnp.sum(jnp.where(on_lane, lanes, 0.0), axis=1, keepdims=True)
    high, low = split_low(jnp.where(here, slot_gated, 0.0))
    gated = contract_rows(of_expert.astype(LOW), high) + contract_rows(of_expert.astype(LOW), low)
    gated = jnp.where(hits, gated, 0.0)
    logit_grad = gated - gates_ref[...] * jnp.sum(gated, axis=0, keepdims=True)
    logit_grad = jnp.where(hits, logit_grad, 0.0)
    high, low = split_low(logit_grad)
    router_ref[...] = dot(high, h_ref[...]) + dot(low, h_ref[...])
    router_rows = ext_ref[2 : 2 + experts, :].astype(LOW)
    expand = (iota((experts, count), 1) >> shift) == iota((experts, count), 0)
    wanted = (iota((1, count), 1) & (half - 1)) + base_ref[0]
    one_hot = (dot(col_ref[...], expand.astype(LOW)) == wanted.astype(FULL)).astype(LOW)
    for block in range(blocks):
        rows = back_ref[:, block * half : (block + 1) * half, :].reshape(count, LANES)
        at = slice(block * LANES, (block + 1) * LANES)
        part_ref[:, at] = (
            dot(one_hot, rows)
            + contract_rows(high, router_rows[:, at])
            + contract_rows(low, router_rows[:, at])
        )


def backward_kernel(
    part_ref, other_ref, cot_ref, resid_ref, rows_ref, ext_ref, qk_ref, vx_ref, h_ref, qkv_ref, probs_ref,
    mixed_ref, router_ref, qk_out, vx_out, one_ref, rgrad_ref, qkg_ref, vg_ref,
):
    group_rows = rows_ref.shape[0]
    inner = qk_ref.shape[1] // 2
    h_grad = part_ref[...] + other_ref[...]
    residual = resid_ref[...]
    inv_two = inverse_rms(residual)
    normed_two = residual * inv_two
    gain_two_row = 0.5 * jnp.sum(h_grad * normed_two, axis=0, keepdims=True)
    scaled = h_grad * ext_ref[1:2, :]
    resid_grad = cot_ref[...] + inv_two * (
        scaled - normed_two * jnp.mean(scaled * normed_two, axis=1, keepdims=True)
    )
    rgrad_ref[...] = resid_grad
    attn_grad = resid_grad.astype(LOW)
    vx_out[:, inner : 2 * inner] = contract_rows(attn_grad, mixed_ref[...]).astype(LOW)
    mixed_grad = dot(attn_grad, vx_ref[:, inner : 2 * inner]).astype(LOW)
    low_lanes = iota((group_rows, LANES), 1) < HEAD_DIM
    for pair in range(inner // LANES):
        at = pair * LANES
        queries = qkv_ref[:, at : at + LANES]
        key_rows = qkv_ref[:, inner + at : inner + at + LANES]
        value_rows = qkv_ref[:, 2 * inner + at : 2 * inner + at + LANES]
        out_grad = mixed_grad[:, at : at + LANES]
        grads = []
        for sub in range(2):
            own = low_lanes if sub == 0 else ~low_lanes
            probs = probs_ref[2 * pair + sub]
            prob_grad = contract_cols(jnp.where(own, out_grad, jnp.zeros_like(out_grad)), value_rows)
            carry = jnp.sum(prob_grad * probs, axis=1, keepdims=True)
            score_grad = (probs * (prob_grad - carry)).astype(LOW)
            grads.append(
                (
                    dot(score_grad, key_rows),
                    contract_rows(score_grad, queries),
                    contract_rows(probs.astype(LOW), out_grad),
                )
            )
        scale = HEAD_DIM ** (-0.5)
        qkg_ref[:, at : at + LANES] = (jnp.where(low_lanes, grads[0][0], grads[1][0]) * scale).astype(LOW)
        qkg_ref[:, inner + at : inner + at + LANES] = (
            jnp.where(low_lanes, grads[0][1], grads[1][1]) * scale
        ).astype(LOW)
        vg_ref[:, at : at + LANES] = jnp.where(low_lanes, grads[0][2], grads[1][2]).astype(LOW)
    h_one = h_ref[...]
    qk_out[...] = contract_rows(h_one, qkg_ref[...]).astype(LOW)
    vx_out[:, :inner] = contract_rows(h_one, vg_ref[...]).astype(LOW)
    one_grad = contract_cols(qkg_ref[...], qk_ref[...]) + contract_cols(vg_ref[...], vx_ref[:, :inner])
    one_ref[...] = one_grad
    rows = rows_ref[...]
    gain_one_row = jnp.sum(one_grad * (rows * inverse_rms(rows)), axis=0, keepdims=True)
    router_rows = router_ref[...]
    sub = iota(router_rows.shape, 0)
    extra = jnp.where(sub == 0, gain_one_row, jnp.where(sub == 1, gain_two_row, router_rows))
    vx_out[:, 2 * inner :] = extra.T.astype(LOW)


def local(
    block_in,
    seq_lengths,
    routes,
    w_query,
    w_key,
    w_value,
    w_out_proj,
    router,
    gain_attn,
    gain_moe,
    expert_in,
    expert_out,
    cotangent,
):
    dp_count = lax.axis_size("dp")
    core = lax.axis_index("tensor")
    tok_rows, width = block_in.shape
    group_rows, top_count = routes.shape
    experts = router.shape[1]
    half = max(EXTRA_ROWS, top_count * group_rows // experts)
    slots = experts * half
    rows_sent = half * (width // LANES) + EXTRA_ROWS
    inner = w_query.shape[1]
    bits = dp_count.bit_length() - 1
    order_a, order_b = bit_orders()

    expert_ids = jnp.arange(experts, dtype=jnp.int32)
    hits = jnp.any(routes[:, :, None] == expert_ids[None, None, :], axis=1)
    places = jnp.arange(group_rows, dtype=jnp.int32)
    earlier = (places[:, None] > places[None, :]).astype(LOW)
    slot_col = jnp.where(hits, dot(earlier, hits.astype(LOW)), -1.0).astype(LOW)
    slot_row = slot_col.T
    base = core * half
    slot_ids = (base + jnp.arange(half, dtype=jnp.int32)).astype(LOW)
    in_slot = slot_row[:, None, :] == slot_ids[None, :, None]
    dispatch = in_slot.astype(LOW).reshape(slots, group_rows)
    base = base.reshape(1).astype(jnp.int32)
    cot_picked = dot(dispatch, cotangent.astype(LOW)).astype(LOW).reshape(experts, half, width)

    extra_width = -(-(2 + experts) // LANES) * LANES
    extra = jnp.concatenate(
        [
            gain_attn[:, None],
            gain_moe[:, None],
            router,
            jnp.zeros((router.shape[0], extra_width - 2 - experts), LOW),
        ],
        axis=1,
    )
    qk_full = jnp.concatenate([w_query, w_key], axis=1)
    vx_full = jnp.concatenate([w_value, w_out_proj.T, extra], axis=1)
    qk_full = qk_full.reshape((1,) * bits + qk_full.shape)
    vx_full = vx_full.reshape((1,) * bits + vx_full.shape)
    for step in range(bits):
        vx_full = double(vx_full, order_b[step], bits)
        qk_full = double(qk_full, order_a[step], bits)
        if step == bits - 2:
            cot_picked, qk_full, vx_full = lax.optimization_barrier((cot_picked, qk_full, vx_full))
    qk_full = qk_full.reshape(width, 2 * inner)
    vx_full = vx_full.reshape(width, 2 * inner + extra_width)
    cot_own = trade(cot_picked)

    rows_all = lax.all_gather(block_in, "tensor", axis=0, tiled=True)
    shape = jax.ShapeDtypeStruct
    attn_part, h_one, qkv, probs, mixed, ext = call(
        attention_kernel,
        [
            shape((group_rows, width), FULL),
            shape((group_rows, width), LOW),
            shape((group_rows, 3 * inner), LOW),
            shape((inner // HEAD_DIM, group_rows, group_rows), FULL),
            shape((group_rows, inner), LOW),
            shape((extra_width, width), FULL),
        ],
        seq_lengths,
        rows_all,
        qk_full,
        vx_full,
        flops=8 * group_rows * width * inner + 4 * group_rows * group_rows * inner,
        smem=(0,),
    )
    residual, h_two, gates, sent = call(
        dispatch_kernel,
        [
            shape((group_rows, width), FULL),
            shape((group_rows, width), LOW),
            shape((experts, group_rows), FULL),
            shape((experts, rows_sent, LANES), LOW),
        ],
        base,
        rows_all,
        attn_part,
        swap(attn_part),
        ext,
        slot_row,
        flops=2 * experts * half * group_rows * width,
        smem=(0,),
    )

    sent, cot_own = lax.optimization_barrier((sent, cot_own))
    cot_crossed = cross(cot_own)
    cot_own = (cot_own, swap(cot_own))
    cot_far = (cot_crossed, swap(cot_crossed))
    h_own = trade(sent)
    h_crossed = cross(h_own)
    h_own = (h_own, swap(h_own))
    h_far = (h_crossed, swap(h_crossed))
    first_weight = expert_in[0]
    second_weight = expert_out[0]
    own_back, own_given, own_kept = expert_rows(h_own, cot_own, first_weight, second_weight, half)
    far_back, far_given, far_kept = expert_rows(h_far, cot_far, first_weight, second_weight, half)
    far_total = cross(add_low(far_back, swap(far_given)))
    back = trade(add_low(own_back, swap(own_given), far_total))

    far_out, far_given, *sums = expert_weights(h_far, far_kept, second_weight, (), half)
    own_out, own_given, grad_first, grad_second = expert_weights(
        h_own, own_kept, second_weight, sums, half
    )
    far_total = cross(add_low(far_out, swap(far_given)))
    out_rows = add_low(own_out, swap(own_given), far_total)
    out_rows, back = lax.optimization_barrier((out_rows, back))
    back_out = trade(out_rows).reshape(slots, width)

    h_part, router_part = call(
        combine_kernel,
        [shape((group_rows, width), FULL), shape((experts, width), FULL)],
        base,
        back,
        slot_row,
        slot_col,
        gates,
        ext,
        h_two,
        flops=2 * slots * group_rows * width,
        smem=(0,),
    )
    router_part = jnp.pad(router_part, ((2, extra_width - 2 - experts), (0, 0)))
    qk_part, vx_part, one_part, resid_grad, _, _ = call(
        backward_kernel,
        [
            shape((width, 2 * inner), LOW),
            shape((width, 2 * inner + extra_width), LOW),
            shape((group_rows, width), FULL),
            shape((group_rows, width), FULL),
            shape((group_rows, 2 * inner), LOW),
            shape((group_rows, inner), LOW),
        ],
        h_part,
        swap(h_part),
        cotangent,
        residual,
        rows_all,
        ext,
        qk_full,
        vx_full,
        h_one,
        qkv,
        probs,
        mixed,
        router_part,
        flops=20 * group_rows * width * inner + 12 * group_rows * group_rows * inner,
    )

    own_start = core * tok_rows
    other_start = (1 - core) * tok_rows

    def rows_at(values, start):
        return lax.dynamic_slice_in_dim(values, start, tok_rows, 0)

    one_other = swap(rows_at(one_part, other_start).astype(LOW)).astype(FULL)
    qk_sum = qk_part.reshape((2,) * bits + (width // dp_count, 2 * inner))
    vx_sum = vx_part.reshape((2,) * bits + (width // dp_count, 2 * inner + extra_width))
    for step in range(bits):
        vx_sum = halve(vx_sum, order_b[bits - 1 - step], bits)
        qk_sum = halve(qk_sum, order_a[bits - 1 - step], bits)
        if step == 1:
            vx_sum, qk_sum, back_out = lax.optimization_barrier((vx_sum, qk_sum, back_out))
    qk_sum = qk_sum.reshape(width // dp_count, 2 * inner)
    vx_sum = vx_sum.reshape(width // dp_count, 2 * inner + extra_width)

    out_part = contract_rows(dispatch, back_out)
    block_out = rows_at(residual, own_start) + (
        rows_at(out_part, own_start) + swap(rows_at(out_part, other_start))
    )
    scaled_one = (rows_at(one_part, own_start) + one_other) * ext[0:1, :]
    inv_own = inverse_rms(block_in)
    normed_own = block_in * inv_own
    grad_in = rows_at(resid_grad, own_start) + inv_own * (
        scaled_one - normed_own * jnp.mean(scaled_one * normed_own, axis=1, keepdims=True)
    )
    extra_sum = vx_sum[:, 2 * inner :]
    extra_sum = extra_sum + swap(extra_sum)
    share = extra_sum.shape[0] // 2
    extra_own = lax.dynamic_slice_in_dim(extra_sum, core * share, share, 0)
    return (
        block_out,
        grad_in,
        qk_sum[:, :inner],
        qk_sum[:, inner:],
        vx_sum[:, :inner],
        vx_sum[:, inner : 2 * inner].T,
        extra_own[:, 2 : 2 + experts],
        extra_own[:, 0],
        extra_own[:, 1],
        grad_first[None],
        grad_second[None],
    )


def solution(mesh):
    in_specs = (
        P(("dp", "tensor"), None),
        P("dp", None),
        P("dp", None),
        P("dp", "tensor"),
        P("dp", "tensor"),
        P("dp", "tensor"),
        P("tensor", "dp"),
        P("dp", None),
        P("dp"),
        P("dp"),
        P("dp", None, "tensor"),
        P("dp", "tensor", None),
        P("dp", None),
    )
    out_specs = (
        P(("dp", "tensor"), None),
        P(("dp", "tensor"), None),
        P("dp", "tensor"),
        P("dp", "tensor"),
        P("dp", "tensor"),
        P("tensor", "dp"),
        P(("dp", "tensor"), None),
        P(("dp", "tensor")),
        P(("dp", "tensor")),
        P("dp", None, "tensor"),
        P("dp", "tensor", None),
    )
    return jax.shard_map(local, mesh=mesh, in_specs=in_specs, out_specs=out_specs, check_vma=False)
```

```python
import math

import jax
import jax.numpy as jnp
from jax import lax
from jax.experimental import pallas as pl
from jax.experimental.pallas import tpu as pltpu
from jax.sharding import PartitionSpec as P

HEAD_DIM = 64
LANES = 128


EPSILON = 1e-06
NEGATIVE = -1e30
MIB = 1024 * 1024
EXTRA_ROWS = 16
LOW = jnp.bfloat16
FULL = jnp.float32


def dot(left_side, right_side):
    return jnp.dot(left_side, right_side, preferred_element_type=FULL)


def contract_rows(left_side, right_side):
    return lax.dot_general(
        left_side, right_side, (((0,), (0,)), ((), ())), preferred_element_type=FULL
    )


def contract_cols(left_side, right_side):
    return lax.dot_general(
        left_side, right_side, (((1,), (1,)), ((), ())), preferred_element_type=FULL
    )


def split_low(values):
    high = values.astype(LOW)
    return high, (values - high.astype(FULL)).astype(LOW)


def iota(shape, axis):
    return lax.broadcasted_iota(jnp.int32, shape, axis)


def swap(values):
    return lax.ppermute(values, "tensor", [(0, 1), (1, 0)])


def bit_orders():
    bits = lax.axis_size("dp").bit_length() - 1
    falling = list(range(bits - 1, -1, -1))
    return falling, falling[:-2] + [falling[-1], falling[-2]]


def partners(bit):
    return [(i, i ^ (1 << bit)) for i in range(lax.axis_size("dp"))]


def double(block, bit, bits):
    other = lax.ppermute(block, "dp", partners(bit))
    axis = bits - 1 - bit
    upper = ((lax.axis_index("dp") >> bit) & 1) == 1
    return jnp.where(
        upper,
        jnp.concatenate([other, block], axis=axis),
        jnp.concatenate([block, other], axis=axis),
    )


def halve(block, bit, bits):
    axis, place = bits - 1 - bit, (lax.axis_index("dp") >> bit) & 1
    given = lax.dynamic_index_in_dim(block, 1 - place, axis, keepdims=True).astype(LOW)
    kept = lax.dynamic_index_in_dim(block, place, axis, keepdims=True)
    return kept.astype(FULL) + lax.ppermute(given, "dp", partners(bit)).astype(FULL)


def trade(values):
    experts, dp_count = values.shape[0], lax.axis_size("dp")
    owners = dp_count // experts
    groups = [[owners * e + o for e in range(experts)] for o in range(owners)]
    return lax.all_to_all(
        values, "dp", split_axis=0, concat_axis=0, tiled=True, axis_index_groups=groups
    )


def cross(values):
    return lax.ppermute(values, "dp", partners(0))


def after(values, *others):
    return lax.optimization_barrier((values, *others))[0]


def add_low(*parts):
    return sum(part.astype(FULL) for part in parts).astype(LOW)


def far(values):
    return pltpu.with_memory_space_constraint(values, pltpu.HBM)


def near_shape(shape, kind):
    return jax.ShapeDtypeStruct(shape, kind)


def far_shape(shape, kind):
    return pltpu.HBM(shape, kind)


def call(kernel, out_shape, *operands, flops=0, smem=(), limit=8):
    moved = sum(x.size * x.dtype.itemsize for x in operands)
    return pl.pallas_call(
        kernel,
        out_shape=out_shape,
        in_specs=[
            pl.BlockSpec(memory_space=pltpu.SMEM if i in smem else pltpu.VMEM)
            for i in range(len(operands))
        ],
        out_specs=[pl.BlockSpec(memory_space=pltpu.VMEM) for _ in out_shape],
        compiler_params=pltpu.CompilerParams(vmem_limit_bytes=limit * MIB),
        cost_estimate=pl.CostEstimate(flops=flops, bytes_accessed=2 * moved, transcendentals=0),
    )(*operands)


def inverse_rms(rows):
    return lax.rsqrt(jnp.mean(rows * rows, axis=1, keepdims=True) + EPSILON)


GELU_SCALE = math.sqrt(2.0 / math.pi)
GELU_CUBE = 0.044715


def attention_kernel(
    len_ref, rows_ref, qk_ref, vx_ref, attn_ref, ext_ref, h_ref, qkv_ref, probs_ref, mixed_ref, rows_out, qk_out, vx_out
):
    group_rows = rows_ref.shape[0]
    inner = qk_ref.shape[1] // 2
    rows = rows_ref[...]
    rows_out[...] = rows
    qk_out[...] = qk_ref[...]
    vx_out[...] = vx_ref[...]
    ext = vx_ref[:, 2 * inner :].astype(FULL).T
    ext_ref[...] = ext
    h_one = (rows * inverse_rms(rows) * ext[0:1, :]).astype(LOW)
    h_ref[...] = h_one
    qkv_ref[:, : 2 * inner] = dot(h_one, qk_ref[...]).astype(LOW)
    qkv_ref[:, 2 * inner :] = dot(h_one, vx_ref[:, :inner]).astype(LOW)
    down, across = iota((group_rows, group_rows), 0), iota((group_rows, group_rows), 1)
    allowed = down >= across
    end = jnp.int32(0)
    for place in range(len_ref.shape[1]):
        end = end + len_ref[0, place]
        allowed = allowed & ((down >= end) == (across >= end))
    low_lanes = iota((group_rows, LANES), 1) < HEAD_DIM
    for pair in range(inner // LANES):
        at = pair * LANES
        queries = qkv_ref[:, at : at + LANES]
        key_rows = qkv_ref[:, inner + at : inner + at + LANES]
        value_rows = qkv_ref[:, 2 * inner + at : 2 * inner + at + LANES]
        outs = []
        for sub in range(2):
            own = low_lanes if sub == 0 else ~low_lanes
            scores = contract_cols(jnp.where(own, queries, jnp.zeros_like(queries)), key_rows)
            scores = jnp.where(allowed, scores * HEAD_DIM ** (-0.5), NEGATIVE)
            terms = jnp.exp(scores - jnp.max(scores, axis=1, keepdims=True))
            probs = terms / jnp.sum(terms, axis=1, keepdims=True)
            probs_ref[2 * pair + sub] = probs
            outs.append(dot(probs.astype(LOW), value_rows))
        mixed_ref[:, at : at + LANES] = jnp.where(low_lanes, outs[0], outs[1]).astype(LOW)
    attn_ref[...] = contract_cols(mixed_ref[...], vx_ref[:, inner : 2 * inner])


def slot_tables(slot_row, base, half):
    experts, group_rows = slot_row.shape
    count, shift = experts * half, half.bit_length() - 1
    of_expert = (iota((count, experts), 0) >> shift) == iota((count, experts), 1)
    wanted = (iota((count, 1), 0) & (half - 1)) + base
    here = dot(of_expert.astype(LOW), slot_row) == wanted.astype(FULL)
    return here, of_expert


def dispatch_kernel(
    base_ref, rows_ref, attn_ref, other_ref, ext_ref, slot_ref, resid_ref, h_ref, gates_ref, send_ref
):
    experts, rows_sent, _ = send_ref.shape
    blocks = rows_ref.shape[1] // LANES
    half = (rows_sent - EXTRA_ROWS) // blocks
    count = experts * half
    residual = rows_ref[...] + (attn_ref[...] + other_ref[...])
    resid_ref[...] = residual
    h_two = (residual * inverse_rms(residual) * ext_ref[1:2, :]).astype(LOW)
    h_ref[...] = h_two
    slot_row = slot_ref[...]
    hits = slot_row >= 0
    all_logits = contract_cols(ext_ref[...].astype(LOW), h_two)
    logits = all_logits[2 : 2 + experts, :]
    peak = jnp.max(jnp.where(hits, logits, NEGATIVE), axis=0, keepdims=True)
    terms = jnp.where(hits, jnp.exp(jnp.where(hits, logits - peak, 0.0)), 0.0)
    gates = terms / jnp.sum(terms, axis=0, keepdims=True)
    gates_ref[...] = gates
    here, of_expert = slot_tables(slot_row, base_ref[0], half)
    one_hot = here.astype(LOW)
    picked = dot(one_hot, h_two).astype(LOW).reshape(experts, half, blocks * LANES)
    high, low = split_low(gates)
    by_expert = contract_cols(one_hot, high) + contract_cols(one_hot, low)
    gate_col = jnp.sum(jnp.where(of_expert, by_expert, 0.0), axis=1, keepdims=True)
    on_lane = iota((count, LANES), 1) == (iota((count, LANES), 0) & (half - 1))
    high_rows, low_rows = [
        contract_rows(of_expert.astype(LOW), jnp.where(on_lane, part.astype(FULL), 0.0).astype(LOW))
        for part in split_low(gate_col)
    ]
    sub = iota((EXTRA_ROWS, LANES), 0)
    for block in range(blocks):
        send_ref[:, block * half : (block + 1) * half, :] = picked[
            :, :, block * LANES : (block + 1) * LANES
        ]
    for expert in range(experts):
        send_ref[expert, blocks * half :, :] = jnp.where(
            sub == 0,
            high_rows[expert : expert + 1, :],
            jnp.where(sub == 1, low_rows[expert : expert + 1, :], 0.0),
        ).astype(LOW)


def rows_of(ref, half):
    blocks = (ref.shape[1] - EXTRA_ROWS) // half
    return jnp.concatenate(
        [
            ref[:, at * half : (at + 1) * half, :].reshape(ref.shape[0] * half, LANES)
            for at in range(blocks)
        ],
        axis=1,
    )


def gated_cot(gate, cot_ref):
    sources, half, width = cot_ref.shape
    return (gate * cot_ref[...].reshape(sources * half, width).astype(FULL)).astype(LOW)


def expert_step(half, h_ref, cot_ref, first_ref, second_ref, back_ref, hid_ref, pre_ref, gate_ref):
    sources = h_ref.shape[0]
    blocks = (h_ref.shape[1] - EXTRA_ROWS) // half
    count, shift = sources * half, half.bit_length() - 1
    extra = h_ref[:, blocks * half :, :].reshape(sources * EXTRA_ROWS, LANES)
    source = iota((count, sources * EXTRA_ROWS), 0) >> shift
    row = iota((count, sources * EXTRA_ROWS), 1)
    two_rows = (row == source * EXTRA_ROWS) | (row == source * EXTRA_ROWS + 1)
    on_lane = iota((count, LANES), 1) == (iota((count, LANES), 0) & (half - 1))
    gate_lanes = dot(two_rows.astype(LOW), extra)
    gate = jnp.sum(jnp.where(on_lane, gate_lanes, 0.0), axis=1, keepdims=True)
    gate_ref[...] = jnp.broadcast_to(gate, (count, LANES))
    arrived = gated_cot(gate, cot_ref)
    incoming = rows_of(h_ref, half)
    pre = dot(incoming, first_ref[...])
    grad_hidden = contract_cols(arrived, second_ref[...])
    square = pre * pre
    bend = jnp.tanh(GELU_SCALE * pre * (1.0 + GELU_CUBE * square))
    rise = 0.5 * (1.0 + bend)
    hidden = (pre * rise).astype(LOW)
    hid_ref[...] = hidden
    slope = rise + (0.5 * GELU_SCALE) * pre * (1.0 - bend * bend) * (1.0 + 3.0 * GELU_CUBE * square)
    gated = jnp.sum(hidden.astype(FULL) * grad_hidden, axis=1, keepdims=True)
    grad_pre = (grad_hidden * slope).astype(LOW)
    pre_ref[...] = grad_pre
    grad_rows = contract_cols(grad_pre, first_ref[...]).astype(LOW).reshape(sources, half, blocks * LANES)
    for block in range(blocks):
        back_ref[:, block * half : (block + 1) * half, :] = grad_rows[
            :, :, block * LANES : (block + 1) * LANES
        ]
    source = iota((sources * EXTRA_ROWS, count), 1) >> shift
    row = iota((sources * EXTRA_ROWS, count), 0)
    high, low = [
        jnp.where(on_lane, part.astype(FULL), 0.0).astype(LOW) for part in split_low(gated)
    ]
    rows_back = dot((row == source * EXTRA_ROWS).astype(LOW), high) + dot(
        (row == source * EXTRA_ROWS + 1).astype(LOW), low
    )
    back_ref[:, blocks * half :, :] = rows_back.astype(LOW).reshape(sources, EXTRA_ROWS, LANES)


def part_specs(sources, steps, shapes):
    maps = (lambda i: (jnp.minimum(i, steps - 1), 0, 0), lambda i: (jnp.maximum(i - steps, 0), 0, 0))
    return [pl.BlockSpec((sources, *shape), place) for shape in shapes for place in maps]


def in_halves(steps, first, second):
    pl.when(pl.program_id(0) < steps)(first)
    pl.when(pl.program_id(0) >= steps)(second)


def whole(array):
    rank = len(array.shape)
    return pl.BlockSpec(array.shape, lambda i: (0,) * rank, pipeline_mode=pl.Buffered(1))


def expert_rows(h_rows, cot_rows, first_weight, second_weight, half):
    experts, rows_sent, _ = h_rows[0].shape
    width, hidden_width = first_weight.shape
    sources = min(experts, 256 // half)
    count, steps = sources * half, experts // sources
    total = 2 * experts * half

    def kernel(h_a, h_b, cot_a, cot_b, first_ref, second_ref, back_a, back_b, *kept):
        in_halves(
            steps,
            lambda: expert_step(half, h_a, cot_a, first_ref, second_ref, back_a, *kept),
            lambda: expert_step(half, h_b, cot_b, first_ref, second_ref, back_b, *kept),
        )

    lanes = ((hidden_width, LOW), (hidden_width, LOW), (LANES, FULL))
    back_a, back_b, *kept = pl.pallas_call(
        kernel,
        grid=(2 * steps,),
        out_shape=[near_shape(h_rows[0].shape, LOW)] * 2
        + [far_shape((total, n), kind) for n, kind in lanes],
        in_specs=part_specs(sources, steps, [(rows_sent, LANES), (half, width)])
        + [whole(first_weight), whole(second_weight)],
        out_specs=part_specs(sources, steps, [(rows_sent, LANES)])
        + [pl.BlockSpec((count, n), lambda i: (i, 0)) for n, _ in lanes],
        compiler_params=pltpu.CompilerParams(vmem_limit_bytes=16 * MIB),
        cost_estimate=pl.CostEstimate(
            flops=6 * total * width * hidden_width,
            bytes_accessed=12 * total * width,
            transcendentals=total * hidden_width,
        ),
    )(*h_rows, *cot_rows, far(first_weight), far(second_weight))
    return back_a, back_b, kept


def expert_weights(h_rows, cot_rows, kept, second_weight, sums, half):
    experts, rows_sent, _ = h_rows[0].shape
    hidden_width, width = second_weight.shape
    sources = min(experts, 256 // half)
    count, steps = sources * half, experts // sources
    total = 2 * experts * half

    def kernel(h_a, h_b, cot_a, cot_b, hid_ref, pre_ref, gate_ref, second_ref, *refs):
        out_a, out_b, grad_first, grad_second = refs[-4:]

        @pl.when(pl.program_id(0) == 0)
        def _():
            for at, grad in enumerate((grad_first, grad_second)):
                grad[...] = refs[at][...] if sums else jnp.zeros(grad.shape, FULL)

        def step(h_ref, cot_ref, out_ref):
            hidden, gate = hid_ref[...], gate_ref[:, 0:1]
            produced = dot(hidden, second_ref[...])
            out_ref[...] = (gate * produced).astype(LOW).reshape(out_ref.shape)
            grad_first[...] += contract_rows(rows_of(h_ref, half), pre_ref[...])
            grad_second[...] += contract_rows(hidden, gated_cot(gate, cot_ref))

        in_halves(steps, lambda: step(h_a, cot_a, out_a), lambda: step(h_b, cot_b, out_b))

    grads = [far_shape((width, hidden_width), FULL), far_shape((hidden_width, width), FULL)]
    return pl.pallas_call(
        kernel,
        grid=(2 * steps,),
        out_shape=[near_shape((experts, half, width), LOW)] * 2 + grads,
        in_specs=part_specs(sources, steps, [(rows_sent, LANES), (half, width)])
        + [pl.BlockSpec((count, x.shape[1]), lambda i: (i, 0)) for x in kept]
        + [whole(x) for x in (second_weight, *sums)],
        out_specs=part_specs(sources, steps, [(half, width)]) + [whole(x) for x in grads],
        compiler_params=pltpu.CompilerParams(vmem_limit_bytes=24 * MIB),
        cost_estimate=pl.CostEstimate(
            flops=6 * total * width * hidden_width,
            bytes_accessed=10 * total * width,
            transcendentals=0,
        ),
    )(*h_rows, *cot_rows, *map(far, (*kept, second_weight, *sums)))


def combine_kernel(base_ref, back_ref, slot_ref, col_ref, gates_ref, ext_ref, h_ref, part_ref, router_ref):
    experts, rows_sent, _ = back_ref.shape
    blocks = h_ref.shape[1] // LANES
    half = (rows_sent - EXTRA_ROWS) // blocks
    count = experts * half
    slot_row = slot_ref[...]
    hits = slot_row >= 0
    here, of_expert = slot_tables(slot_row, base_ref[0], half)
    extra = back_ref[:, blocks * half :, :].reshape(experts * EXTRA_ROWS, LANES)
    reach = EXTRA_ROWS
    shift, reach_shift = half.bit_length() - 1, reach.bit_length() - 1
    row = iota((count, experts * reach), 1)
    wanted = (row >> reach_shift) == (iota((count, experts * reach), 0) >> shift)
    wanted = wanted & ((row & (EXTRA_ROWS - 1)) < 2)
    on_lane = iota((count, LANES), 1) == (iota((count, LANES), 0) & (half - 1))
    lanes = dot(wanted.astype(LOW), extra)
    slot_gated = jnp.sum(jnp.where(on_lane, lanes, 0.0), axis=1, keepdims=True)
    high, low = split_low(jnp.where(here, slot_gated, 0.0))
    gated = contract_rows(of_expert.astype(LOW), high) + contract_rows(of_expert.astype(LOW), low)
    gated = jnp.where(hits, gated, 0.0)
    logit_grad = gated - gates_ref[...] * jnp.sum(gated, axis=0, keepdims=True)
    logit_grad = jnp.where(hits, logit_grad, 0.0)
    high, low = split_low(logit_grad)
    router_ref[...] = dot(high, h_ref[...]) + dot(low, h_ref[...])
    router_rows = ext_ref[2 : 2 + experts, :].astype(LOW)
    expand = (iota((experts, count), 1) >> shift) == iota((experts, count), 0)
    wanted = (iota((1, count), 1) & (half - 1)) + base_ref[0]
    one_hot = (dot(col_ref[...], expand.astype(LOW)) == wanted.astype(FULL)).astype(LOW)
    for block in range(blocks):
        rows = back_ref[:, block * half : (block + 1) * half, :].reshape(count, LANES)
        at = slice(block * LANES, (block + 1) * LANES)
        part_ref[:, at] = (
            dot(one_hot, rows)
            + contract_rows(high, router_rows[:, at])
            + contract_rows(low, router_rows[:, at])
        )


def backward_kernel(
    part_ref, other_ref, cot_ref, resid_ref, rows_ref, ext_ref, qk_ref, vx_ref, h_ref, qkv_ref, probs_ref,
    mixed_ref, router_ref, qk_out, vx_out, one_ref, rgrad_ref, qkg_ref, vg_ref,
):
    group_rows = rows_ref.shape[0]
    inner = qk_ref.shape[1] // 2
    h_grad = part_ref[...] + other_ref[...]
    residual = resid_ref[...]
    inv_two = inverse_rms(residual)
    normed_two = residual * inv_two
    gain_two_row = 0.5 * jnp.sum(h_grad * normed_two, axis=0, keepdims=True)
    scaled = h_grad * ext_ref[1:2, :]
    resid_grad = cot_ref[...] + inv_two * (
        scaled - normed_two * jnp.mean(scaled * normed_two, axis=1, keepdims=True)
    )
    rgrad_ref[...] = resid_grad
    attn_grad = resid_grad.astype(LOW)
    vx_out[:, inner : 2 * inner] = contract_rows(attn_grad, mixed_ref[...]).astype(LOW)
    mixed_grad = dot(attn_grad, vx_ref[:, inner : 2 * inner]).astype(LOW)
    low_lanes = iota((group_rows, LANES), 1) < HEAD_DIM
    for pair in range(inner // LANES):
        at = pair * LANES
        queries = qkv_ref[:, at : at + LANES]
        key_rows = qkv_ref[:, inner + at : inner + at + LANES]
        value_rows = qkv_ref[:, 2 * inner + at : 2 * inner + at + LANES]
        out_grad = mixed_grad[:, at : at + LANES]
        grads = []
        for sub in range(2):
            own = low_lanes if sub == 0 else ~low_lanes
            probs = probs_ref[2 * pair + sub]
            prob_grad = contract_cols(jnp.where(own, out_grad, jnp.zeros_like(out_grad)), value_rows)
            carry = jnp.sum(prob_grad * probs, axis=1, keepdims=True)
            score_grad = (probs * (prob_grad - carry)).astype(LOW)
            grads.append(
                (
                    dot(score_grad, key_rows),
                    contract_rows(score_grad, queries),
                    contract_rows(probs.astype(LOW), out_grad),
                )
            )
        scale = HEAD_DIM ** (-0.5)
        qkg_ref[:, at : at + LANES] = (jnp.where(low_lanes, grads[0][0], grads[1][0]) * scale).astype(LOW)
        qkg_ref[:, inner + at : inner + at + LANES] = (
            jnp.where(low_lanes, grads[0][1], grads[1][1]) * scale
        ).astype(LOW)
        vg_ref[:, at : at + LANES] = jnp.where(low_lanes, grads[0][2], grads[1][2]).astype(LOW)
    h_one = h_ref[...]
    qk_out[...] = contract_rows(h_one, qkg_ref[...]).astype(LOW)
    vx_out[:, :inner] = contract_rows(h_one, vg_ref[...]).astype(LOW)
    one_grad = contract_cols(qkg_ref[...], qk_ref[...]) + contract_cols(vg_ref[...], vx_ref[:, :inner])
    one_ref[...] = one_grad
    rows = rows_ref[...]
    gain_one_row = jnp.sum(one_grad * (rows * inverse_rms(rows)), axis=0, keepdims=True)
    router_rows = router_ref[...]
    sub = iota(router_rows.shape, 0)
    extra = jnp.where(sub == 0, gain_one_row, jnp.where(sub == 1, gain_two_row, router_rows))
    vx_out[:, 2 * inner :] = extra.T.astype(LOW)


def local(
    block_in,
    seq_lengths,
    routes,
    w_query,
    w_key,
    w_value,
    w_out_proj,
    router,
    gain_attn,
    gain_moe,
    expert_in,
    expert_out,
    cotangent,
):
    dp_count = lax.axis_size("dp")
    core = lax.axis_index("tensor")
    tok_rows, width = block_in.shape
    group_rows, top_count = routes.shape
    experts = router.shape[1]
    half = max(EXTRA_ROWS, top_count * group_rows // experts)
    slots = experts * half
    rows_sent = half * (width // LANES) + EXTRA_ROWS
    inner = w_query.shape[1]
    bits = dp_count.bit_length() - 1
    order_a, order_b = bit_orders()

    expert_ids = jnp.arange(experts, dtype=jnp.int32)
    hits = jnp.any(routes[:, :, None] == expert_ids[None, None, :], axis=1)
    places = jnp.arange(group_rows, dtype=jnp.int32)
    earlier = (places[:, None] > places[None, :]).astype(LOW)
    slot_col = jnp.where(hits, dot(earlier, hits.astype(LOW)), -1.0).astype(LOW)
    slot_row = slot_col.T
    base = core * half
    slot_ids = (base + jnp.arange(half, dtype=jnp.int32)).astype(LOW)
    in_slot = slot_row[:, None, :] == slot_ids[None, :, None]
    dispatch = in_slot.astype(LOW).reshape(slots, group_rows)
    base = base.reshape(1).astype(jnp.int32)
    cot_picked = dot(dispatch, cotangent.astype(LOW)).astype(LOW).reshape(experts, half, width)

    extra_width = -(-(2 + experts) // LANES) * LANES
    qk_full = jnp.concatenate([w_query, w_key], axis=1)
    router, gain_attn, gain_moe = lax.optimization_barrier((router, gain_attn, gain_moe, qk_full))[:3]
    extra = jnp.concatenate(
        [
            gain_attn[:, None],
            gain_moe[:, None],
            router,
            jnp.zeros((router.shape[0], extra_width - 2 - experts), LOW),
        ],
        axis=1,
    )
    vx_full = jnp.concatenate([w_value, w_out_proj.T, extra], axis=1)
    qk_full = qk_full.reshape((1,) * bits + qk_full.shape)
    vx_full = vx_full.reshape((1,) * bits + vx_full.shape)
    for step in range(bits):
        vx_full = double(vx_full, order_b[step], bits)
        qk_full = double(qk_full, order_a[step], bits)
        if step == bits - 2:
            rows_all = lax.all_gather(after(block_in, vx_full), "tensor", axis=0, tiled=True)
    cot_own = trade(after(cot_picked, rows_all))
    qk_full = qk_full.reshape(width, 2 * inner)
    vx_full = vx_full.reshape(width, 2 * inner + extra_width)

    attn_part, ext, h_one, qkv, probs, mixed, rows_far, qk_far, vx_far = call(
        attention_kernel,
        [
            near_shape((group_rows, width), FULL),
            near_shape((extra_width, width), FULL),
            far_shape((group_rows, width), LOW),
            far_shape((group_rows, 3 * inner), LOW),
            far_shape((inner // HEAD_DIM, group_rows, group_rows), FULL),
            far_shape((group_rows, inner), LOW),
            far_shape(rows_all.shape, FULL),
            far_shape(qk_full.shape, LOW),
            far_shape(vx_full.shape, LOW),
        ],
        seq_lengths,
        rows_all,
        qk_full,
        vx_full,
        limit=14,
        flops=8 * group_rows * width * inner + 4 * group_rows * group_rows * inner,
        smem=(0,),
    )
    residual, h_two, gates, sent = call(
        dispatch_kernel,
        [
            far_shape((group_rows, width), FULL),
            far_shape((group_rows, width), LOW),
            near_shape((experts, group_rows), FULL),
            near_shape((experts, rows_sent, LANES), LOW),
        ],
        base,
        rows_all,
        attn_part,
        swap(attn_part),
        ext,
        slot_row,
        flops=2 * experts * half * group_rows * width,
        smem=(0,),
    )

    cot_crossed = cross(cot_own)
    cot_own = (cot_own, swap(cot_own))
    cot_far = (cot_crossed, swap(cot_crossed))
    h_own = trade(sent)
    h_crossed = cross(after(h_own, cot_crossed))
    h_own = (after(h_own, cot_far[1]), swap(h_own))
    first_weight = expert_in[0]
    second_weight = expert_out[0]
    own_back, own_given, own_kept = expert_rows(h_own, cot_own, first_weight, second_weight, half)
    h_crossed = after(h_crossed, own_back)
    h_far = (h_crossed, swap(h_crossed))
    far_back, far_given, far_kept = expert_rows(h_far, cot_far, first_weight, second_weight, half)
    far_sum = add_low(far_back, swap(far_given))
    far_total = cross(far_sum)
    back = trade(add_low(own_back, swap(own_given), far_total))

    far_kept[0] = after(far_kept[0], far_sum)
    far_out, far_given, *sums = expert_weights(h_far, cot_far, far_kept, second_weight, (), half)
    own_out, own_given, grad_first, grad_second = expert_weights(
        h_own, cot_own, own_kept, second_weight, sums, half
    )
    far_total = cross(after(add_low(far_out, swap(far_given)), far_total))
    out_rows = add_low(own_out, swap(own_given), far_total)
    h_part, router_part = call(
        combine_kernel,
        [near_shape((group_rows, width), FULL), near_shape((experts, width), FULL)],
        base,
        after(back, own_out),
        slot_row,
        slot_col,
        gates,
        ext,
        far(h_two),
        flops=2 * slots * group_rows * width,
        smem=(0,),
    )
    router_part = jnp.pad(router_part, ((2, extra_width - 2 - experts), (0, 0)))
    qk_part, vx_part, one_part, resid_grad, _, _ = call(
        backward_kernel,
        [
            near_shape((width, 2 * inner), LOW),
            near_shape((width, 2 * inner + extra_width), LOW),
            near_shape((group_rows, width), FULL),
            near_shape((group_rows, width), FULL),
            near_shape((group_rows, 2 * inner), LOW),
            near_shape((group_rows, inner), LOW),
        ],
        h_part,
        swap(h_part),
        *map(far, (cotangent, residual, rows_far)),
        ext,
        *map(far, (qk_far, vx_far, h_one, qkv, probs, mixed)),
        router_part,
        limit=14,
        flops=20 * group_rows * width * inner + 12 * group_rows * group_rows * inner,
    )

    own_start = core * tok_rows
    other_start = (1 - core) * tok_rows

    def rows_at(values, start):
        return lax.dynamic_slice_in_dim(values, start, tok_rows, 0)

    one_other = swap(rows_at(one_part, other_start).astype(LOW)).astype(FULL)
    qk_sum = qk_part.reshape((2,) * bits + (width // dp_count, 2 * inner))
    vx_sum = vx_part.reshape((2,) * bits + (width // dp_count, 2 * inner + extra_width))
    for step in range(bits):
        vx_sum = halve(vx_sum, order_b[bits - 1 - step], bits)
        qk_sum = halve(qk_sum, order_a[bits - 1 - step], bits)
        if step == 0:
            back_out = trade(after(out_rows, qk_sum)).reshape(slots, width)
    qk_sum = qk_sum.reshape(width // dp_count, 2 * inner)
    vx_sum = vx_sum.reshape(width // dp_count, 2 * inner + extra_width)

    out_part = contract_rows(dispatch, back_out)
    block_out = rows_at(residual, own_start) + (
        rows_at(out_part, own_start) + swap(rows_at(out_part, other_start))
    )
    scaled_one = (rows_at(one_part, own_start) + one_other) * ext[0:1, :]
    inv_own = inverse_rms(block_in)
    normed_own = block_in * inv_own
    grad_in = rows_at(resid_grad, own_start) + inv_own * (
        scaled_one - normed_own * jnp.mean(scaled_one * normed_own, axis=1, keepdims=True)
    )
    extra_sum = vx_sum[:, 2 * inner :]
    extra_sum = extra_sum + swap(extra_sum)
    share = extra_sum.shape[0] // 2
    extra_own = lax.dynamic_slice_in_dim(extra_sum, core * share, share, 0)
    return (
        block_out,
        grad_in,
        qk_sum[:, :inner],
        qk_sum[:, inner:],
        vx_sum[:, :inner],
        vx_sum[:, inner : 2 * inner].T,
        extra_own[:, 2 : 2 + experts],
        extra_own[:, 0],
        extra_own[:, 1],
        grad_first[None],
        grad_second[None],
    )


def solution(mesh):
    in_specs = (
        P(("dp", "tensor"), None),
        P("dp", None),
        P("dp", None),
        P("dp", "tensor"),
        P("dp", "tensor"),
        P("dp", "tensor"),
        P("tensor", "dp"),
        P("dp", None),
        P("dp"),
        P("dp"),
        P("dp", None, "tensor"),
        P("dp", "tensor", None),
        P("dp", None),
    )
    out_specs = (
        P(("dp", "tensor"), None),
        P(("dp", "tensor"), None),
        P("dp", "tensor"),
        P("dp", "tensor"),
        P("dp", "tensor"),
        P("tensor", "dp"),
        P(("dp", "tensor"), None),
        P(("dp", "tensor")),
        P(("dp", "tensor")),
        P("dp", None, "tensor"),
        P("dp", "tensor", None),
    )
    return jax.shard_map(local, mesh=mesh, in_specs=in_specs, out_specs=out_specs, check_vma=False)
```

```python
import math

import jax
import jax.numpy as jnp
from jax import lax
from jax.experimental import pallas as pl
from jax.experimental.pallas import tpu as pltpu
from jax.sharding import PartitionSpec as P

HEAD_DIM = 64
LANES = 128


EPSILON = 1e-06
NEGATIVE = -1e30
MIB = 1024 * 1024
EXTRA_ROWS = 16
LOW = jnp.bfloat16
FULL = jnp.float32


def dot(left_side, right_side):
    return jnp.dot(left_side, right_side, preferred_element_type=FULL)


def contract_rows(left_side, right_side):
    return lax.dot_general(
        left_side, right_side, (((0,), (0,)), ((), ())), preferred_element_type=FULL
    )


def contract_cols(left_side, right_side):
    return lax.dot_general(
        left_side, right_side, (((1,), (1,)), ((), ())), preferred_element_type=FULL
    )


def split_low(values):
    high = values.astype(LOW)
    return high, (values - high.astype(FULL)).astype(LOW)


def iota(shape, axis):
    return lax.broadcasted_iota(jnp.int32, shape, axis)


def swap(values):
    return lax.ppermute(values, "tensor", [(0, 1), (1, 0)])


def bit_orders():
    bits = lax.axis_size("dp").bit_length() - 1
    falling = list(range(bits - 1, -1, -1))
    return falling, falling[:-2] + [falling[-1], falling[-2]]


def partners(bit):
    return [(i, i ^ (1 << bit)) for i in range(lax.axis_size("dp"))]


def double(block, bit, bits):
    other = lax.ppermute(block, "dp", partners(bit))
    axis = bits - 1 - bit
    upper = ((lax.axis_index("dp") >> bit) & 1) == 1
    return jnp.where(
        upper,
        jnp.concatenate([other, block], axis=axis),
        jnp.concatenate([block, other], axis=axis),
    )


def halve(block, bit, bits):
    axis, place = bits - 1 - bit, (lax.axis_index("dp") >> bit) & 1
    given = lax.dynamic_index_in_dim(block, 1 - place, axis, keepdims=True).astype(LOW)
    kept = lax.dynamic_index_in_dim(block, place, axis, keepdims=True)
    return kept.astype(FULL) + lax.ppermute(given, "dp", partners(bit)).astype(FULL)


def trade(values):
    experts, dp_count = values.shape[0], lax.axis_size("dp")
    owners = dp_count // experts
    groups = [[owners * e + o for e in range(experts)] for o in range(owners)]
    return lax.all_to_all(
        values, "dp", split_axis=0, concat_axis=0, tiled=True, axis_index_groups=groups
    )


def cross(values):
    return lax.ppermute(values, "dp", partners(0))


def after(values, *others):
    return lax.optimization_barrier((values, *others))[0]


def add_low(*parts):
    return sum(part.astype(FULL) for part in parts).astype(LOW)


def far(values):
    return pltpu.with_memory_space_constraint(values, pltpu.HBM)


def near_shape(shape, kind):
    return jax.ShapeDtypeStruct(shape, kind)


def far_shape(shape, kind):
    return pltpu.HBM(shape, kind)


def call(kernel, out_shape, *operands, flops=0, smem=(), limit=8):
    moved = sum(x.size * x.dtype.itemsize for x in operands)
    return pl.pallas_call(
        kernel,
        out_shape=out_shape,
        in_specs=[
            pl.BlockSpec(memory_space=pltpu.SMEM if i in smem else pltpu.VMEM)
            for i in range(len(operands))
        ],
        out_specs=[pl.BlockSpec(memory_space=pltpu.VMEM) for _ in out_shape],
        compiler_params=pltpu.CompilerParams(vmem_limit_bytes=limit * MIB),
        cost_estimate=pl.CostEstimate(flops=flops, bytes_accessed=2 * moved, transcendentals=0),
    )(*operands)


def inverse_rms(rows):
    return lax.rsqrt(jnp.mean(rows * rows, axis=1, keepdims=True) + EPSILON)


GELU_SCALE = math.sqrt(2.0 / math.pi)
GELU_CUBE = 0.044715


def attention_kernel(
    len_ref, rows_ref, qk_ref, vx_ref, attn_ref, ext_ref, h_ref, qkv_ref, probs_ref, mixed_ref, rows_out, qk_out, vx_out
):
    group_rows = rows_ref.shape[0]
    inner = qk_ref.shape[1] // 2
    rows = rows_ref[...]
    rows_out[...] = rows
    qk_out[...] = qk_ref[...]
    vx_out[...] = vx_ref[...]
    ext = vx_ref[:, 2 * inner :].astype(FULL).T
    ext_ref[...] = ext
    h_one = (rows * inverse_rms(rows) * ext[0:1, :]).astype(LOW)
    h_ref[...] = h_one
    qkv_ref[:, : 2 * inner] = dot(h_one, qk_ref[...]).astype(LOW)
    qkv_ref[:, 2 * inner :] = dot(h_one, vx_ref[:, :inner]).astype(LOW)
    down, across = iota((group_rows, group_rows), 0), iota((group_rows, group_rows), 1)
    allowed = down >= across
    end = jnp.int32(0)
    for place in range(len_ref.shape[1]):
        end = end + len_ref[0, place]
        allowed = allowed & ((down >= end) == (across >= end))
    low_lanes = iota((group_rows, LANES), 1) < HEAD_DIM
    for pair in range(inner // LANES):
        at = pair * LANES
        queries = qkv_ref[:, at : at + LANES]
        key_rows = qkv_ref[:, inner + at : inner + at + LANES]
        value_rows = qkv_ref[:, 2 * inner + at : 2 * inner + at + LANES]
        outs = []
        for sub in range(2):
            own = low_lanes if sub == 0 else ~low_lanes
            scores = contract_cols(jnp.where(own, queries, jnp.zeros_like(queries)), key_rows)
            scores = jnp.where(allowed, scores * HEAD_DIM ** (-0.5), NEGATIVE)
            terms = jnp.exp(scores - jnp.max(scores, axis=1, keepdims=True))
            probs = terms / jnp.sum(terms, axis=1, keepdims=True)
            probs_ref[2 * pair + sub] = probs
            outs.append(dot(probs.astype(LOW), value_rows))
        mixed_ref[:, at : at + LANES] = jnp.where(low_lanes, outs[0], outs[1]).astype(LOW)
    attn_ref[...] = contract_cols(mixed_ref[...], vx_ref[:, inner : 2 * inner])


def slot_tables(slot_row, base, half):
    experts, group_rows = slot_row.shape
    count, shift = experts * half, half.bit_length() - 1
    of_expert = (iota((count, experts), 0) >> shift) == iota((count, experts), 1)
    wanted = (iota((count, 1), 0) & (half - 1)) + base
    here = dot(of_expert.astype(LOW), slot_row) == wanted.astype(FULL)
    return here, of_expert


def dispatch_kernel(
    base_ref, rows_ref, attn_ref, other_ref, ext_ref, slot_ref, resid_ref, h_ref, gates_ref, send_ref
):
    experts, rows_sent, _ = send_ref.shape
    blocks = rows_ref.shape[1] // LANES
    half = (rows_sent - EXTRA_ROWS) // blocks
    count = experts * half
    residual = rows_ref[...] + (attn_ref[...] + other_ref[...])
    resid_ref[...] = residual
    h_two = (residual * inverse_rms(residual) * ext_ref[1:2, :]).astype(LOW)
    h_ref[...] = h_two
    slot_row = slot_ref[...]
    hits = slot_row >= 0
    all_logits = contract_cols(ext_ref[...].astype(LOW), h_two)
    logits = all_logits[2 : 2 + experts, :]
    peak = jnp.max(jnp.where(hits, logits, NEGATIVE), axis=0, keepdims=True)
    terms = jnp.where(hits, jnp.exp(jnp.where(hits, logits - peak, 0.0)), 0.0)
    gates = terms / jnp.sum(terms, axis=0, keepdims=True)
    gates_ref[...] = gates
    here, of_expert = slot_tables(slot_row, base_ref[0], half)
    one_hot = here.astype(LOW)
    picked = dot(one_hot, h_two).astype(LOW).reshape(experts, half, blocks * LANES)
    high, low = split_low(gates)
    by_expert = contract_cols(one_hot, high) + contract_cols(one_hot, low)
    gate_col = jnp.sum(jnp.where(of_expert, by_expert, 0.0), axis=1, keepdims=True)
    on_lane = iota((count, LANES), 1) == (iota((count, LANES), 0) & (half - 1))
    high_rows, low_rows = [
        contract_rows(of_expert.astype(LOW), jnp.where(on_lane, part.astype(FULL), 0.0).astype(LOW))
        for part in split_low(gate_col)
    ]
    sub = iota((EXTRA_ROWS, LANES), 0)
    for block in range(blocks):
        send_ref[:, block * half : (block + 1) * half, :] = picked[
            :, :, block * LANES : (block + 1) * LANES
        ]
    for expert in range(experts):
        send_ref[expert, blocks * half :, :] = jnp.where(
            sub == 0,
            high_rows[expert : expert + 1, :],
            jnp.where(sub == 1, low_rows[expert : expert + 1, :], 0.0),
        ).astype(LOW)


def rows_of(ref, half):
    blocks = (ref.shape[1] - EXTRA_ROWS) // half
    return jnp.concatenate(
        [
            ref[:, at * half : (at + 1) * half, :].reshape(ref.shape[0] * half, LANES)
            for at in range(blocks)
        ],
        axis=1,
    )


def gated_cot(gate, cot_ref):
    sources, half, width = cot_ref.shape
    return (gate * cot_ref[...].reshape(sources * half, width).astype(FULL)).astype(LOW)


def expert_step(half, h_ref, cot_ref, first_ref, second_ref, back_ref, hid_ref, pre_ref, gate_ref):
    sources = h_ref.shape[0]
    blocks = (h_ref.shape[1] - EXTRA_ROWS) // half
    count, shift = sources * half, half.bit_length() - 1
    extra = h_ref[:, blocks * half :, :].reshape(sources * EXTRA_ROWS, LANES)
    source = iota((count, sources * EXTRA_ROWS), 0) >> shift
    row = iota((count, sources * EXTRA_ROWS), 1)
    two_rows = (row == source * EXTRA_ROWS) | (row == source * EXTRA_ROWS + 1)
    on_lane = iota((count, LANES), 1) == (iota((count, LANES), 0) & (half - 1))
    gate_lanes = dot(two_rows.astype(LOW), extra)
    gate = jnp.sum(jnp.where(on_lane, gate_lanes, 0.0), axis=1, keepdims=True)
    gate_ref[...] = jnp.broadcast_to(gate, (count, LANES))
    arrived = gated_cot(gate, cot_ref)
    incoming = rows_of(h_ref, half)
    pre = dot(incoming, first_ref[...])
    grad_hidden = contract_cols(arrived, second_ref[...])
    square = pre * pre
    bend = jnp.tanh(GELU_SCALE * pre * (1.0 + GELU_CUBE * square))
    rise = 0.5 * (1.0 + bend)
    hidden = (pre * rise).astype(LOW)
    hid_ref[...] = hidden
    slope = rise + (0.5 * GELU_SCALE) * pre * (1.0 - bend * bend) * (1.0 + 3.0 * GELU_CUBE * square)
    gated = jnp.sum(hidden.astype(FULL) * grad_hidden, axis=1, keepdims=True)
    grad_pre = (grad_hidden * slope).astype(LOW)
    pre_ref[...] = grad_pre
    grad_rows = contract_cols(grad_pre, first_ref[...]).astype(LOW).reshape(sources, half, blocks * LANES)
    for block in range(blocks):
        back_ref[:, block * half : (block + 1) * half, :] = grad_rows[
            :, :, block * LANES : (block + 1) * LANES
        ]
    source = iota((sources * EXTRA_ROWS, count), 1) >> shift
    row = iota((sources * EXTRA_ROWS, count), 0)
    high, low = [
        jnp.where(on_lane, part.astype(FULL), 0.0).astype(LOW) for part in split_low(gated)
    ]
    rows_back = dot((row == source * EXTRA_ROWS).astype(LOW), high) + dot(
        (row == source * EXTRA_ROWS + 1).astype(LOW), low
    )
    back_ref[:, blocks * half :, :] = rows_back.astype(LOW).reshape(sources, EXTRA_ROWS, LANES)


def part_specs(sources, steps, shapes):
    maps = (lambda i: (jnp.minimum(i, steps - 1), 0, 0), lambda i: (jnp.maximum(i - steps, 0), 0, 0))
    return [pl.BlockSpec((sources, *shape), place) for shape in shapes for place in maps]


def in_halves(steps, first, second):
    pl.when(pl.program_id(0) < steps)(first)
    pl.when(pl.program_id(0) >= steps)(second)


def whole(array):
    rank = len(array.shape)
    return pl.BlockSpec(array.shape, lambda i: (0,) * rank, pipeline_mode=pl.Buffered(1))


def expert_rows(h_rows, cot_rows, first_weight, second_weight, half):
    experts, rows_sent, _ = h_rows[0].shape
    width, hidden_width = first_weight.shape
    sources = min(experts, 256 // half)
    count, steps = sources * half, experts // sources
    total = 2 * experts * half

    def kernel(h_a, h_b, cot_a, cot_b, first_ref, second_ref, back_a, back_b, *kept):
        in_halves(
            steps,
            lambda: expert_step(half, h_a, cot_a, first_ref, second_ref, back_a, *kept),
            lambda: expert_step(half, h_b, cot_b, first_ref, second_ref, back_b, *kept),
        )

    lanes = ((hidden_width, LOW), (hidden_width, LOW), (LANES, FULL))
    back_a, back_b, *kept = pl.pallas_call(
        kernel,
        grid=(2 * steps,),
        out_shape=[near_shape(h_rows[0].shape, LOW)] * 2
        + [far_shape((total, n), kind) for n, kind in lanes],
        in_specs=part_specs(sources, steps, [(rows_sent, LANES), (half, width)])
        + [whole(first_weight), whole(second_weight)],
        out_specs=part_specs(sources, steps, [(rows_sent, LANES)])
        + [pl.BlockSpec((count, n), lambda i: (i, 0)) for n, _ in lanes],
        compiler_params=pltpu.CompilerParams(vmem_limit_bytes=16 * MIB),
        cost_estimate=pl.CostEstimate(
            flops=6 * total * width * hidden_width,
            bytes_accessed=12 * total * width,
            transcendentals=total * hidden_width,
        ),
    )(*h_rows, *cot_rows, far(first_weight), far(second_weight))
    return back_a, back_b, kept


def expert_weights(h_rows, cot_rows, kept, second_weight, sums, half):
    experts, rows_sent, _ = h_rows[0].shape
    hidden_width, width = second_weight.shape
    sources = min(experts, 256 // half)
    count, steps = sources * half, experts // sources
    total = 2 * experts * half

    def kernel(h_a, h_b, cot_a, cot_b, hid_ref, pre_ref, gate_ref, second_ref, *refs):
        out_a, out_b, grad_first, grad_second = refs[-4:]

        @pl.when(pl.program_id(0) == 0)
        def _():
            for at, grad in enumerate((grad_first, grad_second)):
                grad[...] = refs[at][...] if sums else jnp.zeros(grad.shape, FULL)

        def step(h_ref, cot_ref, out_ref):
            hidden, gate = hid_ref[...], gate_ref[:, 0:1]
            produced = dot(hidden, second_ref[...])
            out_ref[...] = (gate * produced).astype(LOW).reshape(out_ref.shape)
            grad_first[...] += contract_rows(rows_of(h_ref, half), pre_ref[...])
            grad_second[...] += contract_rows(hidden, gated_cot(gate, cot_ref))

        in_halves(steps, lambda: step(h_a, cot_a, out_a), lambda: step(h_b, cot_b, out_b))

    grads = [far_shape((width, hidden_width), FULL), far_shape((hidden_width, width), FULL)]
    return pl.pallas_call(
        kernel,
        grid=(2 * steps,),
        out_shape=[near_shape((experts, half, width), LOW)] * 2 + grads,
        in_specs=part_specs(sources, steps, [(rows_sent, LANES), (half, width)])
        + [pl.BlockSpec((count, x.shape[1]), lambda i: (i, 0)) for x in kept]
        + [whole(x) for x in (second_weight, *sums)],
        out_specs=part_specs(sources, steps, [(half, width)]) + [whole(x) for x in grads],
        compiler_params=pltpu.CompilerParams(vmem_limit_bytes=24 * MIB),
        cost_estimate=pl.CostEstimate(
            flops=6 * total * width * hidden_width,
            bytes_accessed=10 * total * width,
            transcendentals=0,
        ),
    )(*h_rows, *cot_rows, *map(far, (*kept, second_weight, *sums)))


def combine_kernel(base_ref, back_ref, slot_ref, col_ref, gates_ref, ext_ref, h_ref, part_ref, router_ref):
    experts, rows_sent, _ = back_ref.shape
    blocks = h_ref.shape[1] // LANES
    half = (rows_sent - EXTRA_ROWS) // blocks
    count = experts * half
    slot_row = slot_ref[...]
    hits = slot_row >= 0
    here, of_expert = slot_tables(slot_row, base_ref[0], half)
    extra = back_ref[:, blocks * half :, :].reshape(experts * EXTRA_ROWS, LANES)
    reach = EXTRA_ROWS
    shift, reach_shift = half.bit_length() - 1, reach.bit_length() - 1
    row = iota((count, experts * reach), 1)
    wanted = (row >> reach_shift) == (iota((count, experts * reach), 0) >> shift)
    wanted = wanted & ((row & (EXTRA_ROWS - 1)) < 2)
    on_lane = iota((count, LANES), 1) == (iota((count, LANES), 0) & (half - 1))
    lanes = dot(wanted.astype(LOW), extra)
    slot_gated = jnp.sum(jnp.where(on_lane, lanes, 0.0), axis=1, keepdims=True)
    high, low = split_low(jnp.where(here, slot_gated, 0.0))
    gated = contract_rows(of_expert.astype(LOW), high) + contract_rows(of_expert.astype(LOW), low)
    gated = jnp.where(hits, gated, 0.0)
    logit_grad = gated - gates_ref[...] * jnp.sum(gated, axis=0, keepdims=True)
    logit_grad = jnp.where(hits, logit_grad, 0.0)
    high, low = split_low(logit_grad)
    router_ref[...] = dot(high, h_ref[...]) + dot(low, h_ref[...])
    router_rows = ext_ref[2 : 2 + experts, :].astype(LOW)
    expand = (iota((experts, count), 1) >> shift) == iota((experts, count), 0)
    wanted = (iota((1, count), 1) & (half - 1)) + base_ref[0]
    one_hot = (dot(col_ref[...], expand.astype(LOW)) == wanted.astype(FULL)).astype(LOW)
    for block in range(blocks):
        rows = back_ref[:, block * half : (block + 1) * half, :].reshape(count, LANES)
        at = slice(block * LANES, (block + 1) * LANES)
        part_ref[:, at] = (
            dot(one_hot, rows)
            + contract_rows(high, router_rows[:, at])
            + contract_rows(low, router_rows[:, at])
        )


def backward_kernel(
    part_ref, other_ref, cot_ref, resid_ref, rows_ref, ext_ref, qk_ref, vx_ref, h_ref, qkv_ref, probs_ref,
    mixed_ref, router_ref, qk_out, vx_out, one_ref, rgrad_ref, qkg_ref, vg_ref,
):
    group_rows = rows_ref.shape[0]
    inner = qk_ref.shape[1] // 2
    h_grad = part_ref[...] + other_ref[...]
    residual = resid_ref[...]
    inv_two = inverse_rms(residual)
    normed_two = residual * inv_two
    gain_two_row = 0.5 * jnp.sum(h_grad * normed_two, axis=0, keepdims=True)
    scaled = h_grad * ext_ref[1:2, :]
    resid_grad = cot_ref[...] + inv_two * (
        scaled - normed_two * jnp.mean(scaled * normed_two, axis=1, keepdims=True)
    )
    rgrad_ref[...] = resid_grad
    attn_grad = resid_grad.astype(LOW)
    vx_out[:, inner : 2 * inner] = contract_rows(attn_grad, mixed_ref[...]).astype(LOW)
    mixed_grad = dot(attn_grad, vx_ref[:, inner : 2 * inner]).astype(LOW)
    low_lanes = iota((group_rows, LANES), 1) < HEAD_DIM
    for pair in range(inner // LANES):
        at = pair * LANES
        queries = qkv_ref[:, at : at + LANES]
        key_rows = qkv_ref[:, inner + at : inner + at + LANES]
        value_rows = qkv_ref[:, 2 * inner + at : 2 * inner + at + LANES]
        out_grad = mixed_grad[:, at : at + LANES]
        grads = []
        for sub in range(2):
            own = low_lanes if sub == 0 else ~low_lanes
            probs = probs_ref[2 * pair + sub]
            prob_grad = contract_cols(jnp.where(own, out_grad, jnp.zeros_like(out_grad)), value_rows)
            carry = jnp.sum(prob_grad * probs, axis=1, keepdims=True)
            score_grad = (probs * (prob_grad - carry)).astype(LOW)
            grads.append(
                (
                    dot(score_grad, key_rows),
                    contract_rows(score_grad, queries),
                    contract_rows(probs.astype(LOW), out_grad),
                )
            )
        scale = HEAD_DIM ** (-0.5)
        qkg_ref[:, at : at + LANES] = (jnp.where(low_lanes, grads[0][0], grads[1][0]) * scale).astype(LOW)
        qkg_ref[:, inner + at : inner + at + LANES] = (
            jnp.where(low_lanes, grads[0][1], grads[1][1]) * scale
        ).astype(LOW)
        vg_ref[:, at : at + LANES] = jnp.where(low_lanes, grads[0][2], grads[1][2]).astype(LOW)
    h_one = h_ref[...]
    qk_out[...] = contract_rows(h_one, qkg_ref[...]).astype(LOW)
    vx_out[:, :inner] = contract_rows(h_one, vg_ref[...]).astype(LOW)
    one_grad = contract_cols(qkg_ref[...], qk_ref[...]) + contract_cols(vg_ref[...], vx_ref[:, :inner])
    one_ref[...] = one_grad
    rows = rows_ref[...]
    gain_one_row = jnp.sum(one_grad * (rows * inverse_rms(rows)), axis=0, keepdims=True)
    router_rows = router_ref[...]
    sub = iota(router_rows.shape, 0)
    extra = jnp.where(sub == 0, gain_one_row, jnp.where(sub == 1, gain_two_row, router_rows))
    vx_out[:, 2 * inner :] = extra.T.astype(LOW)


def local(
    block_in,
    seq_lengths,
    routes,
    w_query,
    w_key,
    w_value,
    w_out_proj,
    router,
    gain_attn,
    gain_moe,
    expert_in,
    expert_out,
    cotangent,
):
    dp_count = lax.axis_size("dp")
    core = lax.axis_index("tensor")
    tok_rows, width = block_in.shape
    group_rows, top_count = routes.shape
    experts = router.shape[1]
    half = max(EXTRA_ROWS, top_count * group_rows // experts)
    slots = experts * half
    rows_sent = half * (width // LANES) + EXTRA_ROWS
    inner = w_query.shape[1]
    bits = dp_count.bit_length() - 1
    order_a, order_b = bit_orders()

    expert_ids = jnp.arange(experts, dtype=jnp.int32)
    hits = jnp.any(routes[:, :, None] == expert_ids[None, None, :], axis=1)
    places = jnp.arange(group_rows, dtype=jnp.int32)
    earlier = (places[:, None] > places[None, :]).astype(LOW)
    slot_col = jnp.where(hits, dot(earlier, hits.astype(LOW)), -1.0).astype(LOW)
    slot_row = slot_col.T
    base = core * half
    slot_ids = (base + jnp.arange(half, dtype=jnp.int32)).astype(LOW)
    in_slot = slot_row[:, None, :] == slot_ids[None, :, None]
    dispatch = in_slot.astype(LOW).reshape(slots, group_rows)
    base = base.reshape(1).astype(jnp.int32)
    cot_picked = dot(dispatch, cotangent.astype(LOW)).astype(LOW).reshape(experts, half, width)

    extra_width = -(-(2 + experts) // LANES) * LANES
    extra = jnp.concatenate(
        [
            gain_attn[:, None],
            gain_moe[:, None],
            router,
            jnp.zeros((router.shape[0], extra_width - 2 - experts), LOW),
        ],
        axis=1,
    )
    shard = jnp.concatenate([w_query, w_key, w_value, w_out_proj.T, extra], axis=1)
    lines = [[low + 4 * high for high in range(dp_count // 4)] for low in range(4)]
    line = lax.all_gather(shard, "dp", axis=0, tiled=True, axis_index_groups=lines)
    line = line.reshape((2,) * (bits - 2) + (1, 1) + shard.shape)
    qk_full, vx_full = line[..., : 2 * inner], line[..., 2 * inner :]
    for step in range(bits - 2, bits):
        vx_full = double(vx_full, order_b[step], bits)
        qk_full = double(qk_full, order_a[step], bits)
        if step == bits - 2:
            rows_all = lax.all_gather(after(block_in, vx_full), "tensor", axis=0, tiled=True)
    cot_own = trade(after(cot_picked, rows_all))
    qk_full = qk_full.reshape(width, 2 * inner)
    vx_full = vx_full.reshape(width, 2 * inner + extra_width)

    attn_part, ext, h_one, qkv, probs, mixed, rows_far, qk_far, vx_far = call(
        attention_kernel,
        [
            near_shape((group_rows, width), FULL),
            near_shape((extra_width, width), FULL),
            far_shape((group_rows, width), LOW),
            far_shape((group_rows, 3 * inner), LOW),
            far_shape((inner // HEAD_DIM, group_rows, group_rows), FULL),
            far_shape((group_rows, inner), LOW),
            far_shape(rows_all.shape, FULL),
            far_shape(qk_full.shape, LOW),
            far_shape(vx_full.shape, LOW),
        ],
        seq_lengths,
        rows_all,
        qk_full,
        vx_full,
        limit=14,
        flops=8 * group_rows * width * inner + 4 * group_rows * group_rows * inner,
        smem=(0,),
    )
    residual, h_two, gates, sent = call(
        dispatch_kernel,
        [
            far_shape((group_rows, width), FULL),
            far_shape((group_rows, width), LOW),
            near_shape((experts, group_rows), FULL),
            near_shape((experts, rows_sent, LANES), LOW),
        ],
        base,
        rows_all,
        attn_part,
        swap(attn_part),
        ext,
        slot_row,
        flops=2 * experts * half * group_rows * width,
        smem=(0,),
    )

    cot_crossed = cross(cot_own)
    cot_own = (cot_own, swap(cot_own))
    cot_far = (cot_crossed, swap(cot_crossed))
    h_own = trade(sent)
    h_crossed = cross(after(h_own, cot_crossed))
    h_own = (after(h_own, cot_far[1]), swap(h_own))
    first_weight = expert_in[0]
    second_weight = expert_out[0]
    own_back, own_given, own_kept = expert_rows(h_own, cot_own, first_weight, second_weight, half)
    h_crossed = after(h_crossed, own_back)
    h_far = (h_crossed, swap(h_crossed))
    far_back, far_given, far_kept = expert_rows(h_far, cot_far, first_weight, second_weight, half)
    far_sum = add_low(far_back, swap(far_given))
    far_total = cross(far_sum)
    far_kept[0] = after(far_kept[0], far_sum)
    far_out, far_given, *sums = expert_weights(h_far, cot_far, far_kept, second_weight, (), half)
    back = trade(after(add_low(own_back, swap(own_given), far_total), far_out))
    own_out, out_given, grad_first, grad_second = expert_weights(
        h_own, cot_own, own_kept, second_weight, sums, half
    )
    far_total = cross(after(add_low(far_out, swap(far_given)), far_total))
    out_given = swap(out_given)
    h_part, router_part = call(
        combine_kernel,
        [near_shape((group_rows, width), FULL), near_shape((experts, width), FULL)],
        base,
        after(back, own_out),
        slot_row,
        slot_col,
        gates,
        ext,
        far(h_two),
        flops=2 * slots * group_rows * width,
        smem=(0,),
    )
    router_part = jnp.pad(router_part, ((2, extra_width - 2 - experts), (0, 0)))
    qk_part, vx_part, one_part, resid_grad, _, _ = call(
        backward_kernel,
        [
            near_shape((width, 2 * inner), LOW),
            near_shape((width, 2 * inner + extra_width), LOW),
            near_shape((group_rows, width), FULL),
            near_shape((group_rows, width), FULL),
            near_shape((group_rows, 2 * inner), LOW),
            near_shape((group_rows, inner), LOW),
        ],
        h_part,
        swap(h_part),
        *map(far, (cotangent, residual, rows_far)),
        ext,
        *map(far, (qk_far, vx_far, h_one, qkv, probs, mixed)),
        router_part,
        limit=14,
        flops=20 * group_rows * width * inner + 12 * group_rows * group_rows * inner,
    )

    own_start = core * tok_rows
    other_start = (1 - core) * tok_rows

    def rows_at(values, start):
        return lax.dynamic_slice_in_dim(values, start, tok_rows, 0)

    one_other = swap(rows_at(one_part, other_start).astype(LOW)).astype(FULL)
    qk_sum = qk_part.reshape((2,) * bits + (width // dp_count, 2 * inner))
    vx_sum = vx_part.reshape((2,) * bits + (width // dp_count, 2 * inner + extra_width))
    for step in range(bits):
        vx_sum = halve(vx_sum, order_b[bits - 1 - step], bits)
        qk_sum = halve(qk_sum, order_a[bits - 1 - step], bits)
        if step == 0:
            out_rows = add_low(own_out, out_given, after(far_total, qk_sum))
            back_out = trade(out_rows).reshape(slots, width)
    qk_sum = qk_sum.reshape(width // dp_count, 2 * inner)
    vx_sum = vx_sum.reshape(width // dp_count, 2 * inner + extra_width)

    out_part = contract_rows(dispatch, back_out)
    block_out = rows_at(residual, own_start) + (
        rows_at(out_part, own_start) + swap(rows_at(out_part, other_start))
    )
    scaled_one = (rows_at(one_part, own_start) + one_other) * ext[0:1, :]
    inv_own = inverse_rms(block_in)
    normed_own = block_in * inv_own
    grad_in = rows_at(resid_grad, own_start) + inv_own * (
        scaled_one - normed_own * jnp.mean(scaled_one * normed_own, axis=1, keepdims=True)
    )
    extra_sum = vx_sum[:, 2 * inner :]
    extra_sum = extra_sum + swap(extra_sum)
    share = extra_sum.shape[0] // 2
    extra_own = lax.dynamic_slice_in_dim(extra_sum, core * share, share, 0)
    return (
        block_out,
        grad_in,
        qk_sum[:, :inner],
        qk_sum[:, inner:],
        vx_sum[:, :inner],
        vx_sum[:, inner : 2 * inner].T,
        extra_own[:, 2 : 2 + experts],
        extra_own[:, 0],
        extra_own[:, 1],
        grad_first[None],
        grad_second[None],
    )


def solution(mesh):
    in_specs = (
        P(("dp", "tensor"), None),
        P("dp", None),
        P("dp", None),
        P("dp", "tensor"),
        P("dp", "tensor"),
        P("dp", "tensor"),
        P("tensor", "dp"),
        P("dp", None),
        P("dp"),
        P("dp"),
        P("dp", None, "tensor"),
        P("dp", "tensor", None),
        P("dp", None),
    )
    out_specs = (
        P(("dp", "tensor"), None),
        P(("dp", "tensor"), None),
        P("dp", "tensor"),
        P("dp", "tensor"),
        P("dp", "tensor"),
        P("tensor", "dp"),
        P(("dp", "tensor"), None),
        P(("dp", "tensor")),
        P(("dp", "tensor")),
        P("dp", None, "tensor"),
        P("dp", "tensor", None),
    )
    return jax.shard_map(local, mesh=mesh, in_specs=in_specs, out_specs=out_specs, check_vma=False)
```

```python
import math

import jax
import jax.numpy as jnp
from jax import lax
from jax.experimental import pallas as pl
from jax.experimental.pallas import tpu as pltpu
from jax.sharding import PartitionSpec as P

HEAD_DIM = 64
LANES = 128


EPSILON = 1e-06
NEGATIVE = -1e30
MIB = 1024 * 1024
EXTRA_ROWS = 16
LOW = jnp.bfloat16
FULL = jnp.float32


def dot(left_side, right_side):
    return jnp.dot(left_side, right_side, preferred_element_type=FULL)


def contract_rows(left_side, right_side):
    return lax.dot_general(
        left_side, right_side, (((0,), (0,)), ((), ())), preferred_element_type=FULL
    )


def contract_cols(left_side, right_side):
    return lax.dot_general(
        left_side, right_side, (((1,), (1,)), ((), ())), preferred_element_type=FULL
    )


def split_low(values):
    high = values.astype(LOW)
    return high, (values - high.astype(FULL)).astype(LOW)


def iota(shape, axis):
    return lax.broadcasted_iota(jnp.int32, shape, axis)


def swap(values):
    return lax.ppermute(values, "tensor", [(0, 1), (1, 0)])


def bit_orders():
    bits = lax.axis_size("dp").bit_length() - 1
    falling = list(range(bits - 1, -1, -1))
    return falling, falling[:-2] + [falling[-1], falling[-2]]


def partners(bit):
    return [(i, i ^ (1 << bit)) for i in range(lax.axis_size("dp"))]


def double(block, bit, bits):
    other = lax.ppermute(block, "dp", partners(bit))
    axis = bits - 1 - bit
    upper = ((lax.axis_index("dp") >> bit) & 1) == 1
    return jnp.where(
        upper,
        jnp.concatenate([other, block], axis=axis),
        jnp.concatenate([block, other], axis=axis),
    )


def halve(block, bit, bits):
    axis, place = bits - 1 - bit, (lax.axis_index("dp") >> bit) & 1
    given = lax.dynamic_index_in_dim(block, 1 - place, axis, keepdims=True).astype(LOW)
    kept = lax.dynamic_index_in_dim(block, place, axis, keepdims=True)
    return kept.astype(FULL) + lax.ppermute(given, "dp", partners(bit)).astype(FULL)


def trade(values):
    experts, dp_count = values.shape[0], lax.axis_size("dp")
    owners = dp_count // experts
    groups = [[owners * e + o for e in range(experts)] for o in range(owners)]
    return lax.all_to_all(
        values, "dp", split_axis=0, concat_axis=0, tiled=True, axis_index_groups=groups
    )


def cross(values):
    return lax.ppermute(values, "dp", partners(0))


def after(values, *others):
    return lax.optimization_barrier((values, *others))[0]


def add_low(*parts):
    return sum(part.astype(FULL) for part in parts).astype(LOW)


def far(values):
    return pltpu.with_memory_space_constraint(values, pltpu.HBM)


def near_shape(shape, kind):
    return jax.ShapeDtypeStruct(shape, kind)


def far_shape(shape, kind):
    return pltpu.HBM(shape, kind)


def call(kernel, out_shape, *operands, flops=0, smem=(), limit=8):
    moved = sum(x.size * x.dtype.itemsize for x in operands)
    return pl.pallas_call(
        kernel,
        out_shape=out_shape,
        in_specs=[
            pl.BlockSpec(memory_space=pltpu.SMEM if i in smem else pltpu.VMEM)
            for i in range(len(operands))
        ],
        out_specs=[pl.BlockSpec(memory_space=pltpu.VMEM) for _ in out_shape],
        compiler_params=pltpu.CompilerParams(vmem_limit_bytes=limit * MIB),
        cost_estimate=pl.CostEstimate(flops=flops, bytes_accessed=2 * moved, transcendentals=0),
    )(*operands)


def inverse_rms(rows):
    return lax.rsqrt(jnp.mean(rows * rows, axis=1, keepdims=True) + EPSILON)


GELU_SCALE = math.sqrt(2.0 / math.pi)
GELU_CUBE = 0.044715


def attention_kernel(
    len_ref, rows_ref, qk_ref, vx_ref, attn_ref, ext_ref, h_ref, qkv_ref, probs_ref, mixed_ref, rows_out, qk_out, vx_out
):
    group_rows = rows_ref.shape[0]
    inner = qk_ref.shape[1] // 2
    rows = rows_ref[...]
    rows_out[...] = rows
    qk_out[...] = qk_ref[...]
    vx_out[...] = vx_ref[...]
    ext = vx_ref[:, 2 * inner :].astype(FULL).T
    ext_ref[...] = ext
    h_one = (rows * inverse_rms(rows) * ext[0:1, :]).astype(LOW)
    h_ref[...] = h_one
    qkv_ref[:, : 2 * inner] = dot(h_one, qk_ref[...]).astype(LOW)
    qkv_ref[:, 2 * inner :] = dot(h_one, vx_ref[:, :inner]).astype(LOW)
    down, across = iota((group_rows, group_rows), 0), iota((group_rows, group_rows), 1)
    allowed = down >= across
    end = jnp.int32(0)
    for place in range(len_ref.shape[1]):
        end = end + len_ref[0, place]
        allowed = allowed & ((down >= end) == (across >= end))
    low_lanes = iota((group_rows, LANES), 1) < HEAD_DIM
    for pair in range(inner // LANES):
        at = pair * LANES
        queries = qkv_ref[:, at : at + LANES]
        key_rows = qkv_ref[:, inner + at : inner + at + LANES]
        value_rows = qkv_ref[:, 2 * inner + at : 2 * inner + at + LANES]
        outs = []
        for sub in range(2):
            own = low_lanes if sub == 0 else ~low_lanes
            scores = contract_cols(jnp.where(own, queries, jnp.zeros_like(queries)), key_rows)
            scores = jnp.where(allowed, scores * HEAD_DIM ** (-0.5), NEGATIVE)
            terms = jnp.exp(scores - jnp.max(scores, axis=1, keepdims=True))
            probs = terms / jnp.sum(terms, axis=1, keepdims=True)
            probs_ref[2 * pair + sub] = probs
            outs.append(dot(probs.astype(LOW), value_rows))
        mixed_ref[:, at : at + LANES] = jnp.where(low_lanes, outs[0], outs[1]).astype(LOW)
    attn_ref[...] = contract_cols(mixed_ref[...], vx_ref[:, inner : 2 * inner])


def slot_tables(slot_row, base, half):
    experts, group_rows = slot_row.shape
    count, shift = experts * half, half.bit_length() - 1
    of_expert = (iota((count, experts), 0) >> shift) == iota((count, experts), 1)
    wanted = (iota((count, 1), 0) & (half - 1)) + base
    here = dot(of_expert.astype(LOW), slot_row) == wanted.astype(FULL)
    return here, of_expert


def dispatch_kernel(
    base_ref, rows_ref, attn_ref, other_ref, ext_ref, slot_ref, resid_ref, h_ref, gates_ref, send_ref
):
    experts, rows_sent, _ = send_ref.shape
    blocks = rows_ref.shape[1] // LANES
    half = (rows_sent - EXTRA_ROWS) // blocks
    count = experts * half
    residual = rows_ref[...] + (attn_ref[...] + other_ref[...])
    resid_ref[...] = residual
    h_two = (residual * inverse_rms(residual) * ext_ref[1:2, :]).astype(LOW)
    h_ref[...] = h_two
    slot_row = slot_ref[...]
    hits = slot_row >= 0
    all_logits = contract_cols(ext_ref[...].astype(LOW), h_two)
    logits = all_logits[2 : 2 + experts, :]
    peak = jnp.max(jnp.where(hits, logits, NEGATIVE), axis=0, keepdims=True)
    terms = jnp.where(hits, jnp.exp(jnp.where(hits, logits - peak, 0.0)), 0.0)
    gates = terms / jnp.sum(terms, axis=0, keepdims=True)
    gates_ref[...] = gates
    here, of_expert = slot_tables(slot_row, base_ref[0], half)
    one_hot = here.astype(LOW)
    picked = dot(one_hot, h_two).astype(LOW).reshape(experts, half, blocks * LANES)
    high, low = split_low(gates)
    by_expert = contract_cols(one_hot, high) + contract_cols(one_hot, low)
    gate_col = jnp.sum(jnp.where(of_expert, by_expert, 0.0), axis=1, keepdims=True)
    on_lane = iota((count, LANES), 1) == (iota((count, LANES), 0) & (half - 1))
    high_rows, low_rows = [
        contract_rows(of_expert.astype(LOW), jnp.where(on_lane, part.astype(FULL), 0.0).astype(LOW))
        for part in split_low(gate_col)
    ]
    sub = iota((EXTRA_ROWS, LANES), 0)
    for block in range(blocks):
        send_ref[:, block * half : (block + 1) * half, :] = picked[
            :, :, block * LANES : (block + 1) * LANES
        ]
    for expert in range(experts):
        send_ref[expert, blocks * half :, :] = jnp.where(
            sub == 0,
            high_rows[expert : expert + 1, :],
            jnp.where(sub == 1, low_rows[expert : expert + 1, :], 0.0),
        ).astype(LOW)


def rows_of(ref, half):
    blocks = (ref.shape[1] - EXTRA_ROWS) // half
    return jnp.concatenate(
        [
            ref[:, at * half : (at + 1) * half, :].reshape(ref.shape[0] * half, LANES)
            for at in range(blocks)
        ],
        axis=1,
    )


def gated_cot(gate, cot_ref):
    sources, half, width = cot_ref.shape
    return (gate * cot_ref[...].reshape(sources * half, width).astype(FULL)).astype(LOW)


def expert_step(half, h_ref, cot_ref, first_ref, second_ref, back_ref, hid_ref, pre_ref, gate_ref):
    sources = h_ref.shape[0]
    blocks = (h_ref.shape[1] - EXTRA_ROWS) // half
    count, shift = sources * half, half.bit_length() - 1
    extra = h_ref[:, blocks * half :, :].reshape(sources * EXTRA_ROWS, LANES)
    source = iota((count, sources * EXTRA_ROWS), 0) >> shift
    row = iota((count, sources * EXTRA_ROWS), 1)
    two_rows = (row == source * EXTRA_ROWS) | (row == source * EXTRA_ROWS + 1)
    on_lane = iota((count, LANES), 1) == (iota((count, LANES), 0) & (half - 1))
    gate_lanes = dot(two_rows.astype(LOW), extra)
    gate = jnp.sum(jnp.where(on_lane, gate_lanes, 0.0), axis=1, keepdims=True)
    gate_ref[...] = jnp.broadcast_to(gate, (count, LANES))
    arrived = gated_cot(gate, cot_ref)
    incoming = rows_of(h_ref, half)
    pre = dot(incoming, first_ref[...])
    grad_hidden = contract_cols(arrived, second_ref[...])
    square = pre * pre
    bend = jnp.tanh(GELU_SCALE * pre * (1.0 + GELU_CUBE * square))
    rise = 0.5 * (1.0 + bend)
    hidden = (pre * rise).astype(LOW)
    hid_ref[...] = hidden
    slope = rise + (0.5 * GELU_SCALE) * pre * (1.0 - bend * bend) * (1.0 + 3.0 * GELU_CUBE * square)
    gated = jnp.sum(hidden.astype(FULL) * grad_hidden, axis=1, keepdims=True)
    grad_pre = (grad_hidden * slope).astype(LOW)
    pre_ref[...] = grad_pre
    grad_rows = contract_cols(grad_pre, first_ref[...]).astype(LOW).reshape(sources, half, blocks * LANES)
    for block in range(blocks):
        back_ref[:, block * half : (block + 1) * half, :] = grad_rows[
            :, :, block * LANES : (block + 1) * LANES
        ]
    source = iota((sources * EXTRA_ROWS, count), 1) >> shift
    row = iota((sources * EXTRA_ROWS, count), 0)
    high, low = [
        jnp.where(on_lane, part.astype(FULL), 0.0).astype(LOW) for part in split_low(gated)
    ]
    rows_back = dot((row == source * EXTRA_ROWS).astype(LOW), high) + dot(
        (row == source * EXTRA_ROWS + 1).astype(LOW), low
    )
    back_ref[:, blocks * half :, :] = rows_back.astype(LOW).reshape(sources, EXTRA_ROWS, LANES)


def part_specs(sources, steps, shapes):
    maps = (lambda i: (jnp.minimum(i, steps - 1), 0, 0), lambda i: (jnp.maximum(i - steps, 0), 0, 0))
    return [pl.BlockSpec((sources, *shape), place) for shape in shapes for place in maps]


def in_halves(steps, first, second):
    pl.when(pl.program_id(0) < steps)(first)
    pl.when(pl.program_id(0) >= steps)(second)


def whole(array):
    rank = len(array.shape)
    return pl.BlockSpec(array.shape, lambda i: (0,) * rank, pipeline_mode=pl.Buffered(1))


def expert_rows(h_rows, cot_rows, first_weight, second_weight, half):
    experts, rows_sent, _ = h_rows[0].shape
    width, hidden_width = first_weight.shape
    sources = min(experts, 256 // half)
    count, steps = sources * half, experts // sources
    total = 2 * experts * half

    def kernel(h_a, h_b, cot_a, cot_b, first_ref, second_ref, back_a, back_b, *kept):
        in_halves(
            steps,
            lambda: expert_step(half, h_a, cot_a, first_ref, second_ref, back_a, *kept),
            lambda: expert_step(half, h_b, cot_b, first_ref, second_ref, back_b, *kept),
        )

    lanes = ((hidden_width, LOW), (hidden_width, LOW), (LANES, FULL))
    back_a, back_b, *kept = pl.pallas_call(
        kernel,
        grid=(2 * steps,),
        out_shape=[near_shape(h_rows[0].shape, LOW)] * 2
        + [far_shape((total, n), kind) for n, kind in lanes],
        in_specs=part_specs(sources, steps, [(rows_sent, LANES), (half, width)])
        + [whole(first_weight), whole(second_weight)],
        out_specs=part_specs(sources, steps, [(rows_sent, LANES)])
        + [pl.BlockSpec((count, n), lambda i: (i, 0)) for n, _ in lanes],
        compiler_params=pltpu.CompilerParams(vmem_limit_bytes=16 * MIB),
        cost_estimate=pl.CostEstimate(
            flops=6 * total * width * hidden_width,
            bytes_accessed=12 * total * width,
            transcendentals=total * hidden_width,
        ),
    )(*h_rows, *cot_rows, far(first_weight), far(second_weight))
    return back_a, back_b, kept


def expert_weights(h_rows, cot_rows, kept, second_weight, sums, half):
    experts, rows_sent, _ = h_rows[0].shape
    hidden_width, width = second_weight.shape
    sources = min(experts, 256 // half)
    count, steps = sources * half, experts // sources
    total = 2 * experts * half

    def kernel(h_a, h_b, cot_a, cot_b, hid_ref, pre_ref, gate_ref, second_ref, *refs):
        out_a, out_b, grad_first, grad_second = refs[-4:]

        @pl.when(pl.program_id(0) == 0)
        def _():
            for at, grad in enumerate((grad_first, grad_second)):
                grad[...] = refs[at][...] if sums else jnp.zeros(grad.shape, FULL)

        def step(h_ref, cot_ref, out_ref):
            hidden, gate = hid_ref[...], gate_ref[:, 0:1]
            produced = dot(hidden, second_ref[...])
            out_ref[...] = (gate * produced).astype(LOW).reshape(out_ref.shape)
            grad_first[...] += contract_rows(rows_of(h_ref, half), pre_ref[...])
            grad_second[...] += contract_rows(hidden, gated_cot(gate, cot_ref))

        in_halves(steps, lambda: step(h_a, cot_a, out_a), lambda: step(h_b, cot_b, out_b))

    grads = [far_shape((width, hidden_width), FULL), far_shape((hidden_width, width), FULL)]
    return pl.pallas_call(
        kernel,
        grid=(2 * steps,),
        out_shape=[near_shape((experts, half, width), LOW)] * 2 + grads,
        in_specs=part_specs(sources, steps, [(rows_sent, LANES), (half, width)])
        + [pl.BlockSpec((count, x.shape[1]), lambda i: (i, 0)) for x in kept]
        + [whole(x) for x in (second_weight, *sums)],
        out_specs=part_specs(sources, steps, [(half, width)]) + [whole(x) for x in grads],
        compiler_params=pltpu.CompilerParams(vmem_limit_bytes=24 * MIB),
        cost_estimate=pl.CostEstimate(
            flops=6 * total * width * hidden_width,
            bytes_accessed=10 * total * width,
            transcendentals=0,
        ),
    )(*h_rows, *cot_rows, *map(far, (*kept, second_weight, *sums)))


def combine_kernel(base_ref, back_ref, slot_ref, col_ref, gates_ref, ext_ref, h_ref, part_ref, router_ref):
    experts, rows_sent, _ = back_ref.shape
    blocks = h_ref.shape[1] // LANES
    half = (rows_sent - EXTRA_ROWS) // blocks
    count = experts * half
    slot_row = slot_ref[...]
    hits = slot_row >= 0
    here, of_expert = slot_tables(slot_row, base_ref[0], half)
    extra = back_ref[:, blocks * half :, :].reshape(experts * EXTRA_ROWS, LANES)
    reach = EXTRA_ROWS
    shift, reach_shift = half.bit_length() - 1, reach.bit_length() - 1
    row = iota((count, experts * reach), 1)
    wanted = (row >> reach_shift) == (iota((count, experts * reach), 0) >> shift)
    wanted = wanted & ((row & (EXTRA_ROWS - 1)) < 2)
    on_lane = iota((count, LANES), 1) == (iota((count, LANES), 0) & (half - 1))
    lanes = dot(wanted.astype(LOW), extra)
    slot_gated = jnp.sum(jnp.where(on_lane, lanes, 0.0), axis=1, keepdims=True)
    high, low = split_low(jnp.where(here, slot_gated, 0.0))
    gated = contract_rows(of_expert.astype(LOW), high) + contract_rows(of_expert.astype(LOW), low)
    gated = jnp.where(hits, gated, 0.0)
    logit_grad = gated - gates_ref[...] * jnp.sum(gated, axis=0, keepdims=True)
    logit_grad = jnp.where(hits, logit_grad, 0.0)
    high, low = split_low(logit_grad)
    router_ref[...] = dot(high, h_ref[...]) + dot(low, h_ref[...])
    router_rows = ext_ref[2 : 2 + experts, :].astype(LOW)
    expand = (iota((experts, count), 1) >> shift) == iota((experts, count), 0)
    wanted = (iota((1, count), 1) & (half - 1)) + base_ref[0]
    one_hot = (dot(col_ref[...], expand.astype(LOW)) == wanted.astype(FULL)).astype(LOW)
    for block in range(blocks):
        rows = back_ref[:, block * half : (block + 1) * half, :].reshape(count, LANES)
        at = slice(block * LANES, (block + 1) * LANES)
        part_ref[:, at] = (
            dot(one_hot, rows)
            + contract_rows(high, router_rows[:, at])
            + contract_rows(low, router_rows[:, at])
        )


def backward_kernel(
    part_ref, other_ref, cot_ref, resid_ref, rows_ref, ext_ref, qk_ref, vx_ref, h_ref, qkv_ref, probs_ref,
    mixed_ref, router_ref, qk_out, vx_out, one_ref, rgrad_ref, qkg_ref, vg_ref,
):
    group_rows = rows_ref.shape[0]
    inner = qk_ref.shape[1] // 2
    h_grad = part_ref[...] + other_ref[...]
    residual = resid_ref[...]
    inv_two = inverse_rms(residual)
    normed_two = residual * inv_two
    gain_two_row = 0.5 * jnp.sum(h_grad * normed_two, axis=0, keepdims=True)
    scaled = h_grad * ext_ref[1:2, :]
    resid_grad = cot_ref[...] + inv_two * (
        scaled - normed_two * jnp.mean(scaled * normed_two, axis=1, keepdims=True)
    )
    rgrad_ref[...] = resid_grad
    attn_grad = resid_grad.astype(LOW)
    vx_out[:, inner : 2 * inner] = contract_rows(attn_grad, mixed_ref[...]).astype(LOW)
    mixed_grad = dot(attn_grad, vx_ref[:, inner : 2 * inner]).astype(LOW)
    low_lanes = iota((group_rows, LANES), 1) < HEAD_DIM
    for pair in range(inner // LANES):
        at = pair * LANES
        queries = qkv_ref[:, at : at + LANES]
        key_rows = qkv_ref[:, inner + at : inner + at + LANES]
        value_rows = qkv_ref[:, 2 * inner + at : 2 * inner + at + LANES]
        out_grad = mixed_grad[:, at : at + LANES]
        grads = []
        for sub in range(2):
            own = low_lanes if sub == 0 else ~low_lanes
            probs = probs_ref[2 * pair + sub]
            prob_grad = contract_cols(jnp.where(own, out_grad, jnp.zeros_like(out_grad)), value_rows)
            carry = jnp.sum(prob_grad * probs, axis=1, keepdims=True)
            score_grad = (probs * (prob_grad - carry)).astype(LOW)
            grads.append(
                (
                    dot(score_grad, key_rows),
                    contract_rows(score_grad, queries),
                    contract_rows(probs.astype(LOW), out_grad),
                )
            )
        scale = HEAD_DIM ** (-0.5)
        qkg_ref[:, at : at + LANES] = (jnp.where(low_lanes, grads[0][0], grads[1][0]) * scale).astype(LOW)
        qkg_ref[:, inner + at : inner + at + LANES] = (
            jnp.where(low_lanes, grads[0][1], grads[1][1]) * scale
        ).astype(LOW)
        vg_ref[:, at : at + LANES] = jnp.where(low_lanes, grads[0][2], grads[1][2]).astype(LOW)
    h_one = h_ref[...]
    qk_out[...] = contract_rows(h_one, qkg_ref[...]).astype(LOW)
    vx_out[:, :inner] = contract_rows(h_one, vg_ref[...]).astype(LOW)
    one_grad = contract_cols(qkg_ref[...], qk_ref[...]) + contract_cols(vg_ref[...], vx_ref[:, :inner])
    one_ref[...] = one_grad
    rows = rows_ref[...]
    gain_one_row = jnp.sum(one_grad * (rows * inverse_rms(rows)), axis=0, keepdims=True)
    router_rows = router_ref[...]
    sub = iota(router_rows.shape, 0)
    extra = jnp.where(sub == 0, gain_one_row, jnp.where(sub == 1, gain_two_row, router_rows))
    vx_out[:, 2 * inner :] = extra.T.astype(LOW)


def local(
    block_in,
    seq_lengths,
    routes,
    w_query,
    w_key,
    w_value,
    w_out_proj,
    router,
    gain_attn,
    gain_moe,
    expert_in,
    expert_out,
    cotangent,
):
    dp_count = lax.axis_size("dp")
    core = lax.axis_index("tensor")
    tok_rows, width = block_in.shape
    group_rows, top_count = routes.shape
    experts = router.shape[1]
    half = max(EXTRA_ROWS, top_count * group_rows // experts)
    slots = experts * half
    rows_sent = half * (width // LANES) + EXTRA_ROWS
    inner = w_query.shape[1]
    bits = dp_count.bit_length() - 1
    order_a, order_b = bit_orders()

    expert_ids = jnp.arange(experts, dtype=jnp.int32)
    hits = jnp.any(routes[:, :, None] == expert_ids[None, None, :], axis=1)
    places = jnp.arange(group_rows, dtype=jnp.int32)
    earlier = (places[:, None] > places[None, :]).astype(LOW)
    slot_col = jnp.where(hits, dot(earlier, hits.astype(LOW)), -1.0).astype(LOW)
    slot_row = slot_col.T
    base = core * half
    slot_ids = (base + jnp.arange(half, dtype=jnp.int32)).astype(LOW)
    in_slot = slot_row[:, None, :] == slot_ids[None, :, None]
    dispatch = in_slot.astype(LOW).reshape(slots, group_rows)
    base = base.reshape(1).astype(jnp.int32)
    cot_picked = dot(dispatch, cotangent.astype(LOW)).astype(LOW).reshape(experts, half, width)

    extra_width = -(-(2 + experts) // LANES) * LANES
    extra = jnp.concatenate(
        [
            gain_attn[:, None],
            gain_moe[:, None],
            router,
            jnp.zeros((router.shape[0], extra_width - 2 - experts), LOW),
        ],
        axis=1,
    )
    shard = jnp.concatenate([w_query, w_key, w_value, w_out_proj.T, extra], axis=1)
    lines = [[low + 4 * high for high in range(dp_count // 4)] for low in range(4)]
    line = lax.all_gather(shard, "dp", axis=0, tiled=True, axis_index_groups=lines)
    line = line.reshape((2,) * (bits - 2) + (1, 1) + shard.shape)
    qk_full, vx_full = line[..., : 2 * inner], line[..., 2 * inner :]
    for step in range(bits - 2, bits):
        vx_full = double(vx_full, order_b[step], bits)
        qk_full = double(qk_full, order_a[step], bits)
        if step == bits - 2:
            rows_all = lax.all_gather(after(block_in, vx_full), "tensor", axis=0, tiled=True)
    cot_own = trade(after(cot_picked, rows_all))
    qk_full = qk_full.reshape(width, 2 * inner)
    vx_full = vx_full.reshape(width, 2 * inner + extra_width)

    attn_part, ext, h_one, qkv, probs, mixed, rows_far, qk_far, vx_far = call(
        attention_kernel,
        [
            near_shape((group_rows, width), FULL),
            near_shape((extra_width, width), FULL),
            far_shape((group_rows, width), LOW),
            far_shape((group_rows, 3 * inner), LOW),
            far_shape((inner // HEAD_DIM, group_rows, group_rows), FULL),
            far_shape((group_rows, inner), LOW),
            far_shape(rows_all.shape, FULL),
            far_shape(qk_full.shape, LOW),
            far_shape(vx_full.shape, LOW),
        ],
        seq_lengths,
        rows_all,
        qk_full,
        vx_full,
        limit=14,
        flops=8 * group_rows * width * inner + 4 * group_rows * group_rows * inner,
        smem=(0,),
    )
    residual, h_two, gates, sent = call(
        dispatch_kernel,
        [
            far_shape((group_rows, width), FULL),
            far_shape((group_rows, width), LOW),
            near_shape((experts, group_rows), FULL),
            near_shape((experts, rows_sent, LANES), LOW),
        ],
        base,
        rows_all,
        attn_part,
        swap(attn_part),
        ext,
        slot_row,
        flops=2 * experts * half * group_rows * width,
        smem=(0,),
    )

    cot_crossed = cross(cot_own)
    cot_own = (cot_own, swap(cot_own))
    cot_far = (cot_crossed, swap(cot_crossed))
    h_own = trade(sent)
    h_crossed = cross(after(h_own, cot_crossed))
    h_own = (after(h_own, cot_far[1]), swap(h_own))
    first_weight = expert_in[0]
    second_weight = expert_out[0]
    own_back, own_given, own_kept = expert_rows(h_own, cot_own, first_weight, second_weight, half)
    h_crossed = after(h_crossed, own_back)
    h_far = (h_crossed, swap(h_crossed))
    far_back, far_given, far_kept = expert_rows(h_far, cot_far, first_weight, second_weight, half)
    far_sum = add_low(far_back, swap(far_given))
    far_total = cross(far_sum)
    far_kept[0] = after(far_kept[0], far_sum)
    far_out, far_given, *sums = expert_weights(h_far, cot_far, far_kept, second_weight, (), half)
    back_sum = after(add_low(own_back, swap(own_given), far_total), far_out)
    back = trade(back_sum)
    out_far = add_low(far_out, swap(far_given))
    own_kept[0] = after(own_kept[0], out_far, back_sum)
    own_out, out_given, grad_first, grad_second = expert_weights(
        h_own, cot_own, own_kept, second_weight, sums, half
    )
    out_far = cross(after(out_far, far_total))
    out_given = swap(out_given)
    h_part, router_part = call(
        combine_kernel,
        [near_shape((group_rows, width), FULL), near_shape((experts, width), FULL)],
        base,
        after(back, own_out, out_far),
        slot_row,
        slot_col,
        gates,
        ext,
        far(h_two),
        flops=2 * slots * group_rows * width,
        smem=(0,),
    )
    router_part = jnp.pad(router_part, ((2, extra_width - 2 - experts), (0, 0)))
    qk_part, vx_part, one_part, resid_grad, _, _ = call(
        backward_kernel,
        [
            near_shape((width, 2 * inner), LOW),
            near_shape((width, 2 * inner + extra_width), LOW),
            near_shape((group_rows, width), FULL),
            near_shape((group_rows, width), FULL),
            near_shape((group_rows, 2 * inner), LOW),
            near_shape((group_rows, inner), LOW),
        ],
        h_part,
        swap(h_part),
        *map(far, (cotangent, residual, rows_far)),
        ext,
        *map(far, (qk_far, vx_far, h_one, qkv, probs, mixed)),
        router_part,
        limit=14,
        flops=20 * group_rows * width * inner + 12 * group_rows * group_rows * inner,
    )

    own_start = core * tok_rows
    other_start = (1 - core) * tok_rows

    def rows_at(values, start):
        return lax.dynamic_slice_in_dim(values, start, tok_rows, 0)

    one_other = swap(rows_at(one_part, other_start).astype(LOW)).astype(FULL)
    qk_sum = qk_part.reshape((2,) * bits + (width // dp_count, 2 * inner))
    vx_sum = vx_part.reshape((2,) * bits + (width // dp_count, 2 * inner + extra_width))
    for step in range(bits):
        vx_sum = halve(vx_sum, order_b[bits - 1 - step], bits)
        qk_sum = halve(qk_sum, order_a[bits - 1 - step], bits)
        if step == 0:
            out_rows = add_low(own_out, out_given, after(out_far, one_other))
            back_out = trade(out_rows).reshape(slots, width)
    qk_sum = qk_sum.reshape(width // dp_count, 2 * inner)
    vx_sum = vx_sum.reshape(width // dp_count, 2 * inner + extra_width)

    out_part = contract_rows(dispatch, back_out)
    block_out = rows_at(residual, own_start) + (
        rows_at(out_part, own_start) + swap(rows_at(out_part, other_start))
    )
    scaled_one = (rows_at(one_part, own_start) + one_other) * ext[0:1, :]
    inv_own = inverse_rms(block_in)
    normed_own = block_in * inv_own
    grad_in = rows_at(resid_grad, own_start) + inv_own * (
        scaled_one - normed_own * jnp.mean(scaled_one * normed_own, axis=1, keepdims=True)
    )
    extra_sum = vx_sum[:, 2 * inner :]
    extra_sum = extra_sum + swap(extra_sum)
    share = extra_sum.shape[0] // 2
    extra_own = lax.dynamic_slice_in_dim(extra_sum, core * share, share, 0)
    return (
        block_out,
        grad_in,
        qk_sum[:, :inner],
        qk_sum[:, inner:],
        vx_sum[:, :inner],
        vx_sum[:, inner : 2 * inner].T,
        extra_own[:, 2 : 2 + experts],
        extra_own[:, 0],
        extra_own[:, 1],
        grad_first[None],
        grad_second[None],
    )


def solution(mesh):
    in_specs = (
        P(("dp", "tensor"), None),
        P("dp", None),
        P("dp", None),
        P("dp", "tensor"),
        P("dp", "tensor"),
        P("dp", "tensor"),
        P("tensor", "dp"),
        P("dp", None),
        P("dp"),
        P("dp"),
        P("dp", None, "tensor"),
        P("dp", "tensor", None),
        P("dp", None),
    )
    out_specs = (
        P(("dp", "tensor"), None),
        P(("dp", "tensor"), None),
        P("dp", "tensor"),
        P("dp", "tensor"),
        P("dp", "tensor"),
        P("tensor", "dp"),
        P(("dp", "tensor"), None),
        P(("dp", "tensor")),
        P(("dp", "tensor")),
        P("dp", None, "tensor"),
        P("dp", "tensor", None),
    )
    return jax.shard_map(local, mesh=mesh, in_specs=in_specs, out_specs=out_specs, check_vma=False)
```

```python
import math

import jax
import jax.numpy as jnp
from jax import lax
from jax.experimental import pallas as pl
from jax.experimental.pallas import tpu as pltpu
from jax.sharding import PartitionSpec as P

HEAD_DIM = 64
LANES = 128


EPSILON = 1e-06
NEGATIVE = -1e30
MIB = 1024 * 1024
EXTRA_ROWS = 16
LOW = jnp.bfloat16
FULL = jnp.float32


def dot(left_side, right_side):
    return jnp.dot(left_side, right_side, preferred_element_type=FULL)


def contract_rows(left_side, right_side):
    return lax.dot_general(
        left_side, right_side, (((0,), (0,)), ((), ())), preferred_element_type=FULL
    )


def contract_cols(left_side, right_side):
    return lax.dot_general(
        left_side, right_side, (((1,), (1,)), ((), ())), preferred_element_type=FULL
    )


def split_low(values):
    high = values.astype(LOW)
    return high, (values - high.astype(FULL)).astype(LOW)


def iota(shape, axis):
    return lax.broadcasted_iota(jnp.int32, shape, axis)


def swap(values):
    return lax.ppermute(values, "tensor", [(0, 1), (1, 0)])


def bit_orders():
    bits = lax.axis_size("dp").bit_length() - 1
    falling = list(range(bits - 1, -1, -1))
    return falling, falling[:-2] + [falling[-1], falling[-2]]


def partners(bit):
    return [(i, i ^ (1 << bit)) for i in range(lax.axis_size("dp"))]


def double(block, bit, bits):
    other = lax.ppermute(block, "dp", partners(bit))
    axis = bits - 1 - bit
    upper = ((lax.axis_index("dp") >> bit) & 1) == 1
    return jnp.where(
        upper,
        jnp.concatenate([other, block], axis=axis),
        jnp.concatenate([block, other], axis=axis),
    )


def halve(block, bit, bits):
    axis, place = bits - 1 - bit, (lax.axis_index("dp") >> bit) & 1
    given = lax.dynamic_index_in_dim(block, 1 - place, axis, keepdims=True).astype(LOW)
    kept = lax.dynamic_index_in_dim(block, place, axis, keepdims=True)
    return kept.astype(FULL) + lax.ppermute(given, "dp", partners(bit)).astype(FULL)


def trade(values):
    experts, dp_count = values.shape[0], lax.axis_size("dp")
    owners = dp_count // experts
    groups = [[owners * e + o for e in range(experts)] for o in range(owners)]
    return lax.all_to_all(
        values, "dp", split_axis=0, concat_axis=0, tiled=True, axis_index_groups=groups
    )


def cross(values):
    return lax.ppermute(values, "dp", partners(0))


def after(values, *others):
    return lax.optimization_barrier((values, *others))[0]


def add_low(*parts):
    return sum(part.astype(FULL) for part in parts).astype(LOW)


def far(values):
    return pltpu.with_memory_space_constraint(values, pltpu.HBM)


def near_shape(shape, kind):
    return jax.ShapeDtypeStruct(shape, kind)


def far_shape(shape, kind):
    return pltpu.HBM(shape, kind)


def call(kernel, out_shape, *operands, flops=0, smem=(), limit=8):
    moved = sum(x.size * x.dtype.itemsize for x in operands)
    return pl.pallas_call(
        kernel,
        out_shape=out_shape,
        in_specs=[
            pl.BlockSpec(memory_space=pltpu.SMEM if i in smem else pltpu.VMEM)
            for i in range(len(operands))
        ],
        out_specs=[pl.BlockSpec(memory_space=pltpu.VMEM) for _ in out_shape],
        compiler_params=pltpu.CompilerParams(vmem_limit_bytes=limit * MIB),
        cost_estimate=pl.CostEstimate(flops=flops, bytes_accessed=2 * moved, transcendentals=0),
    )(*operands)


def inverse_rms(rows):
    return lax.rsqrt(jnp.mean(rows * rows, axis=1, keepdims=True) + EPSILON)


GELU_SCALE = math.sqrt(2.0 / math.pi)
GELU_CUBE = 0.044715


def attention_kernel(
    len_ref, rows_ref, qk_ref, vx_ref, attn_ref, ext_ref, h_ref, qkv_ref, probs_ref, mixed_ref, rows_out, qk_out, vx_out
):
    group_rows = rows_ref.shape[0]
    inner = qk_ref.shape[1] // 2
    rows = rows_ref[...]
    rows_out[...] = rows
    qk_out[...] = qk_ref[...]
    vx_out[...] = vx_ref[...]
    ext = vx_ref[:, 2 * inner :].astype(FULL).T
    ext_ref[...] = ext
    h_one = (rows * inverse_rms(rows) * ext[0:1, :]).astype(LOW)
    h_ref[...] = h_one
    qkv_ref[:, : 2 * inner] = dot(h_one, qk_ref[...]).astype(LOW)
    qkv_ref[:, 2 * inner :] = dot(h_one, vx_ref[:, :inner]).astype(LOW)
    down, across = iota((group_rows, group_rows), 0), iota((group_rows, group_rows), 1)
    allowed = down >= across
    end = jnp.int32(0)
    for place in range(len_ref.shape[1]):
        end = end + len_ref[0, place]
        allowed = allowed & ((down >= end) == (across >= end))
    low_lanes = iota((group_rows, LANES), 1) < HEAD_DIM
    for pair in range(inner // LANES):
        at = pair * LANES
        queries = qkv_ref[:, at : at + LANES]
        key_rows = qkv_ref[:, inner + at : inner + at + LANES]
        value_rows = qkv_ref[:, 2 * inner + at : 2 * inner + at + LANES]
        outs = []
        for sub in range(2):
            own = low_lanes if sub == 0 else ~low_lanes
            scores = contract_cols(jnp.where(own, queries, jnp.zeros_like(queries)), key_rows)
            scores = jnp.where(allowed, scores * HEAD_DIM ** (-0.5), NEGATIVE)
            terms = jnp.exp(scores - jnp.max(scores, axis=1, keepdims=True))
            probs = terms / jnp.sum(terms, axis=1, keepdims=True)
            probs_ref[2 * pair + sub] = probs
            outs.append(dot(probs.astype(LOW), value_rows))
        mixed_ref[:, at : at + LANES] = jnp.where(low_lanes, outs[0], outs[1]).astype(LOW)
    attn_ref[...] = contract_cols(mixed_ref[...], vx_ref[:, inner : 2 * inner])


def slot_tables(slot_row, base, half):
    experts, group_rows = slot_row.shape
    count, shift = experts * half, half.bit_length() - 1
    of_expert = (iota((count, experts), 0) >> shift) == iota((count, experts), 1)
    wanted = (iota((count, 1), 0) & (half - 1)) + base
    here = dot(of_expert.astype(LOW), slot_row) == wanted.astype(FULL)
    return here, of_expert


def dispatch_kernel(
    base_ref, rows_ref, attn_ref, other_ref, ext_ref, slot_ref, resid_ref, h_ref, gates_ref, send_ref
):
    experts, rows_sent, _ = send_ref.shape
    blocks = rows_ref.shape[1] // LANES
    half = (rows_sent - EXTRA_ROWS) // blocks
    count = experts * half
    residual = rows_ref[...] + (attn_ref[...] + other_ref[...])
    resid_ref[...] = residual
    h_two = (residual * inverse_rms(residual) * ext_ref[1:2, :]).astype(LOW)
    h_ref[...] = h_two
    slot_row = slot_ref[...]
    hits = slot_row >= 0
    all_logits = contract_cols(ext_ref[...].astype(LOW), h_two)
    logits = all_logits[2 : 2 + experts, :]
    peak = jnp.max(jnp.where(hits, logits, NEGATIVE), axis=0, keepdims=True)
    terms = jnp.where(hits, jnp.exp(jnp.where(hits, logits - peak, 0.0)), 0.0)
    gates = terms / jnp.sum(terms, axis=0, keepdims=True)
    gates_ref[...] = gates
    here, of_expert = slot_tables(slot_row, base_ref[0], half)
    one_hot = here.astype(LOW)
    picked = dot(one_hot, h_two).astype(LOW).reshape(experts, half, blocks * LANES)
    high, low = split_low(gates)
    by_expert = contract_cols(one_hot, high) + contract_cols(one_hot, low)
    gate_col = jnp.sum(jnp.where(of_expert, by_expert, 0.0), axis=1, keepdims=True)
    on_lane = iota((count, LANES), 1) == (iota((count, LANES), 0) & (half - 1))
    high_rows, low_rows = [
        contract_rows(of_expert.astype(LOW), jnp.where(on_lane, part.astype(FULL), 0.0).astype(LOW))
        for part in split_low(gate_col)
    ]
    sub = iota((EXTRA_ROWS, LANES), 0)
    for block in range(blocks):
        send_ref[:, block * half : (block + 1) * half, :] = picked[
            :, :, block * LANES : (block + 1) * LANES
        ]
    for expert in range(experts):
        send_ref[expert, blocks * half :, :] = jnp.where(
            sub == 0,
            high_rows[expert : expert + 1, :],
            jnp.where(sub == 1, low_rows[expert : expert + 1, :], 0.0),
        ).astype(LOW)


def rows_of(ref, half):
    blocks = (ref.shape[1] - EXTRA_ROWS) // half
    return jnp.concatenate(
        [
            ref[:, at * half : (at + 1) * half, :].reshape(ref.shape[0] * half, LANES)
            for at in range(blocks)
        ],
        axis=1,
    )


def gated_cot(gate, cot_ref):
    sources, half, width = cot_ref.shape
    return (gate * cot_ref[...].reshape(sources * half, width).astype(FULL)).astype(LOW)


def expert_step(half, h_ref, cot_ref, first_ref, second_ref, back_ref, hid_ref, pre_ref, gate_ref):
    sources = h_ref.shape[0]
    blocks = (h_ref.shape[1] - EXTRA_ROWS) // half
    count, shift = sources * half, half.bit_length() - 1
    extra = h_ref[:, blocks * half :, :].reshape(sources * EXTRA_ROWS, LANES)
    source = iota((count, sources * EXTRA_ROWS), 0) >> shift
    row = iota((count, sources * EXTRA_ROWS), 1)
    two_rows = (row == source * EXTRA_ROWS) | (row == source * EXTRA_ROWS + 1)
    on_lane = iota((count, LANES), 1) == (iota((count, LANES), 0) & (half - 1))
    gate_lanes = dot(two_rows.astype(LOW), extra)
    gate = jnp.sum(jnp.where(on_lane, gate_lanes, 0.0), axis=1, keepdims=True)
    gate_ref[...] = jnp.broadcast_to(gate, (count, LANES))
    arrived = gated_cot(gate, cot_ref)
    incoming = rows_of(h_ref, half)
    pre = dot(incoming, first_ref[...])
    grad_hidden = contract_cols(arrived, second_ref[...])
    square = pre * pre
    bend = jnp.tanh(GELU_SCALE * pre * (1.0 + GELU_CUBE * square))
    rise = 0.5 * (1.0 + bend)
    hidden = (pre * rise).astype(LOW)
    hid_ref[...] = hidden
    slope = rise + (0.5 * GELU_SCALE) * pre * (1.0 - bend * bend) * (1.0 + 3.0 * GELU_CUBE * square)
    gated = jnp.sum(hidden.astype(FULL) * grad_hidden, axis=1, keepdims=True)
    grad_pre = (grad_hidden * slope).astype(LOW)
    pre_ref[...] = grad_pre
    grad_rows = contract_cols(grad_pre, first_ref[...]).astype(LOW).reshape(sources, half, blocks * LANES)
    for block in range(blocks):
        back_ref[:, block * half : (block + 1) * half, :] = grad_rows[
            :, :, block * LANES : (block + 1) * LANES
        ]
    source = iota((sources * EXTRA_ROWS, count), 1) >> shift
    row = iota((sources * EXTRA_ROWS, count), 0)
    high, low = [
        jnp.where(on_lane, part.astype(FULL), 0.0).astype(LOW) for part in split_low(gated)
    ]
    rows_back = dot((row == source * EXTRA_ROWS).astype(LOW), high) + dot(
        (row == source * EXTRA_ROWS + 1).astype(LOW), low
    )
    back_ref[:, blocks * half :, :] = rows_back.astype(LOW).reshape(sources, EXTRA_ROWS, LANES)


def part_specs(sources, steps, shapes):
    maps = (lambda i: (jnp.minimum(i, steps - 1), 0, 0), lambda i: (jnp.maximum(i - steps, 0), 0, 0))
    return [pl.BlockSpec((sources, *shape), place) for shape in shapes for place in maps]


def in_halves(steps, first, second):
    pl.when(pl.program_id(0) < steps)(first)
    pl.when(pl.program_id(0) >= steps)(second)


def whole(array):
    rank = len(array.shape)
    return pl.BlockSpec(array.shape, lambda i: (0,) * rank, pipeline_mode=pl.Buffered(1))


def expert_rows(h_rows, cot_rows, first_weight, second_weight, half):
    experts, rows_sent, _ = h_rows[0].shape
    width, hidden_width = first_weight.shape
    sources = min(experts, 256 // half)
    count, steps = sources * half, experts // sources
    total = 2 * experts * half

    def kernel(h_a, h_b, cot_a, cot_b, first_ref, second_ref, back_a, back_b, *kept):
        in_halves(
            steps,
            lambda: expert_step(half, h_a, cot_a, first_ref, second_ref, back_a, *kept),
            lambda: expert_step(half, h_b, cot_b, first_ref, second_ref, back_b, *kept),
        )

    lanes = ((hidden_width, LOW), (hidden_width, LOW), (LANES, FULL))
    back_a, back_b, *kept = pl.pallas_call(
        kernel,
        grid=(2 * steps,),
        out_shape=[near_shape(h_rows[0].shape, LOW)] * 2
        + [far_shape((total, n), kind) for n, kind in lanes],
        in_specs=part_specs(sources, steps, [(rows_sent, LANES), (half, width)])
        + [whole(first_weight), whole(second_weight)],
        out_specs=part_specs(sources, steps, [(rows_sent, LANES)])
        + [pl.BlockSpec((count, n), lambda i: (i, 0)) for n, _ in lanes],
        compiler_params=pltpu.CompilerParams(vmem_limit_bytes=16 * MIB),
        cost_estimate=pl.CostEstimate(
            flops=6 * total * width * hidden_width,
            bytes_accessed=12 * total * width,
            transcendentals=total * hidden_width,
        ),
    )(*h_rows, *cot_rows, far(first_weight), far(second_weight))
    return back_a, back_b, kept


def expert_weights(h_rows, cot_rows, kept, second_weight, sums, half):
    experts, rows_sent, _ = h_rows[0].shape
    hidden_width, width = second_weight.shape
    sources = min(experts, 256 // half)
    count, steps = sources * half, experts // sources
    total = 2 * experts * half

    def kernel(h_a, h_b, cot_a, cot_b, hid_ref, pre_ref, gate_ref, second_ref, *refs):
        out_a, out_b, grad_first, grad_second = refs[-4:]

        @pl.when(pl.program_id(0) == 0)
        def _():
            for at, grad in enumerate((grad_first, grad_second)):
                grad[...] = refs[at][...] if sums else jnp.zeros(grad.shape, FULL)

        def step(h_ref, cot_ref, out_ref):
            hidden, gate = hid_ref[...], gate_ref[:, 0:1]
            produced = dot(hidden, second_ref[...])
            out_ref[...] = (gate * produced).astype(LOW).reshape(out_ref.shape)
            grad_first[...] += contract_rows(rows_of(h_ref, half), pre_ref[...])
            grad_second[...] += contract_rows(hidden, gated_cot(gate, cot_ref))

        in_halves(steps, lambda: step(h_a, cot_a, out_a), lambda: step(h_b, cot_b, out_b))

    grads = [far_shape((width, hidden_width), FULL), far_shape((hidden_width, width), FULL)]
    return pl.pallas_call(
        kernel,
        grid=(2 * steps,),
        out_shape=[near_shape((experts, half, width), LOW)] * 2 + grads,
        in_specs=part_specs(sources, steps, [(rows_sent, LANES), (half, width)])
        + [pl.BlockSpec((count, x.shape[1]), lambda i: (i, 0)) for x in kept]
        + [whole(x) for x in (second_weight, *sums)],
        out_specs=part_specs(sources, steps, [(half, width)]) + [whole(x) for x in grads],
        compiler_params=pltpu.CompilerParams(vmem_limit_bytes=24 * MIB),
        cost_estimate=pl.CostEstimate(
            flops=6 * total * width * hidden_width,
            bytes_accessed=10 * total * width,
            transcendentals=0,
        ),
    )(*h_rows, *cot_rows, *map(far, (*kept, second_weight, *sums)))


def combine_kernel(base_ref, back_ref, slot_ref, col_ref, gates_ref, ext_ref, h_ref, part_ref, router_ref):
    experts, rows_sent, _ = back_ref.shape
    blocks = h_ref.shape[1] // LANES
    half = (rows_sent - EXTRA_ROWS) // blocks
    count = experts * half
    slot_row = slot_ref[...]
    hits = slot_row >= 0
    here, of_expert = slot_tables(slot_row, base_ref[0], half)
    extra = back_ref[:, blocks * half :, :].reshape(experts * EXTRA_ROWS, LANES)
    reach = EXTRA_ROWS
    shift, reach_shift = half.bit_length() - 1, reach.bit_length() - 1
    row = iota((count, experts * reach), 1)
    wanted = (row >> reach_shift) == (iota((count, experts * reach), 0) >> shift)
    wanted = wanted & ((row & (EXTRA_ROWS - 1)) < 2)
    on_lane = iota((count, LANES), 1) == (iota((count, LANES), 0) & (half - 1))
    lanes = dot(wanted.astype(LOW), extra)
    slot_gated = jnp.sum(jnp.where(on_lane, lanes, 0.0), axis=1, keepdims=True)
    high, low = split_low(jnp.where(here, slot_gated, 0.0))
    gated = contract_rows(of_expert.astype(LOW), high) + contract_rows(of_expert.astype(LOW), low)
    gated = jnp.where(hits, gated, 0.0)
    logit_grad = gated - gates_ref[...] * jnp.sum(gated, axis=0, keepdims=True)
    logit_grad = jnp.where(hits, logit_grad, 0.0)
    high, low = split_low(logit_grad)
    router_ref[...] = dot(high, h_ref[...]) + dot(low, h_ref[...])
    router_rows = ext_ref[2 : 2 + experts, :].astype(LOW)
    expand = (iota((experts, count), 1) >> shift) == iota((experts, count), 0)
    wanted = (iota((1, count), 1) & (half - 1)) + base_ref[0]
    one_hot = (dot(col_ref[...], expand.astype(LOW)) == wanted.astype(FULL)).astype(LOW)
    for block in range(blocks):
        rows = back_ref[:, block * half : (block + 1) * half, :].reshape(count, LANES)
        at = slice(block * LANES, (block + 1) * LANES)
        part_ref[:, at] = (
            dot(one_hot, rows)
            + contract_rows(high, router_rows[:, at])
            + contract_rows(low, router_rows[:, at])
        )


def backward_kernel(
    part_ref, other_ref, cot_ref, resid_ref, rows_ref, ext_ref, qk_ref, vx_ref, h_ref, qkv_ref, probs_ref,
    mixed_ref, router_ref, qk_out, vx_out, one_ref, rgrad_ref, qkg_ref, vg_ref,
):
    group_rows = rows_ref.shape[0]
    inner = qk_ref.shape[1] // 2
    h_grad = part_ref[...] + other_ref[...]
    residual = resid_ref[...]
    inv_two = inverse_rms(residual)
    normed_two = residual * inv_two
    gain_two_row = 0.5 * jnp.sum(h_grad * normed_two, axis=0, keepdims=True)
    scaled = h_grad * ext_ref[1:2, :]
    resid_grad = cot_ref[...] + inv_two * (
        scaled - normed_two * jnp.mean(scaled * normed_two, axis=1, keepdims=True)
    )
    rgrad_ref[...] = resid_grad
    attn_grad = resid_grad.astype(LOW)
    vx_out[:, inner : 2 * inner] = contract_rows(attn_grad, mixed_ref[...]).astype(LOW)
    mixed_grad = dot(attn_grad, vx_ref[:, inner : 2 * inner]).astype(LOW)
    low_lanes = iota((group_rows, LANES), 1) < HEAD_DIM
    for pair in range(inner // LANES):
        at = pair * LANES
        queries = qkv_ref[:, at : at + LANES]
        key_rows = qkv_ref[:, inner + at : inner + at + LANES]
        value_rows = qkv_ref[:, 2 * inner + at : 2 * inner + at + LANES]
        out_grad = mixed_grad[:, at : at + LANES]
        grads = []
        for sub in range(2):
            own = low_lanes if sub == 0 else ~low_lanes
            probs = probs_ref[2 * pair + sub]
            prob_grad = contract_cols(jnp.where(own, out_grad, jnp.zeros_like(out_grad)), value_rows)
            carry = jnp.sum(prob_grad * probs, axis=1, keepdims=True)
            score_grad = (probs * (prob_grad - carry)).astype(LOW)
            grads.append(
                (
                    dot(score_grad, key_rows),
                    contract_rows(score_grad, queries),
                    contract_rows(probs.astype(LOW), out_grad),
                )
            )
        scale = HEAD_DIM ** (-0.5)
        qkg_ref[:, at : at + LANES] = (jnp.where(low_lanes, grads[0][0], grads[1][0]) * scale).astype(LOW)
        qkg_ref[:, inner + at : inner + at + LANES] = (
            jnp.where(low_lanes, grads[0][1], grads[1][1]) * scale
        ).astype(LOW)
        vg_ref[:, at : at + LANES] = jnp.where(low_lanes, grads[0][2], grads[1][2]).astype(LOW)
    h_one = h_ref[...]
    qk_out[...] = contract_rows(h_one, qkg_ref[...]).astype(LOW)
    vx_out[:, :inner] = contract_rows(h_one, vg_ref[...]).astype(LOW)
    one_grad = contract_cols(qkg_ref[...], qk_ref[...]) + contract_cols(vg_ref[...], vx_ref[:, :inner])
    one_ref[...] = one_grad
    rows = rows_ref[...]
    gain_one_row = jnp.sum(one_grad * (rows * inverse_rms(rows)), axis=0, keepdims=True)
    router_rows = router_ref[...]
    sub = iota(router_rows.shape, 0)
    extra = jnp.where(sub == 0, gain_one_row, jnp.where(sub == 1, gain_two_row, router_rows))
    vx_out[:, 2 * inner :] = extra.T.astype(LOW)


def local(
    block_in,
    seq_lengths,
    routes,
    w_query,
    w_key,
    w_value,
    w_out_proj,
    router,
    gain_attn,
    gain_moe,
    expert_in,
    expert_out,
    cotangent,
):
    dp_count = lax.axis_size("dp")
    core = lax.axis_index("tensor")
    tok_rows, width = block_in.shape
    group_rows, top_count = routes.shape
    experts = router.shape[1]
    half = max(EXTRA_ROWS, top_count * group_rows // experts)
    slots = experts * half
    rows_sent = half * (width // LANES) + EXTRA_ROWS
    inner = w_query.shape[1]
    bits = dp_count.bit_length() - 1
    order_a, order_b = bit_orders()

    expert_ids = jnp.arange(experts, dtype=jnp.int32)
    hits = jnp.any(routes[:, :, None] == expert_ids[None, None, :], axis=1)
    places = jnp.arange(group_rows, dtype=jnp.int32)
    earlier = (places[:, None] > places[None, :]).astype(LOW)
    slot_col = jnp.where(hits, dot(earlier, hits.astype(LOW)), -1.0).astype(LOW)
    slot_row = slot_col.T
    base = core * half
    slot_ids = (base + jnp.arange(half, dtype=jnp.int32)).astype(LOW)
    in_slot = slot_row[:, None, :] == slot_ids[None, :, None]
    dispatch = in_slot.astype(LOW).reshape(slots, group_rows)
    base = base.reshape(1).astype(jnp.int32)
    cot_picked = dot(dispatch, cotangent.astype(LOW)).astype(LOW).reshape(experts, half, width)

    extra_width = -(-(2 + experts) // LANES) * LANES
    extra = jnp.concatenate(
        [
            gain_attn[:, None],
            gain_moe[:, None],
            router,
            jnp.zeros((router.shape[0], extra_width - 2 - experts), LOW),
        ],
        axis=1,
    )
    shard = jnp.concatenate([w_query, w_key, w_value, w_out_proj.T, extra], axis=1)
    lines = [[low + 4 * high for high in range(dp_count // 4)] for low in range(4)]
    line = lax.all_gather(shard, "dp", axis=0, tiled=True, axis_index_groups=lines)
    line = line.reshape((2,) * (bits - 2) + (1, 1) + shard.shape)
    qk_full, vx_full = line[..., : 2 * inner], line[..., 2 * inner :]
    for step in range(bits - 2, bits):
        vx_full = double(vx_full, order_b[step], bits)
        qk_full = double(qk_full, order_a[step], bits)
        if step == bits - 2:
            rows_all = lax.all_gather(after(block_in, vx_full), "tensor", axis=0, tiled=True)
    cot_own = trade(after(cot_picked, rows_all))
    qk_full = qk_full.reshape(width, 2 * inner)
    vx_full = vx_full.reshape(width, 2 * inner + extra_width)

    attn_part, ext, h_one, qkv, probs, mixed, rows_far, qk_far, vx_far = call(
        attention_kernel,
        [
            near_shape((group_rows, width), FULL),
            near_shape((extra_width, width), FULL),
            far_shape((group_rows, width), LOW),
            far_shape((group_rows, 3 * inner), LOW),
            far_shape((inner // HEAD_DIM, group_rows, group_rows), FULL),
            far_shape((group_rows, inner), LOW),
            far_shape(rows_all.shape, FULL),
            far_shape(qk_full.shape, LOW),
            far_shape(vx_full.shape, LOW),
        ],
        seq_lengths,
        rows_all,
        qk_full,
        vx_full,
        limit=14,
        flops=8 * group_rows * width * inner + 4 * group_rows * group_rows * inner,
        smem=(0,),
    )
    residual, h_two, gates, sent = call(
        dispatch_kernel,
        [
            far_shape((group_rows, width), FULL),
            far_shape((group_rows, width), LOW),
            near_shape((experts, group_rows), FULL),
            near_shape((experts, rows_sent, LANES), LOW),
        ],
        base,
        rows_all,
        attn_part,
        swap(attn_part),
        ext,
        slot_row,
        flops=2 * experts * half * group_rows * width,
        smem=(0,),
    )

    cot_crossed = cross(cot_own)
    cot_own = (cot_own, swap(cot_own))
    cot_far = (cot_crossed, swap(cot_crossed))
    h_own = trade(sent)
    h_crossed = cross(after(h_own, cot_crossed))
    h_own = (after(h_own, cot_far[1]), swap(h_own))
    first_weight = expert_in[0]
    second_weight = expert_out[0]
    own_back, own_given, own_kept = expert_rows(h_own, cot_own, first_weight, second_weight, half)
    h_crossed = after(h_crossed, own_back)
    h_far = (h_crossed, swap(h_crossed))
    far_back, far_given, far_kept = expert_rows(h_far, cot_far, first_weight, second_weight, half)
    far_sum = add_low(far_back, swap(far_given))
    far_total = cross(far_sum)
    far_kept[0] = after(far_kept[0], far_sum)
    far_out, far_given, *sums = expert_weights(h_far, cot_far, far_kept, second_weight, (), half)
    back_sum = after(add_low(own_back, swap(own_given), far_total), far_out)
    back = trade(back_sum)
    out_far = add_low(far_out, swap(far_given))
    own_kept[0] = after(own_kept[0], out_far, back_sum)
    own_out, out_given, grad_first, grad_second = expert_weights(
        h_own, cot_own, own_kept, second_weight, sums, half
    )
    out_far = cross(after(out_far, far_total))
    out_given = swap(out_given)
    back_out = trade(add_low(own_out, out_given, out_far)).reshape(slots, width)

    h_part, router_part = call(
        combine_kernel,
        [near_shape((group_rows, width), FULL), near_shape((experts, width), FULL)],
        base,
        after(back, own_out, out_far),
        slot_row,
        slot_col,
        gates,
        ext,
        far(h_two),
        flops=2 * slots * group_rows * width,
        smem=(0,),
    )
    router_part = jnp.pad(router_part, ((2, extra_width - 2 - experts), (0, 0)))
    qk_part, vx_part, one_part, resid_grad, _, _ = call(
        backward_kernel,
        [
            near_shape((width, 2 * inner), LOW),
            near_shape((width, 2 * inner + extra_width), LOW),
            near_shape((group_rows, width), FULL),
            near_shape((group_rows, width), FULL),
            near_shape((group_rows, 2 * inner), LOW),
            near_shape((group_rows, inner), LOW),
        ],
        h_part,
        swap(h_part),
        *map(far, (cotangent, residual, rows_far)),
        ext,
        *map(far, (qk_far, vx_far, h_one, qkv, probs, mixed)),
        router_part,
        limit=14,
        flops=20 * group_rows * width * inner + 12 * group_rows * group_rows * inner,
    )

    own_start = core * tok_rows
    other_start = (1 - core) * tok_rows

    def rows_at(values, start):
        return lax.dynamic_slice_in_dim(values, start, tok_rows, 0)

    one_other = swap(rows_at(one_part, other_start).astype(LOW)).astype(FULL)
    qk_sum = qk_part.reshape((2,) * bits + (width // dp_count, 2 * inner))
    vx_sum = vx_part.reshape((2,) * bits + (width // dp_count, 2 * inner + extra_width))
    for step in range(bits):
        vx_sum = halve(vx_sum, order_b[bits - 1 - step], bits)
        qk_sum = halve(qk_sum, order_a[bits - 1 - step], bits)
        if step == 1:
            back_out = after(back_out, vx_sum, qk_sum)
    qk_sum = qk_sum.reshape(width // dp_count, 2 * inner)
    vx_sum = vx_sum.reshape(width // dp_count, 2 * inner + extra_width)

    out_part = contract_rows(dispatch, back_out)
    block_out = rows_at(residual, own_start) + (
        rows_at(out_part, own_start) + swap(rows_at(out_part, other_start))
    )
    scaled_one = (rows_at(one_part, own_start) + one_other) * ext[0:1, :]
    inv_own = inverse_rms(block_in)
    normed_own = block_in * inv_own
    grad_in = rows_at(resid_grad, own_start) + inv_own * (
        scaled_one - normed_own * jnp.mean(scaled_one * normed_own, axis=1, keepdims=True)
    )
    extra_sum = vx_sum[:, 2 * inner :]
    extra_sum = extra_sum + swap(extra_sum)
    share = extra_sum.shape[0] // 2
    extra_own = lax.dynamic_slice_in_dim(extra_sum, core * share, share, 0)
    return (
        block_out,
        grad_in,
        qk_sum[:, :inner],
        qk_sum[:, inner:],
        vx_sum[:, :inner],
        vx_sum[:, inner : 2 * inner].T,
        extra_own[:, 2 : 2 + experts],
        extra_own[:, 0],
        extra_own[:, 1],
        grad_first[None],
        grad_second[None],
    )


def solution(mesh):
    in_specs = (
        P(("dp", "tensor"), None),
        P("dp", None),
        P("dp", None),
        P("dp", "tensor"),
        P("dp", "tensor"),
        P("dp", "tensor"),
        P("tensor", "dp"),
        P("dp", None),
        P("dp"),
        P("dp"),
        P("dp", None, "tensor"),
        P("dp", "tensor", None),
        P("dp", None),
    )
    out_specs = (
        P(("dp", "tensor"), None),
        P(("dp", "tensor"), None),
        P("dp", "tensor"),
        P("dp", "tensor"),
        P("dp", "tensor"),
        P("tensor", "dp"),
        P(("dp", "tensor"), None),
        P(("dp", "tensor")),
        P(("dp", "tensor")),
        P("dp", None, "tensor"),
        P("dp", "tensor", None),
    )
    return jax.shard_map(local, mesh=mesh, in_specs=in_specs, out_specs=out_specs, check_vma=False)
```

```python
import math

import jax
import jax.numpy as jnp
from jax import lax
from jax.experimental import pallas as pl
from jax.experimental.pallas import tpu as pltpu
from jax.sharding import PartitionSpec as P

HEAD_DIM = 64
LANES = 128


EPSILON = 1e-06
NEGATIVE = -1e30
MIB = 1024 * 1024
EXTRA_ROWS = 16
LOW = jnp.bfloat16
FULL = jnp.float32


def dot(left_side, right_side):
    return jnp.dot(left_side, right_side, preferred_element_type=FULL)


def contract_rows(left_side, right_side):
    return lax.dot_general(
        left_side, right_side, (((0,), (0,)), ((), ())), preferred_element_type=FULL
    )


def contract_cols(left_side, right_side):
    return lax.dot_general(
        left_side, right_side, (((1,), (1,)), ((), ())), preferred_element_type=FULL
    )


def split_low(values):
    high = values.astype(LOW)
    return high, (values - high.astype(FULL)).astype(LOW)


def iota(shape, axis):
    return lax.broadcasted_iota(jnp.int32, shape, axis)


def swap(values):
    return lax.ppermute(values, "tensor", [(0, 1), (1, 0)])


def bit_orders():
    bits = lax.axis_size("dp").bit_length() - 1
    falling = list(range(bits - 1, -1, -1))
    return falling, falling[:-2] + [falling[-1], falling[-2]]


def partners(bit):
    return [(i, i ^ (1 << bit)) for i in range(lax.axis_size("dp"))]


def double(block, bit, bits):
    other = lax.ppermute(block, "dp", partners(bit))
    axis = bits - 1 - bit
    upper = ((lax.axis_index("dp") >> bit) & 1) == 1
    return jnp.where(
        upper,
        jnp.concatenate([other, block], axis=axis),
        jnp.concatenate([block, other], axis=axis),
    )


def halve(block, bit, bits):
    axis, place = bits - 1 - bit, (lax.axis_index("dp") >> bit) & 1
    given = lax.dynamic_index_in_dim(block, 1 - place, axis, keepdims=True).astype(LOW)
    kept = lax.dynamic_index_in_dim(block, place, axis, keepdims=True)
    return kept.astype(FULL) + lax.ppermute(given, "dp", partners(bit)).astype(FULL)


def trade(values):
    experts, dp_count = values.shape[0], lax.axis_size("dp")
    owners = dp_count // experts
    groups = [[owners * e + o for e in range(experts)] for o in range(owners)]
    return lax.all_to_all(
        values, "dp", split_axis=0, concat_axis=0, tiled=True, axis_index_groups=groups
    )


def cross(values):
    return lax.ppermute(values, "dp", partners(0))


def after(values, *others):
    return lax.optimization_barrier((values, *others))[0]


def add_low(*parts):
    return sum(part.astype(FULL) for part in parts).astype(LOW)


def far(values):
    return pltpu.with_memory_space_constraint(values, pltpu.HBM)


def near_shape(shape, kind):
    return jax.ShapeDtypeStruct(shape, kind)


def far_shape(shape, kind):
    return pltpu.HBM(shape, kind)


def call(kernel, out_shape, *operands, flops=0, smem=(), limit=8):
    moved = sum(x.size * x.dtype.itemsize for x in operands)
    return pl.pallas_call(
        kernel,
        out_shape=out_shape,
        in_specs=[
            pl.BlockSpec(memory_space=pltpu.SMEM if i in smem else pltpu.VMEM)
            for i in range(len(operands))
        ],
        out_specs=[pl.BlockSpec(memory_space=pltpu.VMEM) for _ in out_shape],
        compiler_params=pltpu.CompilerParams(vmem_limit_bytes=limit * MIB),
        cost_estimate=pl.CostEstimate(flops=flops, bytes_accessed=2 * moved, transcendentals=0),
    )(*operands)


def inverse_rms(rows):
    return lax.rsqrt(jnp.mean(rows * rows, axis=1, keepdims=True) + EPSILON)


GELU_SCALE = math.sqrt(2.0 / math.pi)
GELU_CUBE = 0.044715


def attention_kernel(
    len_ref, rows_ref, qk_ref, vx_ref, attn_ref, ext_ref, h_ref, qkv_ref, probs_ref, mixed_ref, rows_out, qk_out, vx_out
):
    group_rows = rows_ref.shape[0]
    inner = qk_ref.shape[1] // 2
    rows = rows_ref[...]
    rows_out[...] = rows
    qk_out[...] = qk_ref[...]
    vx_out[...] = vx_ref[...]
    ext = vx_ref[:, 2 * inner :].astype(FULL).T
    ext_ref[...] = ext
    h_one = (rows * inverse_rms(rows) * ext[0:1, :]).astype(LOW)
    h_ref[...] = h_one
    qkv_ref[:, : 2 * inner] = dot(h_one, qk_ref[...]).astype(LOW)
    qkv_ref[:, 2 * inner :] = dot(h_one, vx_ref[:, :inner]).astype(LOW)
    down, across = iota((group_rows, group_rows), 0), iota((group_rows, group_rows), 1)
    allowed = down >= across
    end = jnp.int32(0)
    for place in range(len_ref.shape[1]):
        end = end + len_ref[0, place]
        allowed = allowed & ((down >= end) == (across >= end))
    low_lanes = iota((group_rows, LANES), 1) < HEAD_DIM
    for pair in range(inner // LANES):
        at = pair * LANES
        queries = qkv_ref[:, at : at + LANES]
        key_rows = qkv_ref[:, inner + at : inner + at + LANES]
        value_rows = qkv_ref[:, 2 * inner + at : 2 * inner + at + LANES]
        outs = []
        for sub in range(2):
            own = low_lanes if sub == 0 else ~low_lanes
            scores = contract_cols(jnp.where(own, queries, jnp.zeros_like(queries)), key_rows)
            scores = jnp.where(allowed, scores * HEAD_DIM ** (-0.5), NEGATIVE)
            terms = jnp.exp(scores - jnp.max(scores, axis=1, keepdims=True))
            probs = terms / jnp.sum(terms, axis=1, keepdims=True)
            probs_ref[2 * pair + sub] = probs
            outs.append(dot(probs.astype(LOW), value_rows))
        mixed_ref[:, at : at + LANES] = jnp.where(low_lanes, outs[0], outs[1]).astype(LOW)
    attn_ref[...] = contract_cols(mixed_ref[...], vx_ref[:, inner : 2 * inner])


def slot_tables(slot_row, base, half):
    experts, group_rows = slot_row.shape
    count, shift = experts * half, half.bit_length() - 1
    of_expert = (iota((count, experts), 0) >> shift) == iota((count, experts), 1)
    wanted = (iota((count, 1), 0) & (half - 1)) + base
    here = dot(of_expert.astype(LOW), slot_row) == wanted.astype(FULL)
    return here, of_expert


def dispatch_kernel(
    base_ref, rows_ref, attn_ref, other_ref, ext_ref, slot_ref, resid_ref, h_ref, gates_ref, send_ref
):
    experts, rows_sent, _ = send_ref.shape
    blocks = rows_ref.shape[1] // LANES
    half = (rows_sent - EXTRA_ROWS) // blocks
    count = experts * half
    residual = rows_ref[...] + (attn_ref[...] + other_ref[...])
    resid_ref[...] = residual
    h_two = (residual * inverse_rms(residual) * ext_ref[1:2, :]).astype(LOW)
    h_ref[...] = h_two
    slot_row = slot_ref[...]
    hits = slot_row >= 0
    all_logits = contract_cols(ext_ref[...].astype(LOW), h_two)
    logits = all_logits[2 : 2 + experts, :]
    peak = jnp.max(jnp.where(hits, logits, NEGATIVE), axis=0, keepdims=True)
    terms = jnp.where(hits, jnp.exp(jnp.where(hits, logits - peak, 0.0)), 0.0)
    gates = terms / jnp.sum(terms, axis=0, keepdims=True)
    gates_ref[...] = gates
    here, of_expert = slot_tables(slot_row, base_ref[0], half)
    one_hot = here.astype(LOW)
    picked = dot(one_hot, h_two).astype(LOW).reshape(experts, half, blocks * LANES)
    high, low = split_low(gates)
    by_expert = contract_cols(one_hot, high) + contract_cols(one_hot, low)
    gate_col = jnp.sum(jnp.where(of_expert, by_expert, 0.0), axis=1, keepdims=True)
    on_lane = iota((count, LANES), 1) == (iota((count, LANES), 0) & (half - 1))
    high_rows, low_rows = [
        contract_rows(of_expert.astype(LOW), jnp.where(on_lane, part.astype(FULL), 0.0).astype(LOW))
        for part in split_low(gate_col)
    ]
    sub = iota((EXTRA_ROWS, LANES), 0)
    for block in range(blocks):
        send_ref[:, block * half : (block + 1) * half, :] = picked[
            :, :, block * LANES : (block + 1) * LANES
        ]
    for expert in range(experts):
        send_ref[expert, blocks * half :, :] = jnp.where(
            sub == 0,
            high_rows[expert : expert + 1, :],
            jnp.where(sub == 1, low_rows[expert : expert + 1, :], 0.0),
        ).astype(LOW)


def rows_of(ref, half):
    blocks = (ref.shape[1] - EXTRA_ROWS) // half
    return jnp.concatenate(
        [
            ref[:, at * half : (at + 1) * half, :].reshape(ref.shape[0] * half, LANES)
            for at in range(blocks)
        ],
        axis=1,
    )


def gated_cot(gate, cot_ref):
    sources, half, width = cot_ref.shape
    return (gate * cot_ref[...].reshape(sources * half, width).astype(FULL)).astype(LOW)


def expert_core(half, h_ref, cot_ref, first_ref, second_ref):
    sources = h_ref.shape[0]
    blocks = (h_ref.shape[1] - EXTRA_ROWS) // half
    count, shift = sources * half, half.bit_length() - 1
    extra = h_ref[:, blocks * half :, :].reshape(sources * EXTRA_ROWS, LANES)
    source = iota((count, sources * EXTRA_ROWS), 0) >> shift
    row = iota((count, sources * EXTRA_ROWS), 1)
    two_rows = (row == source * EXTRA_ROWS) | (row == source * EXTRA_ROWS + 1)
    on_lane = iota((count, LANES), 1) == (iota((count, LANES), 0) & (half - 1))
    gate_lanes = dot(two_rows.astype(LOW), extra)
    gate = jnp.sum(jnp.where(on_lane, gate_lanes, 0.0), axis=1, keepdims=True)
    arrived = gated_cot(gate, cot_ref)
    incoming = rows_of(h_ref, half)
    pre = dot(incoming, first_ref[...])
    grad_hidden = contract_cols(arrived, second_ref[...])
    square = pre * pre
    bend = jnp.tanh(GELU_SCALE * pre * (1.0 + GELU_CUBE * square))
    rise = 0.5 * (1.0 + bend)
    hidden = (pre * rise).astype(LOW)
    slope = rise + (0.5 * GELU_SCALE) * pre * (1.0 - bend * bend) * (1.0 + 3.0 * GELU_CUBE * square)
    grad_pre = (grad_hidden * slope).astype(LOW)
    return incoming, gate, arrived, hidden, grad_hidden, grad_pre


def expert_step(half, h_ref, cot_ref, first_ref, second_ref, back_ref):
    sources = h_ref.shape[0]
    blocks = (h_ref.shape[1] - EXTRA_ROWS) // half
    count, shift = sources * half, half.bit_length() - 1
    on_lane = iota((count, LANES), 1) == (iota((count, LANES), 0) & (half - 1))
    _, _, _, hidden, grad_hidden, grad_pre = expert_core(half, h_ref, cot_ref, first_ref, second_ref)
    gated = jnp.sum(hidden.astype(FULL) * grad_hidden, axis=1, keepdims=True)
    grad_rows = contract_cols(grad_pre, first_ref[...]).astype(LOW).reshape(sources, half, blocks * LANES)
    for block in range(blocks):
        back_ref[:, block * half : (block + 1) * half, :] = grad_rows[
            :, :, block * LANES : (block + 1) * LANES
        ]
    source = iota((sources * EXTRA_ROWS, count), 1) >> shift
    row = iota((sources * EXTRA_ROWS, count), 0)
    high, low = [
        jnp.where(on_lane, part.astype(FULL), 0.0).astype(LOW) for part in split_low(gated)
    ]
    rows_back = dot((row == source * EXTRA_ROWS).astype(LOW), high) + dot(
        (row == source * EXTRA_ROWS + 1).astype(LOW), low
    )
    back_ref[:, blocks * half :, :] = rows_back.astype(LOW).reshape(sources, EXTRA_ROWS, LANES)


def part_specs(sources, steps, shapes):
    maps = (lambda i: (jnp.minimum(i, steps - 1), 0, 0), lambda i: (jnp.maximum(i - steps, 0), 0, 0))
    return [pl.BlockSpec((sources, *shape), place) for shape in shapes for place in maps]


def in_halves(steps, first, second):
    pl.when(pl.program_id(0) < steps)(first)
    pl.when(pl.program_id(0) >= steps)(second)


def whole(array):
    rank = len(array.shape)
    return pl.BlockSpec(array.shape, lambda i: (0,) * rank, pipeline_mode=pl.Buffered(1))


def expert_rows(h_rows, cot_rows, first_weight, second_weight, half):
    experts, rows_sent, _ = h_rows[0].shape
    width, hidden_width = first_weight.shape
    sources = min(experts, 256 // half)
    steps, total = experts // sources, 2 * experts * half

    def kernel(h_a, h_b, cot_a, cot_b, first_ref, second_ref, back_a, back_b):
        in_halves(
            steps,
            lambda: expert_step(half, h_a, cot_a, first_ref, second_ref, back_a),
            lambda: expert_step(half, h_b, cot_b, first_ref, second_ref, back_b),
        )

    return pl.pallas_call(
        kernel,
        grid=(2 * steps,),
        out_shape=[near_shape(h_rows[0].shape, LOW)] * 2,
        in_specs=part_specs(sources, steps, [(rows_sent, LANES), (half, width)])
        + [whole(first_weight), whole(second_weight)],
        out_specs=part_specs(sources, steps, [(rows_sent, LANES)]),
        compiler_params=pltpu.CompilerParams(vmem_limit_bytes=16 * MIB),
        cost_estimate=pl.CostEstimate(
            flops=6 * total * width * hidden_width,
            bytes_accessed=8 * total * width,
            transcendentals=total * hidden_width,
        ),
    )(*h_rows, *cot_rows, far(first_weight), far(second_weight))


def expert_weights(h_rows, cot_rows, first_weight, second_weight, sums, half):
    experts, rows_sent, _ = h_rows[0].shape
    hidden_width, width = second_weight.shape
    sources = min(experts, 256 // half)
    steps, total = experts // sources, 2 * experts * half

    def kernel(h_a, h_b, cot_a, cot_b, first_ref, second_ref, *refs):
        out_a, out_b, grad_first, grad_second = refs[-4:]

        @pl.when(pl.program_id(0) == 0)
        def _():
            for at, grad in enumerate((grad_first, grad_second)):
                grad[...] = refs[at][...] if sums else jnp.zeros(grad.shape, FULL)

        def step(h_ref, cot_ref, out_ref):
            incoming, gate, arrived, hidden, _, grad_pre = expert_core(
                half, h_ref, cot_ref, first_ref, second_ref
            )
            produced = dot(hidden, second_ref[...])
            out_ref[...] = (gate * produced).astype(LOW).reshape(out_ref.shape)
            grad_first[...] += contract_rows(incoming, grad_pre)
            grad_second[...] += contract_rows(hidden, arrived)

        in_halves(steps, lambda: step(h_a, cot_a, out_a), lambda: step(h_b, cot_b, out_b))

    grads = [far_shape((width, hidden_width), FULL), far_shape((hidden_width, width), FULL)]
    return pl.pallas_call(
        kernel,
        grid=(2 * steps,),
        out_shape=[near_shape((experts, half, width), LOW)] * 2 + grads,
        in_specs=part_specs(sources, steps, [(rows_sent, LANES), (half, width)])
        + [whole(x) for x in (first_weight, second_weight, *sums)],
        out_specs=part_specs(sources, steps, [(half, width)]) + [whole(x) for x in grads],
        compiler_params=pltpu.CompilerParams(vmem_limit_bytes=28 * MIB),
        cost_estimate=pl.CostEstimate(
            flops=10 * total * width * hidden_width,
            bytes_accessed=10 * total * width,
            transcendentals=total * hidden_width,
        ),
    )(*h_rows, *cot_rows, *map(far, (first_weight, second_weight, *sums)))


def combine_kernel(base_ref, back_ref, slot_ref, col_ref, gates_ref, ext_ref, h_ref, part_ref, router_ref):
    experts, rows_sent, _ = back_ref.shape
    blocks = h_ref.shape[1] // LANES
    half = (rows_sent - EXTRA_ROWS) // blocks
    count = experts * half
    slot_row = slot_ref[...]
    hits = slot_row >= 0
    here, of_expert = slot_tables(slot_row, base_ref[0], half)
    extra = back_ref[:, blocks * half :, :].reshape(experts * EXTRA_ROWS, LANES)
    reach = EXTRA_ROWS
    shift, reach_shift = half.bit_length() - 1, reach.bit_length() - 1
    row = iota((count, experts * reach), 1)
    wanted = (row >> reach_shift) == (iota((count, experts * reach), 0) >> shift)
    wanted = wanted & ((row & (EXTRA_ROWS - 1)) < 2)
    on_lane = iota((count, LANES), 1) == (iota((count, LANES), 0) & (half - 1))
    lanes = dot(wanted.astype(LOW), extra)
    slot_gated = jnp.sum(jnp.where(on_lane, lanes, 0.0), axis=1, keepdims=True)
    high, low = split_low(jnp.where(here, slot_gated, 0.0))
    gated = contract_rows(of_expert.astype(LOW), high) + contract_rows(of_expert.astype(LOW), low)
    gated = jnp.where(hits, gated, 0.0)
    logit_grad = gated - gates_ref[...] * jnp.sum(gated, axis=0, keepdims=True)
    logit_grad = jnp.where(hits, logit_grad, 0.0)
    high, low = split_low(logit_grad)
    router_ref[...] = dot(high, h_ref[...]) + dot(low, h_ref[...])
    router_rows = ext_ref[2 : 2 + experts, :].astype(LOW)
    expand = (iota((experts, count), 1) >> shift) == iota((experts, count), 0)
    wanted = (iota((1, count), 1) & (half - 1)) + base_ref[0]
    one_hot = (dot(col_ref[...], expand.astype(LOW)) == wanted.astype(FULL)).astype(LOW)
    for block in range(blocks):
        rows = back_ref[:, block * half : (block + 1) * half, :].reshape(count, LANES)
        at = slice(block * LANES, (block + 1) * LANES)
        part_ref[:, at] = (
            dot(one_hot, rows)
            + contract_rows(high, router_rows[:, at])
            + contract_rows(low, router_rows[:, at])
        )


def backward_kernel(
    part_ref, other_ref, cot_ref, resid_ref, rows_ref, ext_ref, qk_ref, vx_ref, h_ref, qkv_ref, probs_ref,
    mixed_ref, router_ref, qk_out, vx_out, one_ref, rgrad_ref, qkg_ref, vg_ref,
):
    group_rows = rows_ref.shape[0]
    inner = qk_ref.shape[1] // 2
    h_grad = part_ref[...] + other_ref[...]
    residual = resid_ref[...]
    inv_two = inverse_rms(residual)
    normed_two = residual * inv_two
    gain_two_row = 0.5 * jnp.sum(h_grad * normed_two, axis=0, keepdims=True)
    scaled = h_grad * ext_ref[1:2, :]
    resid_grad = cot_ref[...] + inv_two * (
        scaled - normed_two * jnp.mean(scaled * normed_two, axis=1, keepdims=True)
    )
    rgrad_ref[...] = resid_grad
    attn_grad = resid_grad.astype(LOW)
    vx_out[:, inner : 2 * inner] = contract_rows(attn_grad, mixed_ref[...]).astype(LOW)
    mixed_grad = dot(attn_grad, vx_ref[:, inner : 2 * inner]).astype(LOW)
    low_lanes = iota((group_rows, LANES), 1) < HEAD_DIM
    for pair in range(inner // LANES):
        at = pair * LANES
        queries = qkv_ref[:, at : at + LANES]
        key_rows = qkv_ref[:, inner + at : inner + at + LANES]
        value_rows = qkv_ref[:, 2 * inner + at : 2 * inner + at + LANES]
        out_grad = mixed_grad[:, at : at + LANES]
        grads = []
        for sub in range(2):
            own = low_lanes if sub == 0 else ~low_lanes
            probs = probs_ref[2 * pair + sub]
            prob_grad = contract_cols(jnp.where(own, out_grad, jnp.zeros_like(out_grad)), value_rows)
            carry = jnp.sum(prob_grad * probs, axis=1, keepdims=True)
            score_grad = (probs * (prob_grad - carry)).astype(LOW)
            grads.append(
                (
                    dot(score_grad, key_rows),
                    contract_rows(score_grad, queries),
                    contract_rows(probs.astype(LOW), out_grad),
                )
            )
        scale = HEAD_DIM ** (-0.5)
        qkg_ref[:, at : at + LANES] = (jnp.where(low_lanes, grads[0][0], grads[1][0]) * scale).astype(LOW)
        qkg_ref[:, inner + at : inner + at + LANES] = (
            jnp.where(low_lanes, grads[0][1], grads[1][1]) * scale
        ).astype(LOW)
        vg_ref[:, at : at + LANES] = jnp.where(low_lanes, grads[0][2], grads[1][2]).astype(LOW)
    h_one = h_ref[...]
    qk_out[...] = contract_rows(h_one, qkg_ref[...]).astype(LOW)
    vx_out[:, :inner] = contract_rows(h_one, vg_ref[...]).astype(LOW)
    one_grad = contract_cols(qkg_ref[...], qk_ref[...]) + contract_cols(vg_ref[...], vx_ref[:, :inner])
    one_ref[...] = one_grad
    rows = rows_ref[...]
    gain_one_row = jnp.sum(one_grad * (rows * inverse_rms(rows)), axis=0, keepdims=True)
    router_rows = router_ref[...]
    sub = iota(router_rows.shape, 0)
    extra = jnp.where(sub == 0, gain_one_row, jnp.where(sub == 1, gain_two_row, router_rows))
    vx_out[:, 2 * inner :] = extra.T.astype(LOW)


def local(
    block_in,
    seq_lengths,
    routes,
    w_query,
    w_key,
    w_value,
    w_out_proj,
    router,
    gain_attn,
    gain_moe,
    expert_in,
    expert_out,
    cotangent,
):
    dp_count = lax.axis_size("dp")
    core = lax.axis_index("tensor")
    tok_rows, width = block_in.shape
    group_rows, top_count = routes.shape
    experts = router.shape[1]
    half = max(EXTRA_ROWS, top_count * group_rows // experts)
    slots = experts * half
    rows_sent = half * (width // LANES) + EXTRA_ROWS
    inner = w_query.shape[1]
    bits = dp_count.bit_length() - 1
    order_a, order_b = bit_orders()

    expert_ids = jnp.arange(experts, dtype=jnp.int32)
    hits = jnp.any(routes[:, :, None] == expert_ids[None, None, :], axis=1)
    places = jnp.arange(group_rows, dtype=jnp.int32)
    earlier = (places[:, None] > places[None, :]).astype(LOW)
    slot_col = jnp.where(hits, dot(earlier, hits.astype(LOW)), -1.0).astype(LOW)
    slot_row = slot_col.T
    base = core * half
    slot_ids = (base + jnp.arange(half, dtype=jnp.int32)).astype(LOW)
    in_slot = slot_row[:, None, :] == slot_ids[None, :, None]
    dispatch = in_slot.astype(LOW).reshape(slots, group_rows)
    base = base.reshape(1).astype(jnp.int32)

    extra_width = -(-(2 + experts) // LANES) * LANES
    extra = jnp.concatenate(
        [
            gain_attn[:, None],
            gain_moe[:, None],
            router,
            jnp.zeros((router.shape[0], extra_width - 2 - experts), LOW),
        ],
        axis=1,
    )
    shard = jnp.concatenate([w_query, w_key, w_value, w_out_proj.T, extra], axis=1)
    lines = [[low + 4 * high for high in range(dp_count // 4)] for low in range(4)]
    line = lax.all_gather(shard, "dp", axis=0, tiled=True, axis_index_groups=lines)
    line = line.reshape((2,) * (bits - 2) + (1, 1) + shard.shape)
    qk_full, vx_full = line[..., : 2 * inner], line[..., 2 * inner :]
    for step in range(bits - 2, bits):
        vx_full = double(vx_full, order_b[step], bits)
        qk_full = double(qk_full, order_a[step], bits)
        if step == bits - 2:
            cot_low = after(cotangent, vx_full).astype(LOW)
    cot_own = trade(dot(dispatch, cot_low).astype(LOW).reshape(experts, half, width))
    rows_all = lax.all_gather(block_in, "tensor", axis=0, tiled=True)
    qk_full = qk_full.reshape(width, 2 * inner)
    vx_full = vx_full.reshape(width, 2 * inner + extra_width)

    attn_part, ext, h_one, qkv, probs, mixed, rows_far, qk_far, vx_far = call(
        attention_kernel,
        [
            near_shape((group_rows, width), FULL),
            near_shape((extra_width, width), FULL),
            far_shape((group_rows, width), LOW),
            far_shape((group_rows, 3 * inner), LOW),
            far_shape((inner // HEAD_DIM, group_rows, group_rows), FULL),
            far_shape((group_rows, inner), LOW),
            far_shape(rows_all.shape, FULL),
            far_shape(qk_full.shape, LOW),
            far_shape(vx_full.shape, LOW),
        ],
        seq_lengths,
        rows_all,
        qk_full,
        vx_full,
        limit=14,
        flops=8 * group_rows * width * inner + 4 * group_rows * group_rows * inner,
        smem=(0,),
    )
    residual, h_two, gates, sent = call(
        dispatch_kernel,
        [
            far_shape((group_rows, width), FULL),
            far_shape((group_rows, width), LOW),
            near_shape((experts, group_rows), FULL),
            near_shape((experts, rows_sent, LANES), LOW),
        ],
        base,
        rows_all,
        attn_part,
        swap(attn_part),
        ext,
        slot_row,
        flops=2 * experts * half * group_rows * width,
        smem=(0,),
    )

    cot_crossed = cross(cot_own)
    cot_own = (cot_own, swap(cot_own))
    cot_far = (cot_crossed, swap(cot_crossed))
    h_own = trade(sent)
    h_crossed = cross(after(h_own, cot_crossed))
    h_own = (after(h_own, cot_far[1]), swap(h_own))
    first_weight = expert_in[0]
    second_weight = expert_out[0]
    own_back, own_given = expert_rows(h_own, cot_own, first_weight, second_weight, half)
    h_crossed = after(h_crossed, own_back)
    h_far = (h_crossed, swap(h_crossed))
    far_back, far_given = expert_rows(h_far, cot_far, first_weight, second_weight, half)
    far_sum = add_low(far_back, swap(far_given))
    far_total = cross(far_sum)
    held = after(first_weight, far_sum)
    far_out, far_given, *sums = expert_weights(h_far, cot_far, held, second_weight, (), half)
    back_sum = after(add_low(own_back, swap(own_given), far_total), far_out)
    back = trade(back_sum)
    out_far = add_low(far_out, swap(far_given))
    held = after(first_weight, out_far, back_sum)
    own_out, out_given, grad_first, grad_second = expert_weights(
        h_own, cot_own, held, second_weight, sums, half
    )
    out_far = cross(after(out_far, far_total))
    out_given = swap(out_given)
    back_out = trade(add_low(own_out, out_given, out_far)).reshape(slots, width)

    h_part, router_part = call(
        combine_kernel,
        [near_shape((group_rows, width), FULL), near_shape((experts, width), FULL)],
        base,
        after(back, own_out, out_far),
        slot_row,
        slot_col,
        gates,
        ext,
        far(h_two),
        flops=2 * slots * group_rows * width,
        smem=(0,),
    )
    router_part = jnp.pad(router_part, ((2, extra_width - 2 - experts), (0, 0)))
    qk_part, vx_part, one_part, resid_grad, _, _ = call(
        backward_kernel,
        [
            near_shape((width, 2 * inner), LOW),
            near_shape((width, 2 * inner + extra_width), LOW),
            near_shape((group_rows, width), FULL),
            near_shape((group_rows, width), FULL),
            near_shape((group_rows, 2 * inner), LOW),
            near_shape((group_rows, inner), LOW),
        ],
        h_part,
        swap(h_part),
        *map(far, (cotangent, residual, rows_far)),
        ext,
        *map(far, (qk_far, vx_far, h_one, qkv, probs, mixed)),
        router_part,
        limit=14,
        flops=20 * group_rows * width * inner + 12 * group_rows * group_rows * inner,
    )

    own_start = core * tok_rows
    other_start = (1 - core) * tok_rows

    def rows_at(values, start):
        return lax.dynamic_slice_in_dim(values, start, tok_rows, 0)

    one_other = swap(rows_at(one_part, other_start).astype(LOW)).astype(FULL)
    qk_sum = qk_part.reshape((2,) * bits + (width // dp_count, 2 * inner))
    vx_sum = vx_part.reshape((2,) * bits + (width // dp_count, 2 * inner + extra_width))
    for step in range(bits):
        vx_sum = halve(vx_sum, order_b[bits - 1 - step], bits)
        qk_sum = halve(qk_sum, order_a[bits - 1 - step], bits)
        if step == 1:
            back_out = after(back_out, vx_sum, qk_sum)
    qk_sum = qk_sum.reshape(width // dp_count, 2 * inner)
    vx_sum = vx_sum.reshape(width // dp_count, 2 * inner + extra_width)

    out_part = contract_rows(dispatch, back_out)
    block_out = rows_at(residual, own_start) + (
        rows_at(out_part, own_start) + swap(rows_at(out_part, other_start))
    )
    scaled_one = (rows_at(one_part, own_start) + one_other) * ext[0:1, :]
    inv_own = inverse_rms(block_in)
    normed_own = block_in * inv_own
    grad_in = rows_at(resid_grad, own_start) + inv_own * (
        scaled_one - normed_own * jnp.mean(scaled_one * normed_own, axis=1, keepdims=True)
    )
    extra_sum = vx_sum[:, 2 * inner :]
    extra_sum = extra_sum + swap(extra_sum)
    share = extra_sum.shape[0] // 2
    extra_own = lax.dynamic_slice_in_dim(extra_sum, core * share, share, 0)
    return (
        block_out,
        grad_in,
        qk_sum[:, :inner],
        qk_sum[:, inner:],
        vx_sum[:, :inner],
        vx_sum[:, inner : 2 * inner].T,
        extra_own[:, 2 : 2 + experts],
        extra_own[:, 0],
        extra_own[:, 1],
        grad_first[None],
        grad_second[None],
    )


def solution(mesh):
    in_specs = (
        P(("dp", "tensor"), None),
        P("dp", None),
        P("dp", None),
        P("dp", "tensor"),
        P("dp", "tensor"),
        P("dp", "tensor"),
        P("tensor", "dp"),
        P("dp", None),
        P("dp"),
        P("dp"),
        P("dp", None, "tensor"),
        P("dp", "tensor", None),
        P("dp", None),
    )
    out_specs = (
        P(("dp", "tensor"), None),
        P(("dp", "tensor"), None),
        P("dp", "tensor"),
        P("dp", "tensor"),
        P("dp", "tensor"),
        P("tensor", "dp"),
        P(("dp", "tensor"), None),
        P(("dp", "tensor")),
        P(("dp", "tensor")),
        P("dp", None, "tensor"),
        P("dp", "tensor", None),
    )
    return jax.shard_map(local, mesh=mesh, in_specs=in_specs, out_specs=out_specs, check_vma=False)
```

```python
import math

import jax
import jax.numpy as jnp
from jax import lax
from jax.experimental import pallas as pl
from jax.experimental.pallas import tpu as pltpu
from jax.sharding import PartitionSpec as P

HEAD_DIM = 64
LANES = 128


EPSILON = 1e-06
NEGATIVE = -1e30
MIB = 1024 * 1024
EXTRA_ROWS = 16
LOW = jnp.bfloat16
FULL = jnp.float32


def dot(left_side, right_side):
    return jnp.dot(left_side, right_side, preferred_element_type=FULL)


def contract_rows(left_side, right_side):
    return lax.dot_general(
        left_side, right_side, (((0,), (0,)), ((), ())), preferred_element_type=FULL
    )


def contract_cols(left_side, right_side):
    return lax.dot_general(
        left_side, right_side, (((1,), (1,)), ((), ())), preferred_element_type=FULL
    )


def split_low(values):
    high = values.astype(LOW)
    return high, (values - high.astype(FULL)).astype(LOW)


def iota(shape, axis):
    return lax.broadcasted_iota(jnp.int32, shape, axis)


def swap(values):
    return lax.ppermute(values, "tensor", [(0, 1), (1, 0)])


def bit_orders():
    bits = lax.axis_size("dp").bit_length() - 1
    falling = list(range(bits - 1, -1, -1))
    return falling, falling[:-2] + [falling[-1], falling[-2]]


def partners(bit):
    return [(i, i ^ (1 << bit)) for i in range(lax.axis_size("dp"))]


def double(block, bit, bits):
    other = lax.ppermute(block, "dp", partners(bit))
    axis = bits - 1 - bit
    upper = ((lax.axis_index("dp") >> bit) & 1) == 1
    return jnp.where(
        upper,
        jnp.concatenate([other, block], axis=axis),
        jnp.concatenate([block, other], axis=axis),
    )


def halve(block, bit, bits):
    axis, place = bits - 1 - bit, (lax.axis_index("dp") >> bit) & 1
    given = lax.dynamic_index_in_dim(block, 1 - place, axis, keepdims=True).astype(LOW)
    kept = lax.dynamic_index_in_dim(block, place, axis, keepdims=True)
    return kept.astype(FULL) + lax.ppermute(given, "dp", partners(bit)).astype(FULL)


def trade(values):
    experts, dp_count = values.shape[0], lax.axis_size("dp")
    owners = dp_count // experts
    groups = [[owners * e + o for e in range(experts)] for o in range(owners)]
    return lax.all_to_all(
        values, "dp", split_axis=0, concat_axis=0, tiled=True, axis_index_groups=groups
    )


def cross(values):
    return lax.ppermute(values, "dp", partners(0))


def after(values, *others):
    return lax.optimization_barrier((values, *others))[0]


def add_low(*parts):
    return sum(part.astype(FULL) for part in parts).astype(LOW)


def far(values):
    return pltpu.with_memory_space_constraint(values, pltpu.HBM)


def near_shape(shape, kind):
    return jax.ShapeDtypeStruct(shape, kind)


def far_shape(shape, kind):
    return pltpu.HBM(shape, kind)


def call(kernel, out_shape, *operands, flops=0, smem=(), limit=8):
    moved = sum(x.size * x.dtype.itemsize for x in operands)
    return pl.pallas_call(
        kernel,
        out_shape=out_shape,
        in_specs=[
            pl.BlockSpec(memory_space=pltpu.SMEM if i in smem else pltpu.VMEM)
            for i in range(len(operands))
        ],
        out_specs=[pl.BlockSpec(memory_space=pltpu.VMEM) for _ in out_shape],
        compiler_params=pltpu.CompilerParams(vmem_limit_bytes=limit * MIB),
        cost_estimate=pl.CostEstimate(flops=flops, bytes_accessed=2 * moved, transcendentals=0),
    )(*operands)


def inverse_rms(rows):
    return lax.rsqrt(jnp.mean(rows * rows, axis=1, keepdims=True) + EPSILON)


GELU_SCALE = math.sqrt(2.0 / math.pi)
GELU_CUBE = 0.044715


def attention_kernel(
    len_ref, rows_ref, qk_ref, vx_ref, attn_ref, ext_ref, h_ref, qkv_ref, probs_ref, mixed_ref, rows_out, qk_out, vx_out
):
    group_rows = rows_ref.shape[0]
    inner = vx_ref.shape[1] // 2
    rows = rows_ref[...]
    rows_out[...] = rows
    qk_out[...] = qk_ref[...]
    vx_out[...] = vx_ref[...]
    ext = qk_ref[:, 2 * inner :].astype(FULL).T
    ext_ref[...] = ext
    h_one = (rows * inverse_rms(rows) * ext[0:1, :]).astype(LOW)
    h_ref[...] = h_one
    qkv_ref[:, : 2 * inner] = dot(h_one, qk_ref[:, : 2 * inner]).astype(LOW)
    qkv_ref[:, 2 * inner :] = dot(h_one, vx_ref[:, :inner]).astype(LOW)
    down, across = iota((group_rows, group_rows), 0), iota((group_rows, group_rows), 1)
    allowed = down >= across
    end = jnp.int32(0)
    for place in range(len_ref.shape[1]):
        end = end + len_ref[0, place]
        allowed = allowed & ((down >= end) == (across >= end))
    low_lanes = iota((group_rows, LANES), 1) < HEAD_DIM
    for pair in range(inner // LANES):
        at = pair * LANES
        queries = qkv_ref[:, at : at + LANES]
        key_rows = qkv_ref[:, inner + at : inner + at + LANES]
        value_rows = qkv_ref[:, 2 * inner + at : 2 * inner + at + LANES]
        outs = []
        for sub in range(2):
            own = low_lanes if sub == 0 else ~low_lanes
            scores = contract_cols(jnp.where(own, queries, jnp.zeros_like(queries)), key_rows)
            scores = jnp.where(allowed, scores * HEAD_DIM ** (-0.5), NEGATIVE)
            terms = jnp.exp(scores - jnp.max(scores, axis=1, keepdims=True))
            probs = terms / jnp.sum(terms, axis=1, keepdims=True)
            probs_ref[2 * pair + sub] = probs
            outs.append(dot(probs.astype(LOW), value_rows))
        mixed_ref[:, at : at + LANES] = jnp.where(low_lanes, outs[0], outs[1]).astype(LOW)
    attn_ref[...] = contract_cols(mixed_ref[...], vx_ref[:, inner:])


def slot_tables(slot_row, base, half):
    experts, group_rows = slot_row.shape
    count, shift = experts * half, half.bit_length() - 1
    of_expert = (iota((count, experts), 0) >> shift) == iota((count, experts), 1)
    wanted = (iota((count, 1), 0) & (half - 1)) + base
    here = dot(of_expert.astype(LOW), slot_row) == wanted.astype(FULL)
    return here, of_expert


def dispatch_kernel(
    base_ref, rows_ref, attn_ref, other_ref, ext_ref, slot_ref, resid_ref, h_ref, gates_ref, send_ref
):
    experts, rows_sent, _ = send_ref.shape
    blocks = rows_ref.shape[1] // LANES
    half = (rows_sent - EXTRA_ROWS) // blocks
    count = experts * half
    residual = rows_ref[...] + (attn_ref[...] + other_ref[...])
    resid_ref[...] = residual
    h_two = (residual * inverse_rms(residual) * ext_ref[1:2, :]).astype(LOW)
    h_ref[...] = h_two
    slot_row = slot_ref[...]
    hits = slot_row >= 0
    all_logits = contract_cols(ext_ref[...].astype(LOW), h_two)
    logits = all_logits[2 : 2 + experts, :]
    peak = jnp.max(jnp.where(hits, logits, NEGATIVE), axis=0, keepdims=True)
    terms = jnp.where(hits, jnp.exp(jnp.where(hits, logits - peak, 0.0)), 0.0)
    gates = terms / jnp.sum(terms, axis=0, keepdims=True)
    gates_ref[...] = gates
    here, of_expert = slot_tables(slot_row, base_ref[0], half)
    one_hot = here.astype(LOW)
    picked = dot(one_hot, h_two).astype(LOW).reshape(experts, half, blocks * LANES)
    high, low = split_low(gates)
    by_expert = contract_cols(one_hot, high) + contract_cols(one_hot, low)
    gate_col = jnp.sum(jnp.where(of_expert, by_expert, 0.0), axis=1, keepdims=True)
    on_lane = iota((count, LANES), 1) == (iota((count, LANES), 0) & (half - 1))
    high_rows, low_rows = [
        contract_rows(of_expert.astype(LOW), jnp.where(on_lane, part.astype(FULL), 0.0).astype(LOW))
        for part in split_low(gate_col)
    ]
    sub = iota((EXTRA_ROWS, LANES), 0)
    for block in range(blocks):
        send_ref[:, block * half : (block + 1) * half, :] = picked[
            :, :, block * LANES : (block + 1) * LANES
        ]
    for expert in range(experts):
        send_ref[expert, blocks * half :, :] = jnp.where(
            sub == 0,
            high_rows[expert : expert + 1, :],
            jnp.where(sub == 1, low_rows[expert : expert + 1, :], 0.0),
        ).astype(LOW)


def rows_of(ref, half):
    blocks = (ref.shape[1] - EXTRA_ROWS) // half
    return jnp.concatenate(
        [
            ref[:, at * half : (at + 1) * half, :].reshape(ref.shape[0] * half, LANES)
            for at in range(blocks)
        ],
        axis=1,
    )


def gated_cot(gate, cot_ref):
    sources, half, width = cot_ref.shape
    return (gate * cot_ref[...].reshape(sources * half, width).astype(FULL)).astype(LOW)


def expert_step(half, h_ref, cot_ref, first_ref, second_ref, back_ref, hid_ref, pre_ref, gate_ref):
    sources = h_ref.shape[0]
    blocks = (h_ref.shape[1] - EXTRA_ROWS) // half
    count, shift = sources * half, half.bit_length() - 1
    extra = h_ref[:, blocks * half :, :].reshape(sources * EXTRA_ROWS, LANES)
    source = iota((count, sources * EXTRA_ROWS), 0) >> shift
    row = iota((count, sources * EXTRA_ROWS), 1)
    two_rows = (row == source * EXTRA_ROWS) | (row == source * EXTRA_ROWS + 1)
    on_lane = iota((count, LANES), 1) == (iota((count, LANES), 0) & (half - 1))
    gate_lanes = dot(two_rows.astype(LOW), extra)
    gate = jnp.sum(jnp.where(on_lane, gate_lanes, 0.0), axis=1, keepdims=True)
    gate_ref[...] = jnp.broadcast_to(gate, (count, LANES))
    arrived = gated_cot(gate, cot_ref)
    incoming = rows_of(h_ref, half)
    pre = dot(incoming, first_ref[...])
    grad_hidden = contract_cols(arrived, second_ref[...])
    square = pre * pre
    bend = jnp.tanh(GELU_SCALE * pre * (1.0 + GELU_CUBE * square))
    rise = 0.5 * (1.0 + bend)
    hidden = (pre * rise).astype(LOW)
    hid_ref[...] = hidden
    slope = rise + (0.5 * GELU_SCALE) * pre * (1.0 - bend * bend) * (1.0 + 3.0 * GELU_CUBE * square)
    gated = jnp.sum(hidden.astype(FULL) * grad_hidden, axis=1, keepdims=True)
    grad_pre = (grad_hidden * slope).astype(LOW)
    pre_ref[...] = grad_pre
    grad_rows = contract_cols(grad_pre, first_ref[...]).astype(LOW).reshape(sources, half, blocks * LANES)
    for block in range(blocks):
        back_ref[:, block * half : (block + 1) * half, :] = grad_rows[
            :, :, block * LANES : (block + 1) * LANES
        ]
    source = iota((sources * EXTRA_ROWS, count), 1) >> shift
    row = iota((sources * EXTRA_ROWS, count), 0)
    high, low = [
        jnp.where(on_lane, part.astype(FULL), 0.0).astype(LOW) for part in split_low(gated)
    ]
    rows_back = dot((row == source * EXTRA_ROWS).astype(LOW), high) + dot(
        (row == source * EXTRA_ROWS + 1).astype(LOW), low
    )
    back_ref[:, blocks * half :, :] = rows_back.astype(LOW).reshape(sources, EXTRA_ROWS, LANES)


def part_specs(sources, steps, shapes):
    maps = (lambda i: (jnp.minimum(i, steps - 1), 0, 0), lambda i: (jnp.maximum(i - steps, 0), 0, 0))
    return [pl.BlockSpec((sources, *shape), place) for shape in shapes for place in maps]


def in_halves(steps, first, second):
    pl.when(pl.program_id(0) < steps)(first)
    pl.when(pl.program_id(0) >= steps)(second)


def whole(array):
    rank = len(array.shape)
    return pl.BlockSpec(array.shape, lambda i: (0,) * rank, pipeline_mode=pl.Buffered(1))


def expert_rows(h_rows, cot_rows, first_weight, second_weight, half):
    experts, rows_sent, _ = h_rows[0].shape
    width, hidden_width = first_weight.shape
    sources = min(experts, 256 // half)
    count, steps = sources * half, experts // sources
    total = 2 * experts * half

    def kernel(h_a, h_b, cot_a, cot_b, first_ref, second_ref, back_a, back_b, *kept):
        in_halves(
            steps,
            lambda: expert_step(half, h_a, cot_a, first_ref, second_ref, back_a, *kept),
            lambda: expert_step(half, h_b, cot_b, first_ref, second_ref, back_b, *kept),
        )

    lanes = ((hidden_width, LOW), (hidden_width, LOW), (LANES, FULL))
    back_a, back_b, *kept = pl.pallas_call(
        kernel,
        grid=(2 * steps,),
        out_shape=[near_shape(h_rows[0].shape, LOW)] * 2
        + [far_shape((total, n), kind) for n, kind in lanes],
        in_specs=part_specs(sources, steps, [(rows_sent, LANES), (half, width)])
        + [whole(first_weight), whole(second_weight)],
        out_specs=part_specs(sources, steps, [(rows_sent, LANES)])
        + [pl.BlockSpec((count, n), lambda i: (i, 0)) for n, _ in lanes],
        compiler_params=pltpu.CompilerParams(vmem_limit_bytes=16 * MIB),
        cost_estimate=pl.CostEstimate(
            flops=6 * total * width * hidden_width,
            bytes_accessed=12 * total * width,
            transcendentals=total * hidden_width,
        ),
    )(*h_rows, *cot_rows, far(first_weight), far(second_weight))
    return back_a, back_b, kept


def expert_weights(h_rows, cot_rows, kept, second_weight, sums, half):
    experts, rows_sent, _ = h_rows[0].shape
    hidden_width, width = second_weight.shape
    sources = min(experts, 256 // half)
    count, steps = sources * half, experts // sources
    total = 2 * experts * half

    def kernel(h_a, h_b, cot_a, cot_b, hid_ref, pre_ref, gate_ref, second_ref, *refs):
        out_a, out_b, grad_first, grad_second = refs[-4:]

        @pl.when(pl.program_id(0) == 0)
        def _():
            for at, grad in enumerate((grad_first, grad_second)):
                grad[...] = refs[at][...] if sums else jnp.zeros(grad.shape, FULL)

        def step(h_ref, cot_ref, out_ref):
            hidden, gate = hid_ref[...], gate_ref[:, 0:1]
            produced = dot(hidden, second_ref[...])
            out_ref[...] = (gate * produced).astype(LOW).reshape(out_ref.shape)
            grad_first[...] += contract_rows(rows_of(h_ref, half), pre_ref[...])
            grad_second[...] += contract_rows(hidden, gated_cot(gate, cot_ref))

        in_halves(steps, lambda: step(h_a, cot_a, out_a), lambda: step(h_b, cot_b, out_b))

    grads = [far_shape((width, hidden_width), FULL), far_shape((hidden_width, width), FULL)]
    return pl.pallas_call(
        kernel,
        grid=(2 * steps,),
        out_shape=[near_shape((experts, half, width), LOW)] * 2 + grads,
        in_specs=part_specs(sources, steps, [(rows_sent, LANES), (half, width)])
        + [pl.BlockSpec((count, x.shape[1]), lambda i: (i, 0)) for x in kept]
        + [whole(x) for x in (second_weight, *sums)],
        out_specs=part_specs(sources, steps, [(half, width)]) + [whole(x) for x in grads],
        compiler_params=pltpu.CompilerParams(vmem_limit_bytes=24 * MIB),
        cost_estimate=pl.CostEstimate(
            flops=6 * total * width * hidden_width,
            bytes_accessed=10 * total * width,
            transcendentals=0,
        ),
    )(*h_rows, *cot_rows, *map(far, (*kept, second_weight, *sums)))


def combine_kernel(base_ref, back_ref, slot_ref, col_ref, gates_ref, ext_ref, h_ref, part_ref, router_ref):
    experts, rows_sent, _ = back_ref.shape
    blocks = h_ref.shape[1] // LANES
    half = (rows_sent - EXTRA_ROWS) // blocks
    count = experts * half
    slot_row = slot_ref[...]
    hits = slot_row >= 0
    here, of_expert = slot_tables(slot_row, base_ref[0], half)
    extra = back_ref[:, blocks * half :, :].reshape(experts * EXTRA_ROWS, LANES)
    reach = EXTRA_ROWS
    shift, reach_shift = half.bit_length() - 1, reach.bit_length() - 1
    row = iota((count, experts * reach), 1)
    wanted = (row >> reach_shift) == (iota((count, experts * reach), 0) >> shift)
    wanted = wanted & ((row & (EXTRA_ROWS - 1)) < 2)
    on_lane = iota((count, LANES), 1) == (iota((count, LANES), 0) & (half - 1))
    lanes = dot(wanted.astype(LOW), extra)
    slot_gated = jnp.sum(jnp.where(on_lane, lanes, 0.0), axis=1, keepdims=True)
    high, low = split_low(jnp.where(here, slot_gated, 0.0))
    gated = contract_rows(of_expert.astype(LOW), high) + contract_rows(of_expert.astype(LOW), low)
    gated = jnp.where(hits, gated, 0.0)
    logit_grad = gated - gates_ref[...] * jnp.sum(gated, axis=0, keepdims=True)
    logit_grad = jnp.where(hits, logit_grad, 0.0)
    high, low = split_low(logit_grad)
    router_ref[...] = dot(high, h_ref[...]) + dot(low, h_ref[...])
    router_rows = ext_ref[2 : 2 + experts, :].astype(LOW)
    expand = (iota((experts, count), 1) >> shift) == iota((experts, count), 0)
    wanted = (iota((1, count), 1) & (half - 1)) + base_ref[0]
    one_hot = (dot(col_ref[...], expand.astype(LOW)) == wanted.astype(FULL)).astype(LOW)
    for block in range(blocks):
        rows = back_ref[:, block * half : (block + 1) * half, :].reshape(count, LANES)
        at = slice(block * LANES, (block + 1) * LANES)
        part_ref[:, at] = (
            dot(one_hot, rows)
            + contract_rows(high, router_rows[:, at])
            + contract_rows(low, router_rows[:, at])
        )


def backward_kernel(
    part_ref, other_ref, cot_ref, resid_ref, rows_ref, ext_ref, qk_ref, vx_ref, h_ref, qkv_ref, probs_ref,
    mixed_ref, router_ref, qk_out, vx_out, one_ref, rgrad_ref, qkg_ref, vg_ref,
):
    group_rows = rows_ref.shape[0]
    inner = vx_ref.shape[1] // 2
    h_grad = part_ref[...] + other_ref[...]
    residual = resid_ref[...]
    inv_two = inverse_rms(residual)
    normed_two = residual * inv_two
    gain_two_row = 0.5 * jnp.sum(h_grad * normed_two, axis=0, keepdims=True)
    scaled = h_grad * ext_ref[1:2, :]
    resid_grad = cot_ref[...] + inv_two * (
        scaled - normed_two * jnp.mean(scaled * normed_two, axis=1, keepdims=True)
    )
    rgrad_ref[...] = resid_grad
    attn_grad = resid_grad.astype(LOW)
    vx_out[:, inner:] = contract_rows(attn_grad, mixed_ref[...]).astype(LOW)
    mixed_grad = dot(attn_grad, vx_ref[:, inner:]).astype(LOW)
    low_lanes = iota((group_rows, LANES), 1) < HEAD_DIM
    for pair in range(inner // LANES):
        at = pair * LANES
        queries = qkv_ref[:, at : at + LANES]
        key_rows = qkv_ref[:, inner + at : inner + at + LANES]
        value_rows = qkv_ref[:, 2 * inner + at : 2 * inner + at + LANES]
        out_grad = mixed_grad[:, at : at + LANES]
        grads = []
        for sub in range(2):
            own = low_lanes if sub == 0 else ~low_lanes
            probs = probs_ref[2 * pair + sub]
            prob_grad = contract_cols(jnp.where(own, out_grad, jnp.zeros_like(out_grad)), value_rows)
            carry = jnp.sum(prob_grad * probs, axis=1, keepdims=True)
            score_grad = (probs * (prob_grad - carry)).astype(LOW)
            grads.append(
                (
                    dot(score_grad, key_rows),
                    contract_rows(score_grad, queries),
                    contract_rows(probs.astype(LOW), out_grad),
                )
            )
        scale = HEAD_DIM ** (-0.5)
        qkg_ref[:, at : at + LANES] = (jnp.where(low_lanes, grads[0][0], grads[1][0]) * scale).astype(LOW)
        qkg_ref[:, inner + at : inner + at + LANES] = (
            jnp.where(low_lanes, grads[0][1], grads[1][1]) * scale
        ).astype(LOW)
        vg_ref[:, at : at + LANES] = jnp.where(low_lanes, grads[0][2], grads[1][2]).astype(LOW)
    h_one = h_ref[...]
    qk_out[:, : 2 * inner] = contract_rows(h_one, qkg_ref[...]).astype(LOW)
    vx_out[:, :inner] = contract_rows(h_one, vg_ref[...]).astype(LOW)
    one_grad = contract_cols(qkg_ref[...], qk_ref[:, : 2 * inner]) + contract_cols(vg_ref[...], vx_ref[:, :inner])
    one_ref[...] = one_grad
    rows = rows_ref[...]
    gain_one_row = jnp.sum(one_grad * (rows * inverse_rms(rows)), axis=0, keepdims=True)
    router_rows = router_ref[...]
    sub = iota(router_rows.shape, 0)
    extra = jnp.where(sub == 0, gain_one_row, jnp.where(sub == 1, gain_two_row, router_rows))
    qk_out[:, 2 * inner :] = extra.T.astype(LOW)


def local(
    block_in,
    seq_lengths,
    routes,
    w_query,
    w_key,
    w_value,
    w_out_proj,
    router,
    gain_attn,
    gain_moe,
    expert_in,
    expert_out,
    cotangent,
):
    dp_count = lax.axis_size("dp")
    core = lax.axis_index("tensor")
    tok_rows, width = block_in.shape
    group_rows, top_count = routes.shape
    experts = router.shape[1]
    half = max(EXTRA_ROWS, top_count * group_rows // experts)
    slots = experts * half
    rows_sent = half * (width // LANES) + EXTRA_ROWS
    inner = w_query.shape[1]
    bits = dp_count.bit_length() - 1
    order_a, order_b = bit_orders()

    expert_ids = jnp.arange(experts, dtype=jnp.int32)
    hits = jnp.any(routes[:, :, None] == expert_ids[None, None, :], axis=1)
    places = jnp.arange(group_rows, dtype=jnp.int32)
    earlier = (places[:, None] > places[None, :]).astype(LOW)
    slot_col = jnp.where(hits, dot(earlier, hits.astype(LOW)), -1.0).astype(LOW)
    slot_row = slot_col.T
    base = core * half
    slot_ids = (base + jnp.arange(half, dtype=jnp.int32)).astype(LOW)
    in_slot = slot_row[:, None, :] == slot_ids[None, :, None]
    dispatch = in_slot.astype(LOW).reshape(slots, group_rows)
    base = base.reshape(1).astype(jnp.int32)
    cot_picked = dot(dispatch, cotangent.astype(LOW)).astype(LOW).reshape(experts, half, width)

    extra_width = -(-(2 + experts) // LANES) * LANES
    extra = jnp.concatenate(
        [
            gain_attn[:, None],
            gain_moe[:, None],
            router,
            jnp.zeros((router.shape[0], extra_width - 2 - experts), LOW),
        ],
        axis=1,
    )
    shard = jnp.concatenate([w_query, w_key, extra, w_value, w_out_proj.T], axis=1)
    lines = [[low + 4 * high for high in range(dp_count // 4)] for low in range(4)]
    line = lax.all_gather(shard, "dp", axis=0, tiled=True, axis_index_groups=lines)
    line = line.reshape((2,) * (bits - 2) + (1, 1) + shard.shape)
    held = 2 * inner + extra_width
    qk_full, vx_full = line[..., :held], line[..., held:]
    for step in range(bits - 2, bits):
        vx_full = double(vx_full, order_b[step], bits)
        qk_full = double(qk_full, order_a[step], bits)
        if step == bits - 2:
            rows_all = lax.all_gather(after(block_in, vx_full), "tensor", axis=0, tiled=True)
    cot_own = trade(after(cot_picked, rows_all))
    qk_full = qk_full.reshape(width, 2 * inner + extra_width)
    vx_full = vx_full.reshape(width, 2 * inner)

    attn_part, ext, h_one, qkv, probs, mixed, rows_far, qk_far, vx_far = call(
        attention_kernel,
        [
            near_shape((group_rows, width), FULL),
            near_shape((extra_width, width), FULL),
            far_shape((group_rows, width), LOW),
            far_shape((group_rows, 3 * inner), LOW),
            far_shape((inner // HEAD_DIM, group_rows, group_rows), FULL),
            far_shape((group_rows, inner), LOW),
            far_shape(rows_all.shape, FULL),
            far_shape(qk_full.shape, LOW),
            far_shape(vx_full.shape, LOW),
        ],
        seq_lengths,
        rows_all,
        qk_full,
        vx_full,
        limit=14,
        flops=8 * group_rows * width * inner + 4 * group_rows * group_rows * inner,
        smem=(0,),
    )
    residual, h_two, gates, sent = call(
        dispatch_kernel,
        [
            far_shape((group_rows, width), FULL),
            far_shape((group_rows, width), LOW),
            near_shape((experts, group_rows), FULL),
            near_shape((experts, rows_sent, LANES), LOW),
        ],
        base,
        rows_all,
        attn_part,
        swap(attn_part),
        ext,
        slot_row,
        flops=2 * experts * half * group_rows * width,
        smem=(0,),
    )

    cot_crossed = cross(cot_own)
    cot_own = (cot_own, swap(cot_own))
    cot_far = (cot_crossed, swap(cot_crossed))
    h_own = trade(sent)
    h_crossed = cross(after(h_own, cot_crossed))
    h_own = (after(h_own, cot_far[1]), swap(h_own))
    first_weight = expert_in[0]
    second_weight = expert_out[0]
    own_back, own_given, own_kept = expert_rows(h_own, cot_own, first_weight, second_weight, half)
    h_crossed = after(h_crossed, own_back)
    h_far = (h_crossed, swap(h_crossed))
    far_back, far_given, far_kept = expert_rows(h_far, cot_far, first_weight, second_weight, half)
    far_sum = add_low(far_back, swap(far_given))
    far_total = cross(far_sum)
    far_kept[0] = after(far_kept[0], far_sum)
    far_out, far_given, *sums = expert_weights(h_far, cot_far, far_kept, second_weight, (), half)
    back_sum = after(add_low(own_back, swap(own_given), far_total), far_out)
    back = trade(back_sum)
    out_far = add_low(far_out, swap(far_given))
    own_kept[0] = after(own_kept[0], out_far, back_sum)
    own_out, out_given, grad_first, grad_second = expert_weights(
        h_own, cot_own, own_kept, second_weight, sums, half
    )
    out_far = cross(after(out_far, far_total))
    out_given = swap(out_given)
    back_out = trade(add_low(own_out, out_given, out_far)).reshape(slots, width)

    h_part, router_part = call(
        combine_kernel,
        [near_shape((group_rows, width), FULL), near_shape((experts, width), FULL)],
        base,
        after(back, own_out, out_far),
        slot_row,
        slot_col,
        gates,
        ext,
        far(h_two),
        flops=2 * slots * group_rows * width,
        smem=(0,),
    )
    router_part = jnp.pad(router_part, ((2, extra_width - 2 - experts), (0, 0)))
    qk_part, vx_part, one_part, resid_grad, _, _ = call(
        backward_kernel,
        [
            near_shape((width, 2 * inner + extra_width), LOW),
            near_shape((width, 2 * inner), LOW),
            near_shape((group_rows, width), FULL),
            near_shape((group_rows, width), FULL),
            near_shape((group_rows, 2 * inner), LOW),
            near_shape((group_rows, inner), LOW),
        ],
        h_part,
        swap(h_part),
        *map(far, (cotangent, residual, rows_far)),
        ext,
        *map(far, (qk_far, vx_far, h_one, qkv, probs, mixed)),
        router_part,
        limit=14,
        flops=20 * group_rows * width * inner + 12 * group_rows * group_rows * inner,
    )

    own_start = core * tok_rows
    other_start = (1 - core) * tok_rows

    def rows_at(values, start):
        return lax.dynamic_slice_in_dim(values, start, tok_rows, 0)

    one_other = swap(rows_at(one_part, other_start).astype(LOW)).astype(FULL)
    qk_sum = qk_part.reshape((2,) * bits + (width // dp_count, 2 * inner + extra_width))
    vx_sum = vx_part.reshape((2,) * bits + (width // dp_count, 2 * inner))
    for step in range(bits):
        vx_sum = halve(vx_sum, order_b[bits - 1 - step], bits)
        qk_sum = halve(qk_sum, order_a[bits - 1 - step], bits)
        if step == 1:
            back_out = after(back_out, vx_sum, qk_sum)
    qk_sum = qk_sum.reshape(width // dp_count, 2 * inner + extra_width)
    vx_sum = vx_sum.reshape(width // dp_count, 2 * inner)

    out_part = contract_rows(dispatch, back_out)
    block_out = rows_at(residual, own_start) + (
        rows_at(out_part, own_start) + swap(rows_at(out_part, other_start))
    )
    scaled_one = (rows_at(one_part, own_start) + one_other) * ext[0:1, :]
    inv_own = inverse_rms(block_in)
    normed_own = block_in * inv_own
    grad_in = rows_at(resid_grad, own_start) + inv_own * (
        scaled_one - normed_own * jnp.mean(scaled_one * normed_own, axis=1, keepdims=True)
    )
    extra_sum = qk_sum[:, 2 * inner :]
    extra_sum = extra_sum + swap(extra_sum)
    share = extra_sum.shape[0] // 2
    extra_own = lax.dynamic_slice_in_dim(extra_sum, core * share, share, 0)
    return (
        block_out,
        grad_in,
        qk_sum[:, :inner],
        qk_sum[:, inner : 2 * inner],
        vx_sum[:, :inner],
        vx_sum[:, inner:].T,
        extra_own[:, 2 : 2 + experts],
        extra_own[:, 0],
        extra_own[:, 1],
        grad_first[None],
        grad_second[None],
    )


def solution(mesh):
    in_specs = (
        P(("dp", "tensor"), None),
        P("dp", None),
        P("dp", None),
        P("dp", "tensor"),
        P("dp", "tensor"),
        P("dp", "tensor"),
        P("tensor", "dp"),
        P("dp", None),
        P("dp"),
        P("dp"),
        P("dp", None, "tensor"),
        P("dp", "tensor", None),
        P("dp", None),
    )
    out_specs = (
        P(("dp", "tensor"), None),
        P(("dp", "tensor"), None),
        P("dp", "tensor"),
        P("dp", "tensor"),
        P("dp", "tensor"),
        P("tensor", "dp"),
        P(("dp", "tensor"), None),
        P(("dp", "tensor")),
        P(("dp", "tensor")),
        P("dp", None, "tensor"),
        P("dp", "tensor", None),
    )
    return jax.shard_map(local, mesh=mesh, in_specs=in_specs, out_specs=out_specs, check_vma=False)
```
